32 devices in a mesh: dp: 8 (over y, x, core), tensor: 4 (over z).
Axes of the slice: x: 2, y: 2, z: 4, core: 2. Of those that a mesh axis runs over, the one named last changes fastest.
Arguments:
- layer_input: bfloat16 [8192, 2048], P('dp'), may hold values from -6 to 6
- lengths: int32 [8], P('dp'), may hold values from 128 to 1024, as said below
- ln1_gain: float32 [2048], replicated, may hold values from 0.5 to 1.5
- ln1_shift: float32 [2048], replicated, may hold values from -1.2 to 1.2
- w_qkv: bfloat16 [2048, 3, 2048], P(None, None, 'tensor'), may hold values from -0.125 to 0.125
- b_qkv: float32 [3, 2048], P(None, 'tensor'), may hold values from -3 to 3
- w_dense: bfloat16 [2048, 2048], P('tensor'), may hold values from -1 to 1
- b_dense: float32 [2048], replicated, may hold values from -1.2 to 1.2
- ln2_gain: float32 [2048], replicated, may hold values from 0.5 to 1.5
- ln2_shift: float32 [2048], replicated, may hold values from -1.2 to 1.2
- w_in: bfloat16 [2048, 8192], P(None, 'tensor'), may hold values from -0.125 to 0.125
- b_in: float32 [8192], P('tensor'), may hold values from -3 to 3
- w_out: bfloat16 [8192, 2048], P('tensor'), may hold values from -0.0625 to 0.0625
- b_out: float32 [2048], replicated, may hold values from -1.2 to 1.2
- grad_out: bfloat16 [8192, 2048], P('dp'), may hold values from -6 to 6
Outputs:
- layer_output: bfloat16 [8192, 2048], P('dp')
- input_grad: bfloat16 [8192, 2048], P('dp')
- ln1_gain_grad: float32 [2048], replicated
- ln1_shift_grad: float32 [2048], replicated
- w_qkv_grad: float32 [2048, 3, 2048], P('dp', None, 'tensor')
- b_qkv_grad: float32 [3, 2048], P(None, 'tensor')
- w_dense_grad: float32 [2048, 2048], P('tensor', 'dp')
- b_dense_grad: float32 [2048], replicated
- ln2_gain_grad: float32 [2048], replicated
- ln2_shift_grad: float32 [2048], replicated
- w_in_grad: float32 [2048, 8192], P('dp', 'tensor')
- b_in_grad: float32 [8192], P('tensor')
- w_out_grad: float32 [8192, 2048], P('tensor', 'dp')
- b_out_grad: float32 [2048], replicated
The draws below stay inside these ranges and needn't reach their ends.
Inputs may be any that keep to these rules, and one draw needn't show every extreme that they name: `lengths`: valid tokens of each sequence, counted from its first position; in every draw some sequence has all 1024.
All inputs are finite; a program needn't handle non-finite values.
Results may differ from the reference program's by a relative error of at most 0.011.
Values sent between devices are 32-bit elements; how exact they have to be, the bound alone decides.
No kernel may reach another device: no remote copies, remote signals or barrier semaphores. Data moves between devices by JAX's collectives and lax.ppermute only.
A program may use at most 320 MiB of HBM per device.

```python
import math
import jax
import jax.numpy as jnp
from jax import lax

D = 2048
HEADS = 8
HD = 256
ROT = 64
FF = 8192
LMAX = 1024
NSEQ = 8
TOKENS = 8192


def draw_lengths(key, part):
    key = jax.random.fold_in(key, 11)
    first, second = jax.random.split(key)
    drawn = jax.random.randint(first, (NSEQ,), LMAX // 8, LMAX + 1)
    chosen = jax.random.randint(second, (), 0, NSEQ)
    return jnp.where(jnp.arange(NSEQ) == chosen, LMAX, drawn).astype(jnp.int32)


def raised(values, rng, source, target, blocks, factor):
    owner, partner = [(jnp.arange(values.shape[axis_at]) // (values.shape[axis_at] // blocks)).reshape([-1 if axis == axis_at else 1 for axis in range(values.ndim)]) for axis_at in (source, target)]
    chosen = jax.random.permutation(rng, blocks)[partner]
    strong = (owner == chosen) | (owner == (partner + blocks // 2) % blocks)
    return jnp.where(strong, factor * values, values)


def steps_of(own_key, extent, pieces, least, top_value):
    loudness = 1.0
    for position, parts in pieces:
        heights = jax.random.uniform(jax.random.fold_in(jax.random.fold_in(own_key, 6), position), (parts,), jnp.float32, least / len(pieces), top_value / len(pieces))
        loudness = loudness * jnp.repeat(jnp.exp(heights), extent[position] // parts).reshape((-1,) + (1,) * (len(extent) - 1 - position))
    return loudness


def centred(rng, dims, scale, limit, cuts=(), held_as=jnp.bfloat16):
    values = scale * jax.random.normal(rng, dims, jnp.float32)
    if cuts:
        values = values * steps_of(rng, dims, cuts, -0.22, 0.18)
    return jnp.clip(values, -limit, limit).astype(held_as)


def heavy_noise(own_key, extent, deviation, most, cuts, heavy, kind=jnp.bfloat16):
    values = deviation * jax.random.normal(own_key, extent, jnp.float32)
    if cuts:
        values = values * steps_of(own_key, extent, cuts, -0.22, 0.18)
    return jnp.clip(raised(values, jax.random.fold_in(own_key, 3), *heavy), -most, most).astype(kind)


def setup_inputs(seed: int = 0) -> dict:
    splits = jax.random.split(jax.random.key(seed), 16)
    return {
        "layer_input": centred(splits[0], (TOKENS, D), 1.0, 6.0, ((0, 8),)),
        "lengths": draw_lengths(jax.random.fold_in(splits[15], 71), 0),
        "ln1_gain": jnp.clip(1.0 + 0.1 * jax.random.normal(splits[2], (D,), jnp.float32), 0.5, 1.5),
        "ln1_shift": centred(splits[3], (D,), 0.2, 1.2, (), jnp.float32),
        "w_qkv": centred(splits[4], (D, 3, HEADS * HD), D ** -0.5, 0.125, ((2, 4),)),
        "b_qkv": centred(splits[5], (3, HEADS * HD), 0.5, 3.0, ((1, 4),), jnp.float32),
        "w_dense": centred(splits[6], (HEADS * HD, D), (max(HEADS * HD // 64, 1)) ** -0.5, 1.0, ((0, 4),)),
        "b_dense": centred(splits[7], (D,), 0.2, 1.2, (), jnp.float32),
        "ln2_gain": jnp.clip(1.0 + 0.1 * jax.random.normal(splits[8], (D,), jnp.float32), 0.5, 1.5),
        "ln2_shift": centred(splits[9], (D,), 0.2, 1.2, (), jnp.float32),
        "w_in": centred(splits[10], (D, FF), D ** -0.5, 0.125, ((1, 4),)),
        "b_in": centred(splits[11], (FF,), 0.5, 3.0, ((0, 4),), jnp.float32),
        "w_out": centred(splits[12], (FF, D), FF ** -0.5, 0.0625, ((0, 4),)),
        "b_out": centred(splits[13], (D,), 0.2, 1.2, (), jnp.float32),
        "grad_out": heavy_noise(splits[14], (TOKENS, D), 1.0, 6.0, ((0, 8),), (0, 1, 8, 2.0)),
    }


@jax.custom_vjp
def low(v):
    return lax.optimization_barrier(v.astype(jnp.bfloat16)).astype(jnp.float32)

@jax.custom_vjp
def low_back(v):
    return v

def low_keep(v):
    return (low(v), None)

def low_pass(kept, grad):
    return (grad,)

def back_keep(v):
    return (v, None)

def back_low(kept, grad):
    return (low(grad),)
low.defvjp(low_keep, low_pass)
low_back.defvjp(back_keep, back_low)
EPS = 1e-05
HIGH = lax.Precision.HIGHEST

def layer_norm(values, gain, shift):
    center = values - lax.optimization_barrier(jnp.mean(values, -1, keepdims=True))
    spread = lax.optimization_barrier(jnp.mean(center * center, -1, keepdims=True))
    return center * lax.rsqrt(spread + EPS) * gain + shift

def rotary_tables(dtype):
    half = ROT // 2
    inverse = 10000.0 ** (-(2.0 * jnp.arange(half).astype(dtype)) / ROT)
    angle = jnp.arange(LMAX).astype(dtype)[:, None] * inverse[None, :]
    return (jnp.cos(angle)[:, None, :], jnp.sin(angle)[:, None, :])

def turn(values, cosine, sine):
    half = ROT // 2
    first = values[..., :half]
    second = values[..., half:ROT]
    rest = values[..., ROT:]
    return jnp.concatenate([first * cosine - second * sine, second * cosine + first * sine, rest], -1)

def layer(xseq, length, params):
    ln1_gain, ln1_shift, w_qkv, b_qkv, w_dense, b_dense, ln2_gain, ln2_shift, w_in, b_in, w_out, b_out = params
    cosine, sine = rotary_tables(xseq.dtype)
    a_one = low(layer_norm(xseq, ln1_gain, ln1_shift))
    qkv = low_back(jnp.einsum('td,dcf->tcf', a_one, w_qkv, precision=HIGH) + b_qkv)
    query = low(turn(qkv[:, 0].reshape(LMAX, HEADS, HD), cosine, sine))
    key_rows = low(turn(qkv[:, 1].reshape(LMAX, HEADS, HD), cosine, sine))
    value = low(qkv[:, 2].reshape(LMAX, HEADS, HD))
    scores = low_back(jnp.einsum('qhd,khd->hqk', query, key_rows, precision=HIGH) * (1.0 / math.sqrt(HD)))
    positions = jnp.arange(LMAX)
    allowed = (positions[None, :] <= positions[:, None]) & (positions[None, :] < length)
    scores = jnp.where(allowed[None], scores, -1e+30)
    top = lax.optimization_barrier(jnp.max(scores, -1, keepdims=True))
    expo = jnp.exp(scores - top)
    probs = expo / lax.optimization_barrier(jnp.sum(expo, -1, keepdims=True))
    mixed = jnp.einsum('hqk,khd->qhd', low(probs), value, precision=HIGH)
    mixed = low(low_back(mixed)).reshape(LMAX, HEADS * HD)
    attn = jnp.dot(mixed, w_dense, precision=HIGH)
    a_two = low(layer_norm(xseq, ln2_gain, ln2_shift))
    hpre = low_back(jnp.dot(a_two, w_in, precision=HIGH) + b_in)
    hidden = low(jax.nn.gelu(hpre, approximate=False))
    feed = jnp.dot(hidden, w_out, precision=HIGH)
    return xseq + attn + feed + b_dense + b_out

def reference(layer_input, lengths, ln1_gain, ln1_shift, w_qkv, b_qkv, w_dense, b_dense, ln2_gain, ln2_shift, w_in, b_in, w_out, b_out, grad_out):
    params = tuple((p.astype(jnp.float32) for p in (ln1_gain, ln1_shift, w_qkv, b_qkv, w_dense, b_dense, ln2_gain, ln2_shift, w_in, b_in, w_out, b_out)))
    inputs = layer_input.astype(jnp.float32).reshape(NSEQ, LMAX, D)
    cotans = grad_out.astype(jnp.float32).reshape(NSEQ, LMAX, D)

    def one(carry, item):
        xseq, length, dyseq = item
        out, pull = jax.vjp(lambda xx, pp: layer(xx, length, pp), xseq, params)
        valid = (jnp.arange(LMAX) < length).astype(jnp.float32)[:, None]
        dxseq, dparams = pull(dyseq * valid)
        carry = jax.tree.map(lambda a, b: a + b, carry, dparams)
        return (carry, (out, dxseq))
    start = tuple((jnp.zeros_like(p) for p in params))
    grads, (outs, dxs) = lax.scan(one, start, (inputs, lengths, cotans))
    layer_output = outs.reshape(TOKENS, D).astype(jnp.bfloat16)
    input_grad = dxs.reshape(TOKENS, D).astype(jnp.bfloat16)
    return (layer_output, input_grad, grads[0], grads[1], grads[2], grads[3], grads[4], grads[5], grads[6], grads[7], grads[8], grads[9], grads[10], grads[11])
```

```python
import math

import jax
import jax.numpy as jnp
import numpy as np
from jax import lax
from jax.experimental import pallas as pl
from jax.experimental.pallas import tpu as pltpu
from jax.sharding import PartitionSpec as P

HD = 256
ROT = 64
EPS = 1e-05
F32 = jnp.float32
BF16 = jnp.bfloat16
VMEM_LIMIT = 48 * 1024 * 1024
FULL_LIMIT = 56 * 1024 * 1024
SMALL_LIMIT = 8 * 1024 * 1024
NT = (((1,), (1,)), ((), ()))
TN = (((0,), (0,)), ((), ()))


def dot(a, b, dims=(((1,), (0,)), ((), ()))):
    return lax.dot_general(a, b, dims, preferred_element_type=F32)


def params():
    return pltpu.CompilerParams(vmem_limit_bytes=VMEM_LIMIT)


def cost(flops, nbytes, long=False):
    return pl.CostEstimate(flops=int(3e11 if long else 4e10), bytes_accessed=int(nbytes), transcendentals=0)


def light(flops, nbytes):
    return pl.CostEstimate(flops=int(flops), bytes_accessed=int(nbytes), transcendentals=0)


ANY = pl.BlockSpec(memory_space=pl.ANY)
HBM = pl.BlockSpec(memory_space=pltpu.HBM)
VMEM = pl.BlockSpec(memory_space=pltpu.VMEM)
SMEM = pl.BlockSpec(memory_space=pltpu.SMEM)


def shape(dims, dtype):
    return jax.ShapeDtypeStruct(dims, dtype)


TOKEN = shape((8, 128), F32)


def turned(values, cosine, lower, upper):
    head = values[:, :128]
    head = (
        head * cosine
        + pltpu.roll(head, 128 - ROT // 2, 1) * lower
        + pltpu.roll(head, ROT // 2, 1) * upper
    )
    return jnp.concatenate([head, values[:, 128:]], 1)


class Stream:
    def __init__(self, pieces, sems, window=4):
        self.copies = [pltpu.make_async_copy(a, b, sems.at[i]) for i, (a, b) in enumerate(pieces)]
        self.window = window
        self.done = 0
        for copy in self.copies[:window]:
            copy.start()

    def next(self):
        self.copies[self.done].wait()
        ahead = self.done + self.window
        if ahead < len(self.copies):
            self.copies[ahead].start()
        self.done += 1


def forward_rows(start, size, unit, x, lengths, flag, gains, w_three, b_three, w_in, b_in, b_after, w_dense, w_out, tables, held, after):
    rows, width = x.shape
    columns, units = w_dense.shape[0], w_in.shape[1]
    heads = columns // HD
    at = start // size
    piece = min(512, units)
    wide = min(512, width)
    scale = 1.0 / math.sqrt(HD)
    past = start > 0
    steps = 3 + units // piece + 1 + width // wide

    def body(*refs):
        len_ref, flag_ref, x_ref, g1, s1, g2, s2, b3_ref, bi_ref, ba_ref, c_ref, l_ref, u_ref = refs[:13]
        w3_hbm, wi_hbm, wd_hbm, wo_hbm = refs[13:17]
        one_ref, two_ref, qkv_ref, o_ref, hidden_ref, slope_ref, *part_refs, token_ref = refs[-14 - size // unit : -7]
        token_ref[...] = jnp.zeros_like(token_ref)
        w3, wi, wd, wo, kv_ref, sems, kv_sem = refs[-7:]
        if past:
            earlier = pltpu.make_async_copy(refs[19].at[pl.ds(1, 2), pl.ds(0, start)], kv_ref, kv_sem)
            earlier.start()
        pieces = [(w3_hbm.at[c], w3.at[c]) for c in range(3)]
        for low in range(0, units, piece):
            here = pl.ds(low, piece)
            pieces.append((wi_hbm.at[:, here], wi.at[:, here]))
        pieces.append((wd_hbm, wd))
        for low in range(0, width, wide):
            here = pl.ds(low, wide)
            pieces.append((wo_hbm.at[:, here], wo.at[:, here]))
        stream = Stream(pieces, sems)
        length = len_ref[0]

        values = x_ref[...].astype(F32)
        center = values - jnp.mean(values, -1, keepdims=True)
        spread = jnp.mean(center * center, -1, keepdims=True)
        normed = center * lax.rsqrt(spread + EPS)
        one_ref[...] = (normed * g1[...] + s1[...]).astype(BF16)
        two_ref[...] = (normed * g2[...] + s2[...]).astype(BF16)

        for c in range(3):
            stream.next()
            acc = dot(one_ref[...], w3[c]) + b3_ref[c]
            for h in range(heads):
                cols = slice(h * HD, (h + 1) * HD)
                one_head = acc[:, cols]
                if c < 2:
                    one_head = turned(one_head, c_ref[...], l_ref[...], u_ref[...])
                qkv_ref[c, :, cols] = one_head.astype(BF16)

        here = lax.broadcasted_iota(jnp.int32, (size, size), 0)
        there = lax.broadcasted_iota(jnp.int32, (size, size), 1)
        seen = (there <= here) & (there + start < length)
        if past:
            inside = lax.broadcasted_iota(jnp.int32, (size, start), 1) < length
            earlier.wait()
        for h in range(heads):
            cols = slice(h * HD, (h + 1) * HD)
            query = qkv_ref[0, :, cols]
            now = jnp.where(seen, dot(query, qkv_ref[1, :, cols], NT) * scale, -1e30)
            top = jnp.max(now, -1, keepdims=True)
            if past:
                old = jnp.where(inside, dot(query, kv_ref[0, :, cols], NT) * scale, -1e30)
                top = jnp.maximum(top, jnp.max(old, -1, keepdims=True))
                old = jnp.exp(old - top)
            now = jnp.exp(now - top)
            total = jnp.sum(now, -1, keepdims=True)
            if past:
                total = total + jnp.sum(old, -1, keepdims=True)
            share = 1.0 / total
            mixed = dot((now * share).astype(BF16), qkv_ref[2, :, cols])
            if past:
                mixed = mixed + dot((old * share).astype(BF16), kv_ref[1, :, cols])
            o_ref[:, cols] = mixed.astype(BF16)

        for low in range(0, units, piece):
            cols = slice(low, low + piece)
            stream.next()
            pre = dot(two_ref[...], wi[:, cols]) + bi_ref[:, cols]
            share = 0.5 + 0.5 * lax.erf(pre * (1.0 / math.sqrt(2.0)))
            hidden_ref[:, cols] = (pre * share).astype(BF16)
            bell = jnp.exp(-0.5 * pre * pre) * (1.0 / math.sqrt(2.0 * math.pi))
            slope_ref[:, cols] = (share + pre * bell).astype(BF16)

        stream.next()
        own = flag_ref[1].astype(F32)
        for low in range(0, width, wide):
            cols = slice(low, low + wide)
            stream.next()
            acc = dot(o_ref[...], wd[:, cols]) + dot(hidden_ref[...], wo[:, cols])
            acc = acc + own * (x_ref[:, cols].astype(F32) + ba_ref[:, cols])
            for i, part_ref in enumerate(part_refs):
                part_ref[:, cols] = acc[i * unit : (i + 1) * unit]

    vec = lambda n: pl.BlockSpec((1, n), lambda i: (0, 0))
    table = pl.BlockSpec((size, 128), lambda i: (at, 0))
    block = lambda n: pl.BlockSpec((size, n), lambda i: (at, 0))
    operands = [lengths, flag, x, *gains, b_three, b_in, b_after, *tables, w_three, w_in, w_dense, w_out]
    specs = [SMEM, SMEM, block(width)] + [vec(width)] * 4
    specs += [pl.BlockSpec((3, 1, columns), lambda i: (0, 0, 0)), vec(units), vec(width)] + [table] * 3 + [HBM] * 4
    aliases = {}
    if past:
        aliases = {len(operands) + i: i for i in range(6)}
        operands += list(held)
        specs += [HBM] * 6
    operands += list(after)
    specs += [ANY] * len(after)
    flops = 2 * size * width * (4 * columns + 2 * units)
    return pl.pallas_call(
        body,
        grid=(1,),
        in_specs=specs,
        out_specs=[
            block(width),
            block(width),
            pl.BlockSpec((3, size, columns), lambda i: (0, at, 0)),
            block(columns),
            block(units),
            block(units),
        ]
        + [pl.BlockSpec((unit, width), lambda i: (0, 0))] * (size // unit)
        + [pl.BlockSpec(TOKEN.shape, lambda i: (0, 0))],
        out_shape=[
            shape((rows, width), BF16),
            shape((rows, width), BF16),
            shape((3, rows, columns), BF16),
            shape((rows, columns), BF16),
            shape((rows, units), BF16),
            shape((rows, units), BF16),
        ]
        + [shape((unit, width), F32)] * (size // unit)
        + [TOKEN],
        scratch_shapes=[
            pltpu.VMEM(w_three.shape, BF16),
            pltpu.VMEM(w_in.shape, BF16),
            pltpu.VMEM(w_dense.shape, BF16),
            pltpu.VMEM(w_out.shape, BF16),
            pltpu.VMEM((2, max(start, 16), columns), BF16),
            pltpu.SemaphoreType.DMA((steps,)),
            pltpu.SemaphoreType.DMA,
        ],
        input_output_aliases=aliases,
        compiler_params=params(),
        cost_estimate=cost(flops, 2 * width * (4 * columns + 2 * units) + size * width * 20),
        name="forward_rows",
    )(*operands)


def mask_rows(lengths, grad_out, after):
    rows, width = grad_out.shape
    step = 256

    def body(*refs):
        len_ref, g_ref = refs[:2]
        out_ref, sum_ref = refs[-2:]
        i = pl.program_id(0)
        here = lax.broadcasted_iota(jnp.int32, (step, 1), 0) + i * step
        valid = (here < len_ref[0]).astype(F32)
        kept = g_ref[...].astype(F32) * valid
        out_ref[...] = kept.astype(BF16)

        @pl.when(i == 0)
        def _():
            sum_ref[...] = jnp.zeros_like(sum_ref)

        sum_ref[...] += jnp.sum(kept, 0, keepdims=True)

    row = pl.BlockSpec((step, width), lambda i: (i, 0))
    return pl.pallas_call(
        body,
        grid=(rows // step,),
        in_specs=[SMEM, row] + [ANY] * len(after),
        out_specs=[row, pl.BlockSpec((1, width), lambda i: (0, 0))],
        out_shape=[shape((rows, width), BF16), shape((1, width), F32)],
        compiler_params=params(),
        cost_estimate=cost(2 * rows * width, 4 * rows * width),
        name="mask_rows",
    )(lengths, grad_out, *after)


def pair_product(lefts, right, slide_left, parity, added, blocks, after, name):
    rows = right.shape[-2]
    many = right.shape[0]
    left_width = sum(left.shape[1] for left in lefts)
    block = (left_width if slide_left else right.shape[2]) // (2 * blocks)
    tall, wide = (block, right.shape[2]) if slide_left else (left_width, block)

    def body(_, *refs):
        right_ref = refs[len(lefts)]
        out_ref, token_ref = refs[-2:]
        token_ref[...] = jnp.zeros_like(token_ref)
        for c in range(many):
            low = 0
            for left_ref in refs[: len(lefts)]:
                here = slice(low, low + left_ref.shape[1])
                low += left_ref.shape[1]
                acc = dot(left_ref[...], right_ref[c], TN)
                if added is not None:
                    acc = acc + refs[len(lefts) + 1][0, c, here]
                out_ref[0, c, here] = acc

    out = pl.BlockSpec((1, many, tall, wide), lambda i, p: (i, 0, 0, 0))
    if slide_left:
        specs = [pl.BlockSpec((rows, block), lambda i, p: (0, 2 * i + p[0]))]
        specs.append(pl.BlockSpec(right.shape, lambda i, p: (0, 0, 0)))
    else:
        specs = [pl.BlockSpec(left.shape, lambda i, p: (0, 0)) for left in lefts]
        specs.append(pl.BlockSpec((many, rows, block), lambda i, p: (0, 0, 2 * i + p[0])))
    operands = [*lefts, right]
    if added is not None:
        operands.append(added)
        specs.append(out)
    return pl.pallas_call(
        body,
        grid_spec=pltpu.PrefetchScalarGridSpec(
            num_scalar_prefetch=1,
            grid=(blocks,),
            in_specs=specs + [ANY] * len(after),
            out_specs=[out, pl.BlockSpec(TOKEN.shape, lambda i, p: (0, 0))],
        ),
        out_shape=[shape((blocks, many, tall, wide), F32), TOKEN],
        compiler_params=params(),
        cost_estimate=cost(2 * rows * blocks * many * tall * wide, 2 * rows * (left_width + many * right.shape[2]) + 4 * blocks * many * tall * wide),
        name=name,
    )(parity, *operands, *after)


def attend_back(lengths, qkv, cotan, w_dense, tables, after):
    rows, columns = qkv.shape[1:]
    width = cotan.shape[1]
    sub = min(256, rows)
    scale = 1.0 / math.sqrt(HD)

    def body(len_ref, q_ref, k_ref, v_ref, g_ref, w_ref, c_ref, l_ref, u_ref, *refs):
        out_ref, bias_ref, dk_ref, dv_ref = refs[-4:]
        length = len_ref[0]
        for low in range(0, rows, sub):
            stop = low + sub
            here = slice(low, stop)
            query, keys, values = q_ref[0, here], k_ref[0, :stop], v_ref[0, :stop]
            scores = dot(query, keys, NT) * scale
            mine = lax.broadcasted_iota(jnp.int32, scores.shape, 0) + low
            there = lax.broadcasted_iota(jnp.int32, scores.shape, 1)
            scores = jnp.where((there <= mine) & (there < length), scores, -1e30)
            expo = jnp.exp(scores - jnp.max(scores, -1, keepdims=True))
            probs = expo * (1.0 / jnp.sum(expo, -1, keepdims=True))
            dmixed = dot(g_ref[here], w_ref[...], NT).astype(BF16)
            dprobs = dot(dmixed, values, NT)
            delta = jnp.sum(probs * dprobs, -1, keepdims=True)
            dscores = (probs * (dprobs - delta)).astype(BF16)
            out_ref[0, here] = turned(
                dot(dscores, keys) * scale, c_ref[here], -l_ref[here], -u_ref[here]
            ).astype(BF16)
            dkey = dot(dscores, query, TN) * scale
            dvalue = dot(probs.astype(BF16), dmixed, TN)
            if low:
                dk_ref[:low] += dkey[:low]
                dv_ref[:low] += dvalue[:low]
            dk_ref[here] = dkey[low:]
            dv_ref[here] = dvalue[low:]
        out_ref[1] = turned(dk_ref[...], c_ref[...], -l_ref[...], -u_ref[...]).astype(BF16)
        out_ref[2] = dv_ref[...].astype(BF16)
        for part in range(3):
            bias_ref[part] = jnp.sum(out_ref[part].astype(F32), 0, keepdims=True)

    part = lambda c: pl.BlockSpec((1, rows, HD), lambda h: (c, 0, h))
    table = pl.BlockSpec((rows, 128), lambda h: (0, 0))
    return pl.pallas_call(
        body,
        grid=(columns // HD,),
        in_specs=[
            SMEM,
            part(0),
            part(1),
            part(2),
            pl.BlockSpec((rows, width), lambda h: (0, 0)),
            pl.BlockSpec((HD, width), lambda h: (h, 0)),
            table,
            table,
            table,
        ]
        + [ANY] * len(after),
        out_specs=[
            pl.BlockSpec((3, rows, HD), lambda h: (0, 0, h)),
            pl.BlockSpec((3, 1, HD), lambda h: (0, 0, h)),
        ],
        out_shape=[shape((3, rows, columns), BF16), shape((3, 1, columns), F32)],
        scratch_shapes=[pltpu.VMEM((rows, HD), F32)] * 2,
        compiler_params=params(),
        cost_estimate=cost(
            2 * rows * columns * width + 10 * rows * rows * columns,
            2 * rows * (width + 7 * columns),
            True,
        ),
        name="attend_back",
    )(lengths, qkv, qkv, qkv, cotan, w_dense, *tables, *after)


def backward_rows(start, size, unit, x, flag, cotan, slope, dqkv, w_three, w_in, w_out, gains, held, after):
    rows, width = x.shape
    columns, units = dqkv.shape[2], slope.shape[1]
    at = start // size
    piece = min(512, units)
    wide = min(512, width)
    steps = units // piece + width // wide

    def body(*refs):
        x_ref, flag_ref, g_ref, slope_ref, q_ref, g1, g2, w3_hbm, wi_hbm, wo_hbm = refs[:10]
        dh_ref, small_ref, bias_ref, *dx_refs = refs[-10 - size // unit : -7]
        w3, wi, wo, one, two, sems, sems3 = refs[-7:]
        pieces = []
        for low in range(0, units, piece):
            here = pl.ds(low, piece)
            pieces.append((wo_hbm.at[here], wo.at[here]))
        for low in range(0, width, wide):
            here = pl.ds(low, wide)
            pieces.append((wi_hbm.at[here], wi.at[here]))
        stream = Stream(pieces, sems)
        three = pltpu.make_async_copy(w3_hbm, w3, sems3)
        for low in range(0, units, piece):
            here = slice(low, low + piece)
            stream.next()
            if low == 0:
                three.start()
            grad = (dot(g_ref[...], wo[here], NT) * slope_ref[:, here].astype(F32)).astype(BF16)
            dh_ref[:, here] = grad
            bias_ref[:, here] = jnp.sum(grad.astype(F32), 0, keepdims=True)
        three.wait()
        for low in range(0, width, wide):
            here = slice(low, low + wide)
            acc = dot(q_ref[0], w3[0, here], NT)
            for c in (1, 2):
                acc = acc + dot(q_ref[c], w3[c, here], NT)
            one[:, here] = acc
            stream.next()
            two[:, here] = dot(dh_ref[...], wi[here], NT)
        gain_one, gain_two = g1[...], g2[...]
        own = flag_ref[1].astype(F32)
        sums = [jnp.zeros((1, width), F32)] * 4
        band = 64
        for low in range(0, size, band):
            here = slice(low, low + band)
            values = x_ref[here].astype(F32)
            center = values - jnp.mean(values, -1, keepdims=True)
            rstd = lax.rsqrt(jnp.mean(center * center, -1, keepdims=True) + EPS)
            normed = center * rstd
            d_one, d_two = one[here], two[here]
            grad = d_one * gain_one + d_two * gain_two
            dx_refs[low // unit][low % unit : low % unit + band] = rstd * (
                grad
                - jnp.mean(grad, -1, keepdims=True)
                - normed * jnp.mean(grad * normed, -1, keepdims=True)
            ) + own * g_ref[here].astype(F32)
            terms = (d_one * normed, d_one, d_two * normed, d_two)
            sums = [s + jnp.sum(t, 0, keepdims=True) for s, t in zip(sums, terms)]
        small_ref[...] = jnp.concatenate(sums + [jnp.zeros((4, width), F32)], 0)

    vec = lambda n: pl.BlockSpec((1, n), lambda i: (0, 0))
    block = lambda n: pl.BlockSpec((size, n), lambda i: (at, 0))
    operands = [x, flag, cotan, slope, dqkv, gains[0], gains[2], w_three, w_in, w_out]
    specs = [block(width), SMEM, block(width), block(units), pl.BlockSpec((3, size, columns), lambda i: (0, at, 0))]
    specs += [vec(width), vec(width)] + [HBM] * 3
    aliases = {}
    if held is not None:
        aliases = {len(operands): 0}
        operands.append(held)
        specs.append(HBM)
    operands += list(after)
    specs += [ANY] * len(after)
    return pl.pallas_call(
        body,
        grid=(1,),
        in_specs=specs,
        out_specs=[
            block(units),
            pl.BlockSpec((8, width), lambda i: (0, 0)),
            vec(units),
        ]
        + [pl.BlockSpec((unit, width), lambda i: (0, 0))] * (size // unit),
        out_shape=[
            shape((rows, units), BF16),
            shape((8, width), F32),
            shape((1, units), F32),
        ]
        + [shape((unit, width), F32)] * (size // unit),
        scratch_shapes=[
            pltpu.VMEM(w_three.shape, BF16),
            pltpu.VMEM(w_in.shape, BF16),
            pltpu.VMEM(w_out.shape, BF16),
            pltpu.VMEM((size, width), F32),
            pltpu.VMEM((size, width), F32),
            pltpu.SemaphoreType.DMA((steps,)),
            pltpu.SemaphoreType.DMA,
        ],
        input_output_aliases=aliases,
        compiler_params=params(),
        cost_estimate=cost(2 * size * width * (2 * units + 3 * columns), 2 * width * (2 * units + 3 * columns) + 16 * size * width, start == 0),
        name="backward_rows",
    )(*operands)


def take_in(flag, unit, came, operand, out, out_at, out_shape, after):
    rows, width = came.shape
    has_unit, has_total = unit is not None, operand is not None

    def body(*refs):
        flag_ref, came_ref = refs[:2]
        if has_total:
            out_ref, rounded, sem = refs[-3:]
            rounded[...] = jnp.where(flag_ref[0] == 1, refs[2 + has_unit][...], came_ref[...]).astype(BF16)
            copy = pltpu.make_async_copy(rounded, out_ref.at[pl.ds(out_at * rows, rows)], sem)
            copy.start()
        if has_unit:
            refs[-4 if has_total else -1][...] = refs[2][...] + came_ref[...]
        if has_total:
            copy.wait()

    operands, specs = [flag, came], [SMEM, VMEM]
    outs, out_specs, aliases, scratch = [], [], {}, []
    if has_unit:
        operands.append(unit)
        specs.append(VMEM)
        outs.append(shape((rows, width), F32))
        out_specs.append(VMEM)
    if has_total:
        operands.append(operand)
        specs.append(VMEM)
        outs.append(shape(out_shape, BF16))
        out_specs.append(HBM)
        scratch = [pltpu.VMEM((rows, width), BF16), pltpu.SemaphoreType.DMA]
        if out is not None:
            aliases = {len(operands): len(outs) - 1}
            operands.append(out)
            specs.append(HBM)
    operands += after
    specs += [ANY] * len(after)
    result = pl.pallas_call(
        body,
        in_specs=specs,
        out_specs=out_specs,
        out_shape=outs,
        scratch_shapes=scratch,
        input_output_aliases=aliases,
        compiler_params=pltpu.CompilerParams(vmem_limit_bytes=SMALL_LIMIT),
        cost_estimate=light(4 * rows * width, 16 * rows * width),
        name="take_in",
    )(*operands)
    held = result[0] if has_unit else None
    return held, (result[-1] if has_total else out)


def pass_on(flag, held, met, unit, after, carried):
    rows, width = held.shape

    def body(flag_ref, held_ref, met_ref, *refs):
        total = held_ref[...] + met_ref[...]
        if unit is not None:
            total = jnp.where(flag_ref[0] == 1, total, refs[0][...])
        refs[-1 - len(carried)][...] = total

    more = [] if unit is None else [unit]
    return pl.pallas_call(
        body,
        in_specs=[SMEM] + [VMEM] * (2 + len(more)) + [HBM] * len(carried) + [ANY] * len(after),
        out_specs=[VMEM] + [HBM] * len(carried),
        out_shape=[shape((rows, width), F32)] + [shape(c.shape, c.dtype) for c in carried],
        input_output_aliases={3 + len(more) + i: 1 + i for i in range(len(carried))},
        compiler_params=pltpu.CompilerParams(vmem_limit_bytes=FULL_LIMIT if carried else SMALL_LIMIT),
        cost_estimate=light(2 * rows * width, 16 * rows * width),
        name="pass_on",
    )(flag, held, met, *more, *carried, *after)


def add_up(arrays, after, long=False):
    def body(*refs):
        total = refs[0][...]
        for ref in refs[1 : len(arrays)]:
            total = total + ref[...]
        refs[-1][...] = total

    return pl.pallas_call(
        body,
        in_specs=[VMEM] * len(arrays) + [ANY] * len(after),
        out_specs=VMEM,
        out_shape=shape(arrays[0].shape, F32),
        compiler_params=pltpu.CompilerParams(vmem_limit_bytes=SMALL_LIMIT),
        cost_estimate=cost(0, 0, True) if long else light(0, 0),
        name="add_up",
    )(*arrays, *after)


def whole_sum(unit, n):
    if n == 1:
        return unit
    if n % 2:
        return lax.psum(unit, "tensor")
    me, half = lax.axis_index("tensor"), n // 2
    held = unit
    for j in range(half - 1):
        held = unit + lax.ppermute(held, "tensor", [(j, j + 1), (n - 1 - j, n - 2 - j)])
    total = held + lax.ppermute(held, "tensor", [(half - 1, half), (half, half - 1)])
    for j in reversed(range(half - 1)):
        came = lax.ppermute(total, "tensor", [(j + 1, j), (n - 2 - j, n - 1 - j)])
        total = jnp.where((me == j) | (me == n - 1 - j), came, total)
    return total


class Line:
    LAG = 3

    def __init__(self, count, flag, finish):
        self.count, self.flag, self.finish = count, flag, finish
        self.units, self.operands, self.came, self.held, self.met = [], {}, {}, {}, {}
        self.step = 0

    def send(self, step, operand):
        pairs = [(0, 1), (3, 2)] * (step < self.count) + [(1, 0), (2, 3)] * (step >= self.LAG)
        self.operands[step] = operand
        self.came[step] = lax.ppermute(operand, "tensor", pairs)

    def pump(self, after, carried=()):
        step = self.step
        self.step += 1
        unit = self.units[step] if step < self.count else None
        held = self.finish(self, step - self.LAG, unit, self.came[step], after)
        if unit is not None:
            self.held[step] = held
            self.met[step] = lax.ppermute(held, "tensor", [(1, 2), (2, 1)])
            after = [held]
        if step == 0:
            self.send(2, self.units[2])
        elif step <= self.count:
            ahead = step + 2
            unit = self.units[ahead] if ahead < self.count else None
            operand, *carried = pass_on(self.flag, self.held[step - 1], self.met[step - 1], unit, after, carried)
            self.send(ahead, operand)
            after = [operand]
        return after, *carried


class SmallSum:
    def __init__(self, values, axis, n):
        self.values, self.axis, self.n, self.apart, self.came = values, axis, n, 1, None

    def exchange(self):
        if self.n & (self.n - 1):
            self.values, self.apart = lax.psum(self.values, self.axis), self.n
        if self.apart >= self.n:
            return False
        self.came = lax.ppermute(self.values, self.axis, [(i, i ^ self.apart) for i in range(self.n)])
        self.apart *= 2
        return True

    def add(self, after):
        self.values = add_up([self.values, self.came], after)
        return [self.values]


def rotary(span):
    half = ROT // 2
    inverse = 10000.0 ** (-(2.0 * np.arange(half)) / ROT)
    angle = np.arange(span)[:, None] * inverse[None, :]
    cosine, sine = np.cos(angle), np.sin(angle)
    ones, zeros = np.ones((span, 128 - ROT)), np.zeros((span, 128 - ROT))
    nil = np.zeros((span, half))
    tables = (
        np.concatenate([cosine, cosine, ones], 1),
        np.concatenate([-sine, nil, zeros], 1),
        np.concatenate([nil, sine, zeros], 1),
    )
    return [jnp.asarray(t, F32) for t in tables]


def make_local(dp, tp):
    def local(
        layer_input,
        lengths,
        ln1_gain,
        ln1_shift,
        w_qkv,
        b_qkv,
        w_dense,
        b_dense,
        ln2_gain,
        ln2_shift,
        w_in,
        b_in,
        w_out,
        b_out,
        grad_out,
    ):
        rows, width = layer_input.shape
        assert lengths.shape[0] == 1
        columns, units = w_dense.shape[0], w_in.shape[1]
        tables = rotary(rows)
        w_three = jnp.transpose(w_qkv, (1, 0, 2))
        vec = lambda v: v.reshape(1, -1)
        gains = (vec(ln1_gain), vec(ln1_shift), vec(ln2_gain), vec(ln2_shift))
        size, unit = 256, 128
        starts = list(range(0, rows, size))
        each = rows // unit
        me = lax.axis_index("tensor")
        flag = jnp.stack([(me == 1) | (me == 2), me == 0]).astype(jnp.int32)
        outs = [None, None]

        def finish(line, done, unit, came, after):
            if done < 0:
                return take_in(flag, unit, came, None, None, 0, None, after)[0]
            which, at = divmod(done, each)
            held, outs[which] = take_in(
                flag, unit, came, line.operands[done + line.LAG], outs[which], at, layer_input.shape, after
            )
            return held

        straight = tp != 4
        line = None if straight else Line(2 * each, flag, finish)
        queue = [] if straight else line.units

        def pump(after, *carried):
            return (after, *carried) if straight else line.pump(after, carried)

        def forward(i, held, after):
            result = forward_rows(
                starts[i], size, unit, layer_input, lengths, flag, gains, w_three, b_qkv[:, None, :], w_in, vec(b_in),
                vec(b_dense + b_out), w_dense, w_out, tables, held, after,
            )
            queue.extend(result[6:-1])
            return result[:6], result[-1:]

        held, after = forward(0, None, [])
        if not straight:
            line.send(0, queue[0])
            line.send(1, queue[1])
        held, after = forward(1, held, [])
        cotan, b_out_grad = mask_rows(lengths, grad_out, after)
        held, after = forward(2, held, pump([b_out_grad])[0])
        held, after = forward(3, held, pump(after)[0])
        a_one, a_two, qkv, mixed, hidden, slope = held

        core = lax.rem(lax.axis_index("dp"), 2).astype(jnp.int32).reshape(1)
        blocks = dp // 2
        pairs = [(i, i ^ 1) for i in range(dp)]
        groups = [[2 * i + c for i in range(blocks)] for c in range(2)]

        def other_half(name, lefts, right, slide_left, after):
            half, token = pair_product(lefts, right, slide_left, 1 - core, None, blocks, after, name)
            return half, [token]

        def own_half(name, lefts, right, slide_left, came, after):
            half, token = pair_product(lefts, right, slide_left, core, came, blocks, after, name)
            return half, [token]

        def swap(half):
            return lax.ppermute(half, "dp", pairs)

        def over_chips(half):
            return lax.psum_scatter(half, "dp", scatter_dimension=0, axis_index_groups=groups, tiled=True)[0]

        out_parts = ([hidden, mixed], cotan[None], False)
        half, after = other_half("w_out_other", *out_parts, pump(after)[0])
        after, half = pump(after, half)
        came_out = swap(half)
        dqkv, b_qkv_grad = attend_back(lengths, qkv, cotan, w_dense, tables, after)
        qkv_parts = ([a_one], dqkv, True)
        out_half, after = own_half("w_out_own", *out_parts, came_out, pump([b_qkv_grad])[0])
        half, after = other_half("w_qkv_other", *qkv_parts, after)
        after, out_half, half = pump(after, out_half, half)
        out_grads = over_chips(out_half)
        came_qkv = swap(half)

        dhpre, smalls, biases = None, [], []

        def backward(i, after):
            nonlocal dhpre
            dhpre, small, bias, *dx = backward_rows(
                starts[i], size, unit, layer_input, flag, cotan, slope, dqkv, w_three, w_in, w_out, gains, dhpre, after
            )
            queue.extend(dx)
            smalls.append(small)
            biases.append(bias)
            return [bias]

        after = backward(0, after)
        qkv_half, after = own_half("w_qkv_own", *qkv_parts, came_qkv, pump(after)[0])
        after, qkv_half = pump(after, qkv_half)
        qkv_grads = over_chips(qkv_half)
        after = backward(1, after)
        after = backward(2, pump(after)[0])
        after = backward(3, pump(after)[0])
        in_parts = ([a_two], dhpre[None], True)
        half, after = other_half("w_in_other", *in_parts, pump(after)[0])
        after, half = pump(after, half)
        came_in = swap(half)

        small = SmallSum(add_up(smalls, after, True), "tensor", tp)
        if small.exchange():
            (after,) = pump([small.values])
            after = small.add(after)
        in_half, after = own_half("w_in_own", *in_parts, came_in, after)
        after, in_half = pump(after, in_half)
        in_grads = over_chips(in_half)
        while small.exchange():
            (after,) = pump(after)
            after = small.add(after)
        flat = jnp.concatenate(
            [small.values[:4].reshape(-1), b_out_grad.reshape(-1), sum(biases).reshape(-1), b_qkv_grad.reshape(-1)]
        )
        small = SmallSum(flat.reshape(-1, 128), "dp", dp)
        while small.exchange():
            (after,) = pump(after)
            after = small.add(after)
        while not straight and line.step < line.count + line.LAG:
            (after,) = pump(after)
        flat = small.values.reshape(-1)
        gain_one, shift_one, gain_two, shift_two, b_out_grad = (
            flat[i * width : (i + 1) * width] for i in range(5)
        )
        b_in_grad = flat[5 * width : 5 * width + units]
        b_qkv_grad = flat[5 * width + units :].reshape(3, columns)
        w_out_grad, w_dense_grad = out_grads[0, :units], out_grads[0, units:]
        w_qkv_grad = jnp.transpose(qkv_grads, (1, 0, 2))
        w_in_grad = in_grads[0]

        if straight:
            totals = [whole_sum(one, tp) for one in queue]
            first, second = jnp.concatenate(totals[:each]), jnp.concatenate(totals[each:])
            outs = [first.astype(BF16), second.astype(BF16)]
        layer_output, input_grad = outs
        return (
            layer_output,
            input_grad,
            gain_one,
            shift_one,
            w_qkv_grad,
            b_qkv_grad,
            w_dense_grad,
            b_out_grad,
            gain_two,
            shift_two,
            w_in_grad,
            b_in_grad,
            w_out_grad,
            b_out_grad,
        )

    return local


def solution(mesh):
    return jax.shard_map(
        make_local(mesh.shape["dp"], mesh.shape["tensor"]),
        mesh=mesh,
        in_specs=(
            P("dp", None),
            P("dp"),
            P(),
            P(),
            P(None, None, "tensor"),
            P(None, "tensor"),
            P("tensor", None),
            P(),
            P(),
            P(),
            P(None, "tensor"),
            P("tensor"),
            P("tensor", None),
            P(),
            P("dp", None),
        ),
        out_specs=(
            P("dp", None),
            P("dp", None),
            P(),
            P(),
            P("dp", None, "tensor"),
            P(None, "tensor"),
            P("tensor", "dp"),
            P(),
            P(),
            P(),
            P("dp", "tensor"),
            P("tensor"),
            P("tensor", "dp"),
            P(),
        ),
        check_vma=False,
    )
```

```python
import math

import jax
import jax.numpy as jnp
import numpy as np
from jax import lax
from jax.experimental import pallas as pl
from jax.experimental.pallas import tpu as pltpu
from jax.sharding import PartitionSpec as P

HD = 256
ROT = 64
EPS = 1e-05
F32 = jnp.float32
BF16 = jnp.bfloat16
SMALL_LIMIT = 8 * 1024 * 1024
NT = (((1,), (1,)), ((), ()))
TN = (((0,), (0,)), ((), ()))


def dot(a, b, dims=(((1,), (0,)), ((), ()))):
    return lax.dot_general(a, b, dims, preferred_element_type=F32)


def params(mebibytes):
    return pltpu.CompilerParams(vmem_limit_bytes=mebibytes * 1024 * 1024)


def cost(flops, nbytes, long=False):
    return pl.CostEstimate(flops=int(3e11 if long else 4e10), bytes_accessed=int(nbytes), transcendentals=0)


def light(flops, nbytes):
    return pl.CostEstimate(flops=int(flops), bytes_accessed=int(nbytes), transcendentals=0)


ANY = pl.BlockSpec(memory_space=pl.ANY)
HBM = pl.BlockSpec(memory_space=pltpu.HBM)
VMEM = pl.BlockSpec(memory_space=pltpu.VMEM)
SMEM = pl.BlockSpec(memory_space=pltpu.SMEM)


def shape(dims, dtype):
    return jax.ShapeDtypeStruct(dims, dtype)


TOKEN = shape((8, 128), F32)


def in_hbm(array):
    return pltpu.with_memory_space_constraint(array, pltpu.HBM)


def in_vmem(array):
    return pltpu.with_memory_space_constraint(array, pltpu.VMEM)


def turned(values, cosine, lower, upper):
    head = values[:, :128]
    head = (
        head * cosine
        + pltpu.roll(head, 128 - ROT // 2, 1) * lower
        + pltpu.roll(head, ROT // 2, 1) * upper
    )
    return jnp.concatenate([head, values[:, 128:]], 1)


class Stream:
    def __init__(self, pieces, sems, window=4):
        self.copies = [pltpu.make_async_copy(a, b, sems.at[i]) for i, (a, b) in enumerate(pieces)]
        self.window = window
        self.done = 0
        for copy in self.copies[:window]:
            copy.start()

    def next(self):
        self.copies[self.done].wait()
        ahead = self.done + self.window
        if ahead < len(self.copies):
            self.copies[ahead].start()
        self.done += 1


class Out:
    def __init__(self, sems):
        self.sems, self.copies = sems, []

    def send(self, source, target):
        copy = pltpu.make_async_copy(source, target, self.sems.at[len(self.copies)])
        copy.start()
        self.copies.append(copy)

    def finish(self):
        for copy in self.copies:
            copy.wait()


def forward_rows(start, size, unit, x, lengths, flag, gains, w_three, b_three, w_in, b_in, b_after, w_dense, w_out, tables, held, after, carried=()):
    rows, width = x.shape
    columns, units = w_dense.shape[0], w_in.shape[1]
    heads = columns // HD
    piece = min(512, units)
    wide = min(512, width)
    scale = 1.0 / math.sqrt(HD)
    past = start > 0
    band = min(256, size)
    bands = size // band
    parts = size // unit
    steps = 3 + units // piece + 1 + width // wide
    first = 4
    sends = 4 + 2 * (units // piece) + (band // unit) * (width // wide)
    vecs = 8 + len(b_after)

    def body(*refs):
        len_ref, flag_ref, g1, s1, g2, s2, b3_ref, bi_ref, *ba_refs = refs[:vecs]
        x_hbm, c_hbm, l_hbm, u_hbm, w3_hbm, wi_hbm, wd_hbm, wo_hbm = refs[vecs : vecs + 8]
        outs = refs[-24 - parts - len(carried) : -17]
        one_hbm, two_hbm, qkv_hbm, o_hbm, hidden_hbm, slope_hbm = outs[:6]
        part_hbms, token_ref = outs[6 : 6 + parts], outs[6 + parts]
        x_ref, c_ref, l_ref, u_ref, w3, wi, wd, wo, kv_ref = refs[-17:-8]
        one_ref, two_ref, qkv_ref, o_ref, hidden_ref, slope_ref, part_ref, sems = refs[-8:]
        token_ref[...] = jnp.zeros_like(token_ref)
        mine = pl.ds(start, size)
        heads_in = [
            pltpu.make_async_copy(a.at[mine], b, sems.at[i])
            for i, (a, b) in enumerate(((x_hbm, x_ref), (c_hbm, c_ref), (l_hbm, l_ref), (u_hbm, u_ref)))
        ]
        for copy in heads_in:
            copy.start()
        pieces = [(w3_hbm.at[c], w3.at[c]) for c in range(3)]
        for low in range(0, units, piece):
            here = pl.ds(low, piece)
            pieces.append((wi_hbm.at[:, here], wi.at[:, here]))
        pieces.append((wd_hbm, wd))
        for low in range(0, width, wide):
            here = pl.ds(low, wide)
            pieces.append((wo_hbm.at[:, here], wo.at[:, here]))
        stream = Stream(pieces, sems.at[pl.ds(first, steps)])
        if past:
            earlier = pltpu.make_async_copy(
                refs[vecs + 10].at[pl.ds(1, 2), pl.ds(0, start)],
                kv_ref.at[:, pl.ds(0, start)],
                sems.at[first + steps + bands * sends],
            )
            earlier.start()
        def block(index, row, local, mine, out):
            values = x_ref[local].astype(F32)
            center = values - jnp.mean(values, -1, keepdims=True)
            spread = jnp.mean(center * center, -1, keepdims=True)
            normed = center * lax.rsqrt(spread + EPS)
            one_ref[...] = (normed * g1[...] + s1[...]).astype(BF16)
            two_ref[...] = (normed * g2[...] + s2[...]).astype(BF16)
            out.send(one_ref, one_hbm.at[mine])
            out.send(two_ref, two_hbm.at[mine])
            if index == 0:
                for copy in heads_in[1:]:
                    copy.wait()

            def place(c, acc):
                for h in range(heads):
                    cols = slice(h * HD, (h + 1) * HD)
                    one_head = acc[:, cols] + b3_ref[c : c + 1, cols]
                    if c < 2:
                        one_head = turned(one_head, c_ref[local], l_ref[local], u_ref[local])
                    qkv_ref[c, :, cols] = one_head.astype(BF16)

            before = None
            for c in range(3):
                if index == 0:
                    stream.next()
                acc = dot(one_ref[...], w3[c])
                if before is not None:
                    place(c - 1, before)
                before = acc
            place(2, before)
            out.send(qkv_ref, qkv_hbm.at[:, mine])
            if index + 1 < bands:
                kv_ref[:, row : row + band] = qkv_ref[1:]

            here = lax.broadcasted_iota(jnp.int32, (band, band), 0)
            there = lax.broadcasted_iota(jnp.int32, (band, band), 1)
            seen = (there <= here) & (there + row < length)
            if row:
                inside = lax.broadcasted_iota(jnp.int32, (band, row), 1) < length
                if index == 0:
                    earlier.wait()
            for h in range(heads):
                cols = slice(h * HD, (h + 1) * HD)
                query = qkv_ref[0, :, cols]
                now = jnp.where(seen, dot(query, qkv_ref[1, :, cols], NT) * scale, -1e30)
                top = jnp.max(now, -1, keepdims=True)
                if row:
                    old = jnp.where(inside, dot(query, kv_ref[0, :row, cols], NT) * scale, -1e30)
                    top = jnp.maximum(top, jnp.max(old, -1, keepdims=True))
                    old = jnp.exp(old - top)
                now = jnp.exp(now - top)
                total = jnp.sum(now, -1, keepdims=True)
                if row:
                    total = total + jnp.sum(old, -1, keepdims=True)
                share = 1.0 / total
                mixed = dot((now * share).astype(BF16), qkv_ref[2, :, cols])
                if row:
                    mixed = mixed + dot((old * share).astype(BF16), kv_ref[1, :row, cols])
                o_ref[:, cols] = mixed.astype(BF16)
            out.send(o_ref, o_hbm.at[mine])

            def bend(low, acc):
                cols = slice(low, low + piece)
                pre = acc + bi_ref[:, cols]
                share = 0.5 + 0.5 * lax.erf(pre * (1.0 / math.sqrt(2.0)))
                hidden_ref[:, cols] = (pre * share).astype(BF16)
                bell = jnp.exp(-0.5 * pre * pre) * (1.0 / math.sqrt(2.0 * math.pi))
                slope_ref[:, cols] = (share + pre * bell).astype(BF16)
                there = pl.ds(low, piece)
                out.send(hidden_ref.at[:, there], hidden_hbm.at[mine, there])
                out.send(slope_ref.at[:, there], slope_hbm.at[mine, there])

            before = None
            for low in range(0, units, piece):
                if index == 0:
                    stream.next()
                acc = dot(two_ref[...], wi[:, low : low + piece])
                if before is not None:
                    bend(low - piece, before)
                before = acc
            bend(units - piece, before)

            if index == 0:
                stream.next()
            for low in range(0, width, wide):
                cols = slice(low, low + wide)
                if index == 0:
                    stream.next()
                acc = dot(o_ref[...], wd[:, cols]) + dot(hidden_ref[...], wo[:, cols])
                more = x_ref[local, cols].astype(F32)
                for ba_ref in ba_refs:
                    more = more + ba_ref[:, cols]
                part_ref[:, cols] = acc + own * more
                for i, part_hbm in enumerate(part_hbms[index * (band // unit) : (index + 1) * (band // unit)]):
                    there = pl.ds(low, wide)
                    out.send(part_ref.at[pl.ds(i * unit, unit), there], part_hbm.at[:, there])

        length = len_ref[0]
        own = flag_ref[1].astype(F32)
        heads_in[0].wait()
        for index in range(bands):
            row = start + index * band
            local = slice(index * band, (index + 1) * band)
            mine = pl.ds(row, band)
            out = Out(sems.at[pl.ds(first + steps + index * sends, sends)])
            block(index, row, local, mine, out)
            out.finish()

    flat = lambda v: v.reshape(1, -1)
    small = [*gains, b_three, flat(b_in), *map(flat, b_after)]
    operands = [lengths, flag, *map(in_hbm, small), *map(in_hbm, (x, *tables, w_three, w_in, w_dense, w_out))]
    specs = [SMEM, SMEM] + [pl.BlockSpec(v.shape, lambda i: (0, 0)) for v in small] + [HBM] * 8
    aliases = {}
    if past:
        aliases = {len(operands) + i: i for i in range(6)}
        operands += [in_hbm(array) for array in held]
        specs += [HBM] * 6
    for i, array in enumerate(carried):
        aliases[len(operands)] = 7 + parts + i
        operands.append(in_hbm(array))
        specs.append(HBM)
    operands += list(after)
    specs += [ANY] * len(after)
    flops = 2 * size * width * (4 * columns + 2 * units)
    whole = [(rows, width), (rows, width), (3, rows, columns), (rows, columns), (rows, units), (rows, units)]
    mine = [(band, width), (band, width), (3, band, columns), (band, columns), (band, units), (band, units)]
    return pl.pallas_call(
        body,
        grid=(1,),
        in_specs=specs,
        out_specs=[HBM] * (6 + parts) + [pl.BlockSpec(TOKEN.shape, lambda i: (0, 0))] + [HBM] * len(carried),
        out_shape=[pltpu.HBM(dims, BF16) for dims in whole] + [pltpu.HBM((unit, width), F32)] * parts + [TOKEN] + [pltpu.HBM(c.shape, c.dtype) for c in carried],
        scratch_shapes=[pltpu.VMEM((size, width), BF16)]
        + [pltpu.VMEM((size, 128), F32)] * 3
        + [pltpu.VMEM(w.shape, BF16) for w in (w_three, w_in, w_dense, w_out)]
        + [pltpu.VMEM((2, max(start + size - band, 16), columns), BF16)]
        + [pltpu.VMEM(dims, BF16) for dims in mine]
        + [pltpu.VMEM((band, width), F32), pltpu.SemaphoreType.DMA((first + steps + bands * sends + 1,))],
        input_output_aliases=aliases,
        compiler_params=params(46),
        cost_estimate=cost(flops, 2 * width * (4 * columns + 2 * units) + size * width * 20),
        name="forward_rows",
    )(*operands)


def mask_rows(lengths, grad_out, after):
    rows, width = grad_out.shape
    step = 256

    def body(*refs):
        len_ref, g_ref = refs[:2]
        out_ref, sum_ref = refs[-2:]
        i = pl.program_id(0)
        here = lax.broadcasted_iota(jnp.int32, (step, 1), 0) + i * step
        valid = (here < len_ref[0]).astype(F32)
        kept = g_ref[...].astype(F32) * valid
        out_ref[...] = kept.astype(BF16)

        @pl.when(i == 0)
        def _():
            sum_ref[...] = jnp.zeros_like(sum_ref)

        sum_ref[...] += jnp.sum(kept, 0, keepdims=True)

    row = pl.BlockSpec((step, width), lambda i: (i, 0))
    return pl.pallas_call(
        body,
        grid=(rows // step,),
        in_specs=[SMEM, row] + [ANY] * len(after),
        out_specs=[row, pl.BlockSpec((1, width), lambda i: (0, 0))],
        out_shape=[pltpu.HBM((rows, width), BF16), shape((1, width), F32)],
        compiler_params=params(46),
        cost_estimate=cost(2 * rows * width, 4 * rows * width),
        name="mask_rows",
    )(lengths, in_hbm(grad_out), *after)


def pair_product(lefts, right, slide_left, parity, added, blocks, after, name, long=False):
    rows = right.shape[-2]
    many = right.shape[0]
    left_width = sum(left.shape[1] for left in lefts)
    block = (left_width if slide_left else right.shape[2]) // (2 * blocks)
    tall, wide = (block, right.shape[2]) if slide_left else (left_width, block)

    def body(_, *refs):
        right_ref = refs[len(lefts)]
        out_ref, token_ref = refs[-2:]
        token_ref[...] = jnp.zeros_like(token_ref)
        for c in range(many):
            low = 0
            for left_ref in refs[: len(lefts)]:
                here = slice(low, low + left_ref.shape[1])
                low += left_ref.shape[1]
                acc = dot(left_ref[...], right_ref[c], TN)
                if added is not None:
                    acc = acc + refs[len(lefts) + 1][0, c, here]
                out_ref[0, c, here] = acc

    out = pl.BlockSpec((1, many, tall, wide), lambda i, p: (i, 0, 0, 0))
    if slide_left:
        specs = [pl.BlockSpec((rows, block), lambda i, p: (0, 2 * i + p[0]))]
        specs.append(pl.BlockSpec(right.shape, lambda i, p: (0, 0, 0)))
    else:
        specs = [pl.BlockSpec(left.shape, lambda i, p: (0, 0)) for left in lefts]
        specs.append(pl.BlockSpec((many, rows, block), lambda i, p: (0, 0, 2 * i + p[0])))
    operands = [*lefts, right]
    if added is not None:
        operands.append(added)
        specs.append(out)
    return pl.pallas_call(
        body,
        grid_spec=pltpu.PrefetchScalarGridSpec(
            num_scalar_prefetch=1,
            grid=(blocks,),
            in_specs=specs + [ANY] * len(after),
            out_specs=[out, pl.BlockSpec(TOKEN.shape, lambda i, p: (0, 0))],
        ),
        out_shape=[pltpu.HBM((blocks, many, tall, wide), F32), TOKEN],
        compiler_params=params(46),
        cost_estimate=cost(2 * rows * blocks * many * tall * wide, 2 * rows * (left_width + many * right.shape[2]) + 4 * blocks * many * tall * wide, long),
        name=name,
    )(parity, *map(in_hbm, operands), *after)


def attend_back(lengths, qkv, cotan, w_dense, tables, after):
    rows, columns = qkv.shape[1:]
    width = cotan.shape[1]
    sub = min(256, rows)
    scale = 1.0 / math.sqrt(HD)

    def body(len_ref, q_ref, k_ref, v_ref, g_ref, w_ref, c_ref, l_ref, u_ref, *refs):
        out_ref, bias_ref, dk_ref, dv_ref = refs[-4:]
        length = len_ref[0]
        for low in range(0, rows, sub):
            stop = low + sub
            here = slice(low, stop)
            query, keys, values = q_ref[0, here], k_ref[0, :stop], v_ref[0, :stop]
            scores = dot(query, keys, NT) * scale
            mine = lax.broadcasted_iota(jnp.int32, scores.shape, 0) + low
            there = lax.broadcasted_iota(jnp.int32, scores.shape, 1)
            scores = jnp.where((there <= mine) & (there < length), scores, -1e30)
            expo = jnp.exp(scores - jnp.max(scores, -1, keepdims=True))
            probs = expo * (1.0 / jnp.sum(expo, -1, keepdims=True))
            dmixed = dot(g_ref[here], w_ref[...], NT).astype(BF16)
            dprobs = dot(dmixed, values, NT)
            delta = jnp.sum(probs * dprobs, -1, keepdims=True)
            dscores = (probs * (dprobs - delta)).astype(BF16)
            out_ref[0, here] = turned(
                dot(dscores, keys) * scale, c_ref[here], -l_ref[here], -u_ref[here]
            ).astype(BF16)
            dkey = dot(dscores, query, TN) * scale
            dvalue = dot(probs.astype(BF16), dmixed, TN)
            if low:
                dk_ref[:low] += dkey[:low]
                dv_ref[:low] += dvalue[:low]
            dk_ref[here] = dkey[low:]
            dv_ref[here] = dvalue[low:]
        out_ref[1] = turned(dk_ref[...], c_ref[...], -l_ref[...], -u_ref[...]).astype(BF16)
        out_ref[2] = dv_ref[...].astype(BF16)
        for part in range(3):
            bias_ref[part] = jnp.sum(out_ref[part].astype(F32), 0, keepdims=True)

    part = lambda c: pl.BlockSpec((1, rows, HD), lambda h: (c, 0, h))
    table = pl.BlockSpec((rows, 128), lambda h: (0, 0))
    return pl.pallas_call(
        body,
        grid=(columns // HD,),
        in_specs=[
            SMEM,
            part(0),
            part(1),
            part(2),
            pl.BlockSpec((rows, width), lambda h: (0, 0)),
            pl.BlockSpec((HD, width), lambda h: (h, 0)),
            table,
            table,
            table,
        ]
        + [ANY] * len(after),
        out_specs=[
            pl.BlockSpec((3, rows, HD), lambda h: (0, 0, h)),
            pl.BlockSpec((3, 1, HD), lambda h: (0, 0, h)),
        ],
        out_shape=[pltpu.HBM((3, rows, columns), BF16), shape((3, 1, columns), F32)],
        scratch_shapes=[pltpu.VMEM((rows, HD), F32)] * 2,
        compiler_params=params(46),
        cost_estimate=cost(
            2 * rows * columns * width + 10 * rows * rows * columns,
            2 * rows * (width + 7 * columns),
            True,
        ),
        name="attend_back",
    )(lengths, *map(in_hbm, (qkv, qkv, qkv, cotan, w_dense, *tables)), *after)


def backward_rows(start, size, unit, x, flag, cotan, slope, dqkv, w_three, w_in, w_out, gains, held, after):
    rows, width = x.shape
    columns, units = dqkv.shape[2], slope.shape[1]
    piece = min(512, units)
    wide = min(512, width)
    parts = size // unit
    steps = units // piece + width // wide
    sends = units // piece + parts

    def body(*refs):
        flag_ref, g1, g2, x_hbm, g_hbm, slope_hbm, q_hbm, w3_hbm, wi_hbm, wo_hbm = refs[:10]
        dh_hbm, *dx_hbms, small_ref, bias_ref = refs[-16 - parts : -13]
        x_ref, g_ref, slope_ref, q_ref, w3, wi, wo, one, two, normed_ref, dh_ref, dx_ref, sems = refs[-13:]
        mine = pl.ds(start, size)
        sources = (g_hbm.at[mine], slope_hbm.at[mine], x_hbm.at[mine], q_hbm.at[:, mine])
        inward = [
            pltpu.make_async_copy(a, b, sems.at[i])
            for i, (a, b) in enumerate(zip(sources, (g_ref, slope_ref, x_ref, q_ref)))
        ]
        for copy in inward[:2]:
            copy.start()
        pieces = []
        for low in range(0, units, piece):
            here = pl.ds(low, piece)
            pieces.append((wo_hbm.at[here], wo.at[here]))
        for low in range(0, width, wide):
            here = pl.ds(low, wide)
            pieces.append((wi_hbm.at[here], wi.at[here]))
        stream = Stream(pieces, sems.at[pl.ds(4, steps)])
        out = Out(sems.at[pl.ds(4 + steps, sends)])
        three = pltpu.make_async_copy(w3_hbm, w3, sems.at[4 + steps + sends])

        def slope_times(low, acc):
            here = slice(low, low + piece)
            grad = (acc * slope_ref[:, here].astype(F32)).astype(BF16)
            dh_ref[:, here] = grad
            bias_ref[:, here] = jnp.sum(grad.astype(F32), 0, keepdims=True)
            there = pl.ds(low, piece)
            out.send(dh_ref.at[:, there], dh_hbm.at[mine, there])

        inward[0].wait()
        before = None
        for low in range(0, units, piece):
            stream.next()
            if low == 0:
                for copy in inward[2:]:
                    copy.start()
                three.start()
                inward[1].wait()
            acc = dot(g_ref[...], wo[low : low + piece], NT)
            if before is not None:
                slope_times(low - piece, before)
            before = acc
        slope_times(units - piece, before)
        for copy in inward[2:]:
            copy.wait()
        three.wait()
        band = 64
        rstds = []
        for low in range(0, size, band):
            here = slice(low, low + band)
            values = x_ref[here].astype(F32)
            center = values - jnp.mean(values, -1, keepdims=True)
            rstds.append(lax.rsqrt(jnp.mean(center * center, -1, keepdims=True) + EPS))
            normed_ref[here] = center * rstds[-1]
        for low in range(0, width, wide):
            here = slice(low, low + wide)
            acc = dot(q_ref[0], w3[0, here], NT)
            for c in (1, 2):
                acc = acc + dot(q_ref[c], w3[c, here], NT)
            one[:, here] = acc
        for low in range(0, width, wide):
            here = slice(low, low + wide)
            stream.next()
            two[:, here] = dot(dh_ref[...], wi[here], NT)
        gain_one, gain_two = g1[...], g2[...]
        own = flag_ref[1].astype(F32)
        sums = [jnp.zeros((1, width), F32)] * 4
        for at, low in enumerate(range(0, size, band)):
            here = slice(low, low + band)
            normed, d_one, d_two = normed_ref[here], one[here], two[here]
            grad = d_one * gain_one + d_two * gain_two
            dx_ref[here] = rstds[at] * (
                grad
                - jnp.mean(grad, -1, keepdims=True)
                - normed * jnp.mean(grad * normed, -1, keepdims=True)
            ) + own * g_ref[here].astype(F32)
            terms = (d_one * normed, d_one, d_two * normed, d_two)
            sums = [s + jnp.sum(t, 0, keepdims=True) for s, t in zip(sums, terms)]
            if (low + band) % unit == 0:
                i = low // unit
                out.send(dx_ref.at[pl.ds(i * unit, unit)], dx_hbms[i])
        small_ref[...] = jnp.concatenate(sums + [jnp.zeros((4, width), F32)], 0)
        out.finish()

    vec = lambda n: pl.BlockSpec((1, n), lambda i: (0, 0))
    operands = [flag, *map(in_hbm, (gains[0], gains[2], x, cotan, slope, dqkv, w_three, w_in, w_out))]
    specs = [SMEM, vec(width), vec(width)] + [HBM] * 7
    aliases = {}
    if held is not None:
        aliases = {len(operands): 0}
        operands.append(in_hbm(held))
        specs.append(HBM)
    operands += list(after)
    specs += [ANY] * len(after)
    return pl.pallas_call(
        body,
        grid=(1,),
        in_specs=specs,
        out_specs=[HBM] * (1 + parts) + [pl.BlockSpec((8, width), lambda i: (0, 0)), vec(units)],
        out_shape=[pltpu.HBM((rows, units), BF16)]
        + [pltpu.HBM((unit, width), F32)] * parts
        + [shape((8, width), F32), shape((1, units), F32)],
        scratch_shapes=[
            pltpu.VMEM((size, width), BF16),
            pltpu.VMEM((size, width), BF16),
            pltpu.VMEM((size, units), BF16),
            pltpu.VMEM((3, size, columns), BF16),
            pltpu.VMEM(w_three.shape, BF16),
            pltpu.VMEM(w_in.shape, BF16),
            pltpu.VMEM(w_out.shape, BF16),
            pltpu.VMEM((size, width), F32),
            pltpu.VMEM((size, width), F32),
            pltpu.VMEM((size, width), F32),
            pltpu.VMEM((size, units), BF16),
            pltpu.VMEM((size, width), F32),
            pltpu.SemaphoreType.DMA((4 + steps + sends + 1,)),
        ],
        input_output_aliases=aliases,
        compiler_params=params(46),
        cost_estimate=cost(2 * size * width * (2 * units + 3 * columns), 2 * width * (2 * units + 3 * columns) + 16 * size * width, start == 0),
        name="backward_rows",
    )(*operands)


def take_in(flag, unit, came, operand, out, out_at, out_shape, after):
    rows, width = came.shape
    has_unit, has_total = unit is not None, operand is not None

    def body(*refs):
        flag_ref, came_ref = refs[:2]
        if has_total:
            out_ref, rounded, sem = refs[-3:]
            rounded[...] = jnp.where(flag_ref[0] == 1, refs[2 + has_unit][...], came_ref[...]).astype(BF16)
            copy = pltpu.make_async_copy(rounded, out_ref.at[pl.ds(out_at * rows, rows)], sem)
            copy.start()
        if has_unit:
            refs[-4 if has_total else -1][...] = refs[2][...] + came_ref[...]
        if has_total:
            copy.wait()

    operands, specs = [flag, in_vmem(came)], [SMEM, VMEM]
    outs, out_specs, aliases, scratch = [], [], {}, []
    if has_unit:
        operands.append(unit)
        specs.append(VMEM)
        outs.append(pltpu.VMEM((rows, width), F32))
        out_specs.append(VMEM)
    if has_total:
        operands.append(in_vmem(operand))
        specs.append(VMEM)
        outs.append(pltpu.HBM(out_shape, BF16))
        out_specs.append(HBM)
        scratch = [pltpu.VMEM((rows, width), BF16), pltpu.SemaphoreType.DMA]
        if out is not None:
            aliases = {len(operands): len(outs) - 1}
            operands.append(in_hbm(out))
            specs.append(HBM)
    operands += after
    specs += [ANY] * len(after)
    result = pl.pallas_call(
        body,
        in_specs=specs,
        out_specs=out_specs,
        out_shape=outs,
        scratch_shapes=scratch,
        input_output_aliases=aliases,
        compiler_params=pltpu.CompilerParams(vmem_limit_bytes=SMALL_LIMIT),
        cost_estimate=light(4 * rows * width, 16 * rows * width),
        name="take_in",
    )(*operands)
    held = result[0] if has_unit else None
    return held, (result[-1] if has_total else out)


def pass_on(flag, held, met, unit, after, carried):
    rows, width = held.shape

    def body(flag_ref, held_ref, met_ref, *refs):
        total = held_ref[...] + met_ref[...]
        if unit is not None:
            total = jnp.where(flag_ref[0] == 1, total, refs[0][...])
        refs[-1 - len(carried)][...] = total

    more = [] if unit is None else [unit]
    return pl.pallas_call(
        body,
        in_specs=[SMEM] + [VMEM] * (2 + len(more)) + [HBM] * len(carried) + [ANY] * len(after),
        out_specs=[VMEM] + [HBM] * len(carried),
        out_shape=[pltpu.VMEM((rows, width), F32)] + [pltpu.HBM(c.shape, c.dtype) for c in carried],
        input_output_aliases={3 + len(more) + i: 1 + i for i in range(len(carried))},
        compiler_params=pltpu.CompilerParams(vmem_limit_bytes=SMALL_LIMIT),
        cost_estimate=light(2 * rows * width, 16 * rows * width),
        name="pass_on",
    )(flag, in_vmem(held), in_vmem(met), *more, *map(in_hbm, carried), *after)


def add_up(arrays, after, long=False):
    def body(*refs):
        total = refs[0][...]
        for ref in refs[1 : len(arrays)]:
            total = total + ref[...]
        refs[-1][...] = total

    return pl.pallas_call(
        body,
        in_specs=[VMEM] * len(arrays) + [ANY] * len(after),
        out_specs=VMEM,
        out_shape=shape(arrays[0].shape, F32),
        compiler_params=pltpu.CompilerParams(vmem_limit_bytes=SMALL_LIMIT),
        cost_estimate=cost(0, 0, True) if long else light(0, 0),
        name="add_up",
    )(*arrays, *after)


def split_rows(array, at, after):
    rows, width = array.shape
    step = math.gcd(at, rows - at)
    first = at // step

    def body(in_ref, *refs):
        one_ref, two_ref = refs[-2:]
        i = pl.program_id(0)

        @pl.when(i < first)
        def _():
            one_ref[...] = in_ref[...]

        @pl.when(i >= first)
        def _():
            two_ref[...] = in_ref[...]

    block = (step, width)
    return pl.pallas_call(
        body,
        grid=(rows // step,),
        in_specs=[pl.BlockSpec(block, lambda i: (i, 0))] + [ANY] * len(after),
        out_specs=[
            pl.BlockSpec(block, lambda i: (jnp.minimum(i, first - 1), 0)),
            pl.BlockSpec(block, lambda i: (jnp.maximum(i - first, 0), 0)),
        ],
        out_shape=[pltpu.HBM((at, width), F32), pltpu.HBM((rows - at, width), F32)],
        compiler_params=pltpu.CompilerParams(vmem_limit_bytes=SMALL_LIMIT),
        cost_estimate=light(0, 8 * rows * width),
        name="split_rows",
    )(in_hbm(array), *after)


def rounded(array):
    def body(in_ref, out_ref):
        out_ref[...] = in_ref[...].astype(BF16)

    block = pl.BlockSpec((min(128, array.shape[0]), array.shape[1]), lambda i: (i, 0))
    return pl.pallas_call(
        body,
        grid=(array.shape[0] // block.block_shape[0],),
        in_specs=[block],
        out_specs=block,
        out_shape=shape(array.shape, BF16),
        name="rounded",
    )(array)


def whole_sum(unit, n):
    if n == 1:
        return unit
    if n % 2:
        return lax.psum(unit, "tensor")
    me, half = lax.axis_index("tensor"), n // 2
    held = unit
    for j in range(half - 1):
        held = unit + lax.ppermute(held, "tensor", [(j, j + 1), (n - 1 - j, n - 2 - j)])
    total = held + lax.ppermute(held, "tensor", [(half - 1, half), (half, half - 1)])
    for j in reversed(range(half - 1)):
        came = lax.ppermute(total, "tensor", [(j + 1, j), (n - 2 - j, n - 1 - j)])
        total = jnp.where((me == j) | (me == n - 1 - j), came, total)
    return total


class Line:
    LAG = 3

    def __init__(self, count, flag, finish):
        self.count, self.flag, self.finish = count, flag, finish
        self.units, self.operands, self.came, self.held, self.met = [], {}, {}, {}, {}
        self.step = 0

    def send(self, step, operand):
        pairs = [(0, 1), (3, 2)] * (step < self.count) + [(1, 0), (2, 3)] * (step >= self.LAG)
        self.operands[step] = operand
        self.came[step] = lax.ppermute(operand, "tensor", pairs)

    def pump(self, after, carried=()):
        step = self.step
        self.step += 1
        unit = self.units[step] if step < self.count else None
        held = self.finish(self, step - self.LAG, unit, self.came[step], after)
        if unit is not None:
            self.held[step] = held
            self.met[step] = lax.ppermute(held, "tensor", [(1, 2), (2, 1)])
            after = [held]
        if step == 0:
            self.send(2, self.units[2])
        elif step <= self.count:
            ahead = step + 2
            unit = self.units[ahead] if ahead < self.count else None
            operand, *carried = pass_on(self.flag, self.held[step - 1], self.met[step - 1], unit, after, carried)
            self.send(ahead, operand)
            after = [operand]
        return after, *carried


class SmallSum:
    def __init__(self, values, axis, n):
        self.values, self.axis, self.n, self.apart, self.came = values, axis, n, 1, None

    def exchange(self):
        if self.n & (self.n - 1):
            self.values, self.apart = lax.psum(self.values, self.axis), self.n
        if self.apart >= self.n:
            return False
        self.came = lax.ppermute(self.values, self.axis, [(i, i ^ self.apart) for i in range(self.n)])
        self.apart *= 2
        return True

    def add(self, after, long=False):
        if self.came is not None:
            self.values, self.came = add_up([self.values, self.came], after, long), None
        return [self.values]


def rotary(span):
    half = ROT // 2
    inverse = 10000.0 ** (-(2.0 * np.arange(half)) / ROT)
    angle = np.arange(span)[:, None] * inverse[None, :]
    cosine, sine = np.cos(angle), np.sin(angle)
    ones, zeros = np.ones((span, 128 - ROT)), np.zeros((span, 128 - ROT))
    nil = np.zeros((span, half))
    tables = (
        np.concatenate([cosine, cosine, ones], 1),
        np.concatenate([-sine, nil, zeros], 1),
        np.concatenate([nil, sine, zeros], 1),
    )
    return [jnp.asarray(t, F32) for t in tables]


def make_local(dp, tp):
    def local(
        layer_input,
        lengths,
        ln1_gain,
        ln1_shift,
        w_qkv,
        b_qkv,
        w_dense,
        b_dense,
        ln2_gain,
        ln2_shift,
        w_in,
        b_in,
        w_out,
        b_out,
        grad_out,
    ):
        rows, width = layer_input.shape
        assert lengths.shape[0] == 1
        columns, units = w_dense.shape[0], w_in.shape[1]
        tables = rotary(rows)
        w_three = jnp.transpose(w_qkv, (1, 0, 2))
        vec = lambda v: v.reshape(1, -1)
        gains = (vec(ln1_gain), vec(ln1_shift), vec(ln2_gain), vec(ln2_shift))
        size, unit = 256, 128
        starts = list(range(0, rows, size))
        each = rows // unit
        me = lax.axis_index("tensor")
        flag = jnp.stack([(me == 1) | (me == 2), me == 0]).astype(jnp.int32)
        outs = [None, None]

        def finish(line, done, unit, came, after):
            if done < 0:
                return take_in(flag, unit, came, None, None, 0, None, after)[0]
            which, at = divmod(done, each)
            held, outs[which] = take_in(
                flag, unit, came, line.operands[done + line.LAG], outs[which], at, layer_input.shape, after
            )
            return held

        straight = tp != 4
        line = None if straight else Line(2 * each, flag, finish)
        queue = [] if straight else line.units

        def pump(after, *carried):
            if straight or line.step == line.count + line.LAG:
                return (after, *carried)
            return line.pump(after, carried)

        def forward(start, size, held, after, carried=()):
            result = forward_rows(
                start, size, unit, layer_input, lengths, flag, gains, w_three, b_qkv, w_in, b_in, (b_dense, b_out),
                w_dense, w_out, tables, held, after, carried,
            )
            parts = size // unit
            queue.extend(result[6 : 6 + parts])
            return result[:6], [result[6 + parts]], result[7 + parts :]

        held, after, _ = forward(0, size, None, [])
        if not straight:
            line.send(0, queue[0])
        held, after, (queue[1],) = forward(size, size, held, [], [queue[1]])
        if not straight:
            line.send(1, queue[1])
        cotan, b_out_grad = mask_rows(lengths, grad_out, after)
        held, after, _ = forward(2 * size, rows - 2 * size, held, pump([b_out_grad])[0])
        a_one, a_two, qkv, mixed, hidden, slope = held

        core = lax.rem(lax.axis_index("dp"), 2).astype(jnp.int32).reshape(1)
        blocks = dp // 2
        pairs = [(i, i ^ 1) for i in range(dp)]
        groups = [[2 * i + c for i in range(blocks)] for c in range(2)]

        def other_half(name, lefts, right, slide_left, after, long=False):
            half, token = pair_product(lefts, right, slide_left, 1 - core, None, blocks, after, name, long)
            return half, [token]

        def own_half(name, lefts, right, slide_left, came, after, long=False):
            half, token = pair_product(lefts, right, slide_left, core, came, blocks, after, name, long)
            return half, [token]

        def swap(half):
            return lax.ppermute(half, "dp", pairs)

        def over_chips(half):
            return lax.psum_scatter(half, "dp", scatter_dimension=0, axis_index_groups=groups, tiled=True)[0]

        out_parts = ([hidden, mixed], cotan[None], False)
        half, after = other_half("w_out_other", *out_parts, pump(after)[0])
        after, half = pump(after, half)
        came_out = swap(half)
        dqkv, b_qkv_grad = attend_back(lengths, qkv, cotan, w_dense, tables, after)
        qkv_parts = ([a_one], dqkv, True)
        out_half, after = own_half("w_out_own", *out_parts, came_out, pump([b_qkv_grad])[0])
        after, out_half = pump(after, out_half)
        out_grads = over_chips(out_half)

        dhpre, smalls, biases = None, [], []

        def backward(i, after):
            nonlocal dhpre
            dhpre, *dx, small, bias = backward_rows(
                starts[i], size, unit, layer_input, flag, cotan, slope, dqkv, w_three, w_in, w_out, gains, dhpre, after
            )
            queue.extend(dx)
            smalls.append(small)
            biases.append(bias)
            return [bias]

        after = backward(0, after)
        after = backward(1, pump(after)[0])
        after = backward(2, pump(after)[0])
        after = backward(3, pump(after)[0])

        small = SmallSum(add_up(smalls, after), "tensor", tp)
        after = [small.values]
        more = small.exchange()
        half, after = other_half("w_qkv_other", *qkv_parts, pump(after)[0])
        after, half = pump(after, half)
        came_qkv = swap(half)
        in_parts = ([a_two], dhpre[None], True)
        half, after = other_half("w_in_other", *in_parts, after, True)
        after, half = pump(after, half)
        came_in = swap(half)
        after = small.add(after)
        more = more and small.exchange()
        qkv_half, after = own_half("w_qkv_own", *qkv_parts, came_qkv, after, True)
        after, qkv_half = pump(after, qkv_half)
        qkv_grads = over_chips(qkv_half)
        in_half, after = own_half("w_in_own", *in_parts, came_in, after, True)
        after, in_half = pump(after, in_half)
        in_grads = over_chips(in_half)
        after = small.add(after, True)
        while more and small.exchange():
            after = pump(pump(after)[0])[0]
            after = small.add(after)
        flat = jnp.concatenate(
            [small.values[:4].reshape(-1), b_out_grad.reshape(-1), sum(biases).reshape(-1), b_qkv_grad.reshape(-1)]
        )
        small = SmallSum(flat.reshape(-1, 128), "dp", dp)
        while small.exchange():
            (after,) = pump(after)
            after = small.add(after)
        w_out_grad, w_dense_grad = split_rows(out_grads[0], units, after)
        after = [w_dense_grad]
        while not straight and line.step < line.count + line.LAG:
            (after,) = pump(after)
        flat = small.values.reshape(-1)
        gain_one, shift_one, gain_two, shift_two, b_out_grad = (
            flat[i * width : (i + 1) * width] for i in range(5)
        )
        b_in_grad = flat[5 * width : 5 * width + units]
        b_qkv_grad = flat[5 * width + units :].reshape(3, columns)
        w_qkv_grad = jnp.transpose(qkv_grads, (1, 0, 2))
        w_in_grad = in_grads[0]

        if straight:
            totals = [whole_sum(one, tp) for one in queue]
            first, second = jnp.concatenate(totals[:each]), jnp.concatenate(totals[each:])
            outs = [rounded(first), rounded(second)]
        layer_output, input_grad = outs
        return (
            layer_output,
            input_grad,
            gain_one,
            shift_one,
            w_qkv_grad,
            b_qkv_grad,
            w_dense_grad,
            b_out_grad,
            gain_two,
            shift_two,
            w_in_grad,
            b_in_grad,
            w_out_grad,
            b_out_grad,
        )

    return local


def solution(mesh):
    return jax.shard_map(
        make_local(mesh.shape["dp"], mesh.shape["tensor"]),
        mesh=mesh,
        in_specs=(
            P("dp", None),
            P("dp"),
            P(),
            P(),
            P(None, None, "tensor"),
            P(None, "tensor"),
            P("tensor", None),
            P(),
            P(),
            P(),
            P(None, "tensor"),
            P("tensor"),
            P("tensor", None),
            P(),
            P("dp", None),
        ),
        out_specs=(
            P("dp", None),
            P("dp", None),
            P(),
            P(),
            P("dp", None, "tensor"),
            P(None, "tensor"),
            P("tensor", "dp"),
            P(),
            P(),
            P(),
            P("dp", "tensor"),
            P("tensor"),
            P("tensor", "dp"),
            P(),
        ),
        check_vma=False,
    )
```

```python
import math

import jax
import jax.numpy as jnp
import numpy as np
from jax import lax
from jax.experimental import pallas as pl
from jax.experimental.pallas import tpu as pltpu
from jax.sharding import PartitionSpec as P

HD = 256
ROT = 64
EPS = 1e-05
F32 = jnp.float32
BF16 = jnp.bfloat16
SMALL_LIMIT = 8 * 1024 * 1024
NT = (((1,), (1,)), ((), ()))
TN = (((0,), (0,)), ((), ()))


def dot(a, b, dims=(((1,), (0,)), ((), ()))):
    return lax.dot_general(a, b, dims, preferred_element_type=F32)


def params(mebibytes):
    return pltpu.CompilerParams(vmem_limit_bytes=mebibytes * 1024 * 1024)


def cost(flops, nbytes, long=False):
    return pl.CostEstimate(flops=int(3e11 if long else 4e10), bytes_accessed=int(nbytes), transcendentals=0)


def alone(flops, nbytes):
    return pl.CostEstimate(flops=int(3e10), bytes_accessed=int(nbytes), transcendentals=0)


def light(flops, nbytes):
    return pl.CostEstimate(flops=int(flops), bytes_accessed=int(nbytes), transcendentals=0)


ANY = pl.BlockSpec(memory_space=pl.ANY)
HBM = pl.BlockSpec(memory_space=pltpu.HBM)
VMEM = pl.BlockSpec(memory_space=pltpu.VMEM)
SMEM = pl.BlockSpec(memory_space=pltpu.SMEM)


def shape(dims, dtype):
    return jax.ShapeDtypeStruct(dims, dtype)


TOKEN = shape((8, 128), F32)


def in_hbm(array):
    return pltpu.with_memory_space_constraint(array, pltpu.HBM)


def in_vmem(array):
    return pltpu.with_memory_space_constraint(array, pltpu.VMEM)


def turned(values, cosine, lower, upper):
    head = values[:, :128]
    head = (
        head * cosine
        + pltpu.roll(head, 128 - ROT // 2, 1) * lower
        + pltpu.roll(head, ROT // 2, 1) * upper
    )
    return jnp.concatenate([head, values[:, 128:]], 1)


class Stream:
    def __init__(self, pieces, sems, window=4):
        self.copies = [pltpu.make_async_copy(a, b, sems.at[i]) for i, (a, b) in enumerate(pieces)]
        self.window = window
        self.done = 0
        for copy in self.copies[:window]:
            copy.start()

    def next(self):
        self.copies[self.done].wait()
        ahead = self.done + self.window
        if ahead < len(self.copies):
            self.copies[ahead].start()
        self.done += 1


class Out:
    def __init__(self, sems):
        self.sems, self.copies = sems, []

    def send(self, source, target):
        copy = pltpu.make_async_copy(source, target, self.sems.at[len(self.copies)])
        copy.start()
        self.copies.append(copy)

    def finish(self):
        for copy in self.copies:
            copy.wait()


def forward_rows(start, size, unit, x, lengths, flag, gains, w_three, b_three, w_in, b_in, b_after, w_dense, w_out, tables, held, after, carried=()):
    rows, width = x.shape
    columns, units = w_dense.shape[0], w_in.shape[1]
    heads = columns // HD
    piece = min(512, units)
    wide = min(512, width)
    scale = 1.0 / math.sqrt(HD)
    past = start > 0
    band = min(256, size)
    bands = size // band
    parts = size // unit
    steps = 3 + units // piece + 1 + width // wide
    first = 4
    sends = 4 + 2 * (units // piece) + (band // unit) * (width // wide)
    vecs = 8 + len(b_after)

    def body(*refs):
        len_ref, flag_ref, g1, s1, g2, s2, b3_ref, bi_ref, *ba_refs = refs[:vecs]
        x_hbm, c_hbm, l_hbm, u_hbm, w3_hbm, wi_hbm, wd_hbm, wo_hbm = refs[vecs : vecs + 8]
        outs = refs[-24 - parts - len(carried) : -17]
        one_hbm, two_hbm, qkv_hbm, o_hbm, hidden_hbm, slope_hbm = outs[:6]
        part_hbms, token_ref = outs[6 : 6 + parts], outs[6 + parts]
        x_ref, c_ref, l_ref, u_ref, w3, wi, wd, wo, kv_ref = refs[-17:-8]
        one_ref, two_ref, qkv_ref, o_ref, hidden_ref, slope_ref, part_ref, sems = refs[-8:]
        token_ref[...] = jnp.zeros_like(token_ref)
        mine = pl.ds(start, size)
        heads_in = [
            pltpu.make_async_copy(a.at[mine], b, sems.at[i])
            for i, (a, b) in enumerate(((x_hbm, x_ref), (c_hbm, c_ref), (l_hbm, l_ref), (u_hbm, u_ref)))
        ]
        for copy in heads_in:
            copy.start()
        pieces = [(w3_hbm.at[c], w3.at[c]) for c in range(3)]
        for low in range(0, units, piece):
            here = pl.ds(low, piece)
            pieces.append((wi_hbm.at[:, here], wi.at[:, here]))
        pieces.append((wd_hbm, wd))
        for low in range(0, width, wide):
            here = pl.ds(low, wide)
            pieces.append((wo_hbm.at[:, here], wo.at[:, here]))
        stream = Stream(pieces, sems.at[pl.ds(first, steps)])
        if past:
            earlier = pltpu.make_async_copy(
                refs[vecs + 10].at[pl.ds(1, 2), pl.ds(0, start)],
                kv_ref.at[:, pl.ds(0, start)],
                sems.at[first + steps + bands * sends],
            )
            earlier.start()
        def block(index, row, local, mine, out):
            values = x_ref[local].astype(F32)
            center = values - jnp.mean(values, -1, keepdims=True)
            spread = jnp.mean(center * center, -1, keepdims=True)
            normed = center * lax.rsqrt(spread + EPS)
            one_ref[...] = (normed * g1[...] + s1[...]).astype(BF16)
            two_ref[...] = (normed * g2[...] + s2[...]).astype(BF16)
            out.send(one_ref, one_hbm.at[mine])
            out.send(two_ref, two_hbm.at[mine])
            if index == 0:
                for copy in heads_in[1:]:
                    copy.wait()

            def place(c, acc):
                for h in range(heads):
                    cols = slice(h * HD, (h + 1) * HD)
                    one_head = acc[:, cols] + b3_ref[c : c + 1, cols]
                    if c < 2:
                        one_head = turned(one_head, c_ref[local], l_ref[local], u_ref[local])
                    qkv_ref[c, :, cols] = one_head.astype(BF16)

            before = None
            for c in range(3):
                if index == 0:
                    stream.next()
                acc = dot(one_ref[...], w3[c])
                if before is not None:
                    place(c - 1, before)
                before = acc
            place(2, before)
            out.send(qkv_ref, qkv_hbm.at[:, mine])
            if index + 1 < bands:
                kv_ref[:, row : row + band] = qkv_ref[1:]

            here = lax.broadcasted_iota(jnp.int32, (band, band), 0)
            there = lax.broadcasted_iota(jnp.int32, (band, band), 1)
            seen = (there <= here) & (there + row < length)
            if row:
                inside = lax.broadcasted_iota(jnp.int32, (band, row), 1) < length
                if index == 0:
                    earlier.wait()
            for h in range(heads):
                cols = slice(h * HD, (h + 1) * HD)
                query = qkv_ref[0, :, cols]
                now = jnp.where(seen, dot(query, qkv_ref[1, :, cols], NT) * scale, -1e30)
                top = jnp.max(now, -1, keepdims=True)
                if row:
                    old = jnp.where(inside, dot(query, kv_ref[0, :row, cols], NT) * scale, -1e30)
                    top = jnp.maximum(top, jnp.max(old, -1, keepdims=True))
                    old = jnp.exp(old - top)
                now = jnp.exp(now - top)
                total = jnp.sum(now, -1, keepdims=True)
                if row:
                    total = total + jnp.sum(old, -1, keepdims=True)
                share = 1.0 / total
                mixed = dot((now * share).astype(BF16), qkv_ref[2, :, cols])
                if row:
                    mixed = mixed + dot((old * share).astype(BF16), kv_ref[1, :row, cols])
                o_ref[:, cols] = mixed.astype(BF16)
            out.send(o_ref, o_hbm.at[mine])

            def bend(low, acc):
                cols = slice(low, low + piece)
                pre = acc + bi_ref[:, cols]
                share = 0.5 + 0.5 * lax.erf(pre * (1.0 / math.sqrt(2.0)))
                hidden_ref[:, cols] = (pre * share).astype(BF16)
                bell = jnp.exp(-0.5 * pre * pre) * (1.0 / math.sqrt(2.0 * math.pi))
                slope_ref[:, cols] = (share + pre * bell).astype(BF16)
                there = pl.ds(low, piece)
                out.send(hidden_ref.at[:, there], hidden_hbm.at[mine, there])
                out.send(slope_ref.at[:, there], slope_hbm.at[mine, there])

            before = None
            for low in range(0, units, piece):
                if index == 0:
                    stream.next()
                acc = dot(two_ref[...], wi[:, low : low + piece])
                if before is not None:
                    bend(low - piece, before)
                before = acc
            bend(units - piece, before)

            if index == 0:
                stream.next()
            for low in range(0, width, wide):
                cols = slice(low, low + wide)
                if index == 0:
                    stream.next()
                acc = dot(o_ref[...], wd[:, cols]) + dot(hidden_ref[...], wo[:, cols])
                more = x_ref[local, cols].astype(F32)
                for ba_ref in ba_refs:
                    more = more + ba_ref[:, cols]
                part_ref[:, cols] = acc + own * more
                for i, part_hbm in enumerate(part_hbms[index * (band // unit) : (index + 1) * (band // unit)]):
                    there = pl.ds(low, wide)
                    out.send(part_ref.at[pl.ds(i * unit, unit), there], part_hbm.at[:, there])

        length = len_ref[0]
        own = flag_ref[1].astype(F32)
        heads_in[0].wait()
        for index in range(bands):
            row = start + index * band
            local = slice(index * band, (index + 1) * band)
            mine = pl.ds(row, band)
            out = Out(sems.at[pl.ds(first + steps + index * sends, sends)])
            block(index, row, local, mine, out)
            out.finish()

    flat = lambda v: v.reshape(1, -1)
    small = [*gains, b_three, flat(b_in), *map(flat, b_after)]
    operands = [lengths, flag, *map(in_hbm, small), *map(in_hbm, (x, *tables, w_three, w_in, w_dense, w_out))]
    specs = [SMEM, SMEM] + [pl.BlockSpec(v.shape, lambda i: (0, 0)) for v in small] + [HBM] * 8
    aliases = {}
    if past:
        aliases = {len(operands) + i: i for i in range(6)}
        operands += [in_hbm(array) for array in held]
        specs += [HBM] * 6
    for i, array in enumerate(carried):
        aliases[len(operands)] = 7 + parts + i
        operands.append(in_hbm(array))
        specs.append(HBM)
    operands += list(after)
    specs += [ANY] * len(after)
    flops = 2 * size * width * (4 * columns + 2 * units)
    whole = [(rows, width), (rows, width), (3, rows, columns), (rows, columns), (rows, units), (rows, units)]
    mine = [(band, width), (band, width), (3, band, columns), (band, columns), (band, units), (band, units)]
    return pl.pallas_call(
        body,
        grid=(1,),
        in_specs=specs,
        out_specs=[HBM] * (6 + parts) + [pl.BlockSpec(TOKEN.shape, lambda i: (0, 0))] + [HBM] * len(carried),
        out_shape=[pltpu.HBM(dims, BF16) for dims in whole] + [pltpu.HBM((unit, width), F32)] * parts + [TOKEN] + [pltpu.HBM(c.shape, c.dtype) for c in carried],
        scratch_shapes=[pltpu.VMEM((size, width), BF16)]
        + [pltpu.VMEM((size, 128), F32)] * 3
        + [pltpu.VMEM(w.shape, BF16) for w in (w_three, w_in, w_dense, w_out)]
        + [pltpu.VMEM((2, max(start + size - band, 16), columns), BF16)]
        + [pltpu.VMEM(dims, BF16) for dims in mine]
        + [pltpu.VMEM((band, width), F32), pltpu.SemaphoreType.DMA((first + steps + bands * sends + 1,))],
        input_output_aliases=aliases,
        compiler_params=params(46),
        cost_estimate=cost(flops, 2 * width * (4 * columns + 2 * units) + size * width * 20),
        name="forward_rows",
    )(*operands)


def mask_rows(lengths, grad_out, after):
    rows, width = grad_out.shape
    step = 256

    def body(*refs):
        len_ref, g_ref = refs[:2]
        out_ref, sum_ref = refs[-2:]
        i = pl.program_id(0)
        here = lax.broadcasted_iota(jnp.int32, (step, 1), 0) + i * step
        valid = (here < len_ref[0]).astype(F32)
        kept = g_ref[...].astype(F32) * valid
        out_ref[...] = kept.astype(BF16)

        @pl.when(i == 0)
        def _():
            sum_ref[...] = jnp.zeros_like(sum_ref)

        sum_ref[...] += jnp.sum(kept, 0, keepdims=True)

    row = pl.BlockSpec((step, width), lambda i: (i, 0))
    return pl.pallas_call(
        body,
        grid=(rows // step,),
        in_specs=[SMEM, row] + [ANY] * len(after),
        out_specs=[row, pl.BlockSpec((1, width), lambda i: (0, 0))],
        out_shape=[pltpu.HBM((rows, width), BF16), shape((1, width), F32)],
        compiler_params=params(46),
        cost_estimate=cost(2 * rows * width, 4 * rows * width),
        name="mask_rows",
    )(lengths, in_hbm(grad_out), *after)


def pair_product(lefts, right, slide_left, parity, added, blocks, after, name, long=False, apart=2):
    rows = right.shape[-2]
    many = right.shape[0]
    left_width = sum(left.shape[1] for left in lefts)
    block = (left_width if slide_left else right.shape[2]) // (apart * blocks)
    tall, wide = (block, right.shape[2]) if slide_left else (left_width, block)

    def body(_, *refs):
        right_ref = refs[len(lefts)]
        out_ref, token_ref = refs[-2:]
        token_ref[...] = jnp.zeros_like(token_ref)
        for c in range(many):
            low = 0
            for left_ref in refs[: len(lefts)]:
                here = slice(low, low + left_ref.shape[1])
                low += left_ref.shape[1]
                acc = dot(left_ref[...], right_ref[c], TN)
                if added is not None:
                    acc = acc + refs[len(lefts) + 1][0, c, here]
                out_ref[0, c, here] = acc

    out = pl.BlockSpec((1, many, tall, wide), lambda i, p: (i, 0, 0, 0))
    if slide_left:
        specs = [pl.BlockSpec((rows, block), lambda i, p: (0, apart * i + p[0]))]
        specs.append(pl.BlockSpec(right.shape, lambda i, p: (0, 0, 0)))
    else:
        specs = [pl.BlockSpec(left.shape, lambda i, p: (0, 0)) for left in lefts]
        specs.append(pl.BlockSpec((many, rows, block), lambda i, p: (0, 0, apart * i + p[0])))
    operands = [*lefts, right]
    if added is not None:
        operands.append(added)
        specs.append(out)
    return pl.pallas_call(
        body,
        grid_spec=pltpu.PrefetchScalarGridSpec(
            num_scalar_prefetch=1,
            grid=(blocks,),
            in_specs=specs + [ANY] * len(after),
            out_specs=[out, pl.BlockSpec(TOKEN.shape, lambda i, p: (0, 0))],
        ),
        out_shape=[pltpu.HBM((blocks, many, tall, wide), F32), TOKEN],
        compiler_params=params(46),
        cost_estimate=cost(2 * rows * blocks * many * tall * wide, 2 * rows * (left_width + many * right.shape[2]) + 4 * blocks * many * tall * wide, long),
        name=name,
    )(parity, *map(in_hbm, operands), *after)


def attend_back(lengths, qkv, cotan, w_dense, tables, after):
    rows, columns = qkv.shape[1:]
    width = cotan.shape[1]
    sub = min(256, rows)
    scale = 1.0 / math.sqrt(HD)

    def body(len_ref, q_ref, k_ref, v_ref, g_ref, w_ref, c_ref, l_ref, u_ref, *refs):
        out_ref, bias_ref, dk_ref, dv_ref = refs[-4:]
        length = len_ref[0]
        for low in range(0, rows, sub):
            stop = low + sub
            here = slice(low, stop)
            query, keys, values = q_ref[0, here], k_ref[0, :stop], v_ref[0, :stop]
            scores = dot(query, keys, NT) * scale
            mine = lax.broadcasted_iota(jnp.int32, scores.shape, 0) + low
            there = lax.broadcasted_iota(jnp.int32, scores.shape, 1)
            scores = jnp.where((there <= mine) & (there < length), scores, -1e30)
            expo = jnp.exp(scores - jnp.max(scores, -1, keepdims=True))
            probs = expo * (1.0 / jnp.sum(expo, -1, keepdims=True))
            dmixed = dot(g_ref[here], w_ref[...], NT).astype(BF16)
            dprobs = dot(dmixed, values, NT)
            delta = jnp.sum(probs * dprobs, -1, keepdims=True)
            dscores = (probs * (dprobs - delta)).astype(BF16)
            out_ref[0, here] = turned(
                dot(dscores, keys) * scale, c_ref[here], -l_ref[here], -u_ref[here]
            ).astype(BF16)
            dkey = dot(dscores, query, TN) * scale
            dvalue = dot(probs.astype(BF16), dmixed, TN)
            if low:
                dk_ref[:low] += dkey[:low]
                dv_ref[:low] += dvalue[:low]
            dk_ref[here] = dkey[low:]
            dv_ref[here] = dvalue[low:]
        out_ref[1] = turned(dk_ref[...], c_ref[...], -l_ref[...], -u_ref[...]).astype(BF16)
        out_ref[2] = dv_ref[...].astype(BF16)
        for part in range(3):
            bias_ref[part] = jnp.sum(out_ref[part].astype(F32), 0, keepdims=True)

    part = lambda c: pl.BlockSpec((1, rows, HD), lambda h: (c, 0, h))
    table = pl.BlockSpec((rows, 128), lambda h: (0, 0))
    return pl.pallas_call(
        body,
        grid=(columns // HD,),
        in_specs=[
            SMEM,
            part(0),
            part(1),
            part(2),
            pl.BlockSpec((rows, width), lambda h: (0, 0)),
            pl.BlockSpec((HD, width), lambda h: (h, 0)),
            table,
            table,
            table,
        ]
        + [ANY] * len(after),
        out_specs=[
            pl.BlockSpec((3, rows, HD), lambda h: (0, 0, h)),
            pl.BlockSpec((3, 1, HD), lambda h: (0, 0, h)),
        ],
        out_shape=[pltpu.HBM((3, rows, columns), BF16), shape((3, 1, columns), F32)],
        scratch_shapes=[pltpu.VMEM((rows, HD), F32)] * 2,
        compiler_params=params(46),
        cost_estimate=cost(
            2 * rows * columns * width + 10 * rows * rows * columns,
            2 * rows * (width + 7 * columns),
            True,
        ),
        name="attend_back",
    )(lengths, *map(in_hbm, (qkv, qkv, qkv, cotan, w_dense, *tables)), *after)


def backward_rows(start, size, unit, x, flag, cotan, slope, dqkv, w_three, w_in, w_out, gains, held, after):
    rows, width = x.shape
    columns, units = dqkv.shape[2], slope.shape[1]
    piece = min(512, units)
    wide = min(512, width)
    parts = size // unit
    steps = units // piece + width // wide
    sends = units // piece + parts

    def body(*refs):
        flag_ref, g1, g2, x_hbm, g_hbm, slope_hbm, q_hbm, w3, wi_hbm, wo_hbm = refs[:10]
        dh_hbm, *dx_hbms, small_ref, bias_ref = refs[-15 - parts : -12]
        x_ref, g_ref, slope_ref, q_ref, wi, wo, one, two, normed_ref, dh_ref, dx_ref, sems = refs[-12:]
        mine = pl.ds(start, size)
        sources = (g_hbm.at[mine], slope_hbm.at[mine], x_hbm.at[mine], q_hbm.at[:, mine])
        inward = [
            pltpu.make_async_copy(a, b, sems.at[i])
            for i, (a, b) in enumerate(zip(sources, (g_ref, slope_ref, x_ref, q_ref)))
        ]
        for copy in inward[:2]:
            copy.start()
        pieces = []
        for low in range(0, units, piece):
            here = pl.ds(low, piece)
            pieces.append((wo_hbm.at[here], wo.at[here]))
        for low in range(0, width, wide):
            here = pl.ds(low, wide)
            pieces.append((wi_hbm.at[here], wi.at[here]))
        stream = Stream(pieces, sems.at[pl.ds(4, steps)])
        out = Out(sems.at[pl.ds(4 + steps, sends)])

        def slope_times(low, acc):
            here = slice(low, low + piece)
            grad = (acc * slope_ref[:, here].astype(F32)).astype(BF16)
            dh_ref[:, here] = grad
            bias_ref[:, here] = jnp.sum(grad.astype(F32), 0, keepdims=True)
            there = pl.ds(low, piece)
            out.send(dh_ref.at[:, there], dh_hbm.at[mine, there])

        inward[0].wait()
        before = None
        for low in range(0, units, piece):
            stream.next()
            if low == 0:
                for copy in inward[2:]:
                    copy.start()
                inward[1].wait()
            acc = dot(g_ref[...], wo[low : low + piece], NT)
            if before is not None:
                slope_times(low - piece, before)
            before = acc
        slope_times(units - piece, before)
        for copy in inward[2:]:
            copy.wait()
        band = 64
        rstds = []
        for low in range(0, size, band):
            here = slice(low, low + band)
            values = x_ref[here].astype(F32)
            center = values - jnp.mean(values, -1, keepdims=True)
            rstds.append(lax.rsqrt(jnp.mean(center * center, -1, keepdims=True) + EPS))
            normed_ref[here] = center * rstds[-1]
        for low in range(0, width, wide):
            here = slice(low, low + wide)
            acc = dot(q_ref[0], w3[0, here], NT)
            for c in (1, 2):
                acc = acc + dot(q_ref[c], w3[c, here], NT)
            one[:, here] = acc
        for low in range(0, width, wide):
            here = slice(low, low + wide)
            stream.next()
            two[:, here] = dot(dh_ref[...], wi[here], NT)
        gain_one, gain_two = g1[...], g2[...]
        own = flag_ref[1].astype(F32)
        sums = [jnp.zeros((1, width), F32)] * 4
        for at, low in enumerate(range(0, size, band)):
            here = slice(low, low + band)
            normed, d_one, d_two = normed_ref[here], one[here], two[here]
            grad = d_one * gain_one + d_two * gain_two
            dx_ref[here] = rstds[at] * (
                grad
                - jnp.mean(grad, -1, keepdims=True)
                - normed * jnp.mean(grad * normed, -1, keepdims=True)
            ) + own * g_ref[here].astype(F32)
            terms = (d_one * normed, d_one, d_two * normed, d_two)
            sums = [s + jnp.sum(t, 0, keepdims=True) for s, t in zip(sums, terms)]
            if (low + band) % unit == 0:
                i = low // unit
                out.send(dx_ref.at[pl.ds(i * unit, unit)], dx_hbms[i])
        small_ref[...] = jnp.concatenate(sums + [jnp.zeros((4, width), F32)], 0)
        out.finish()

    vec = lambda n: pl.BlockSpec((1, n), lambda i: (0, 0))
    operands = [flag, *map(in_hbm, (gains[0], gains[2], x, cotan, slope, dqkv)), in_vmem(w_three), in_hbm(w_in), in_hbm(w_out)]
    specs = [SMEM, vec(width), vec(width)] + [HBM] * 4 + [VMEM] + [HBM] * 2
    aliases = {}
    if held is not None:
        aliases = {len(operands): 0}
        operands.append(in_hbm(held))
        specs.append(HBM)
    operands += list(after)
    specs += [ANY] * len(after)
    return pl.pallas_call(
        body,
        grid=(1,),
        in_specs=specs,
        out_specs=[HBM] * (1 + parts) + [pl.BlockSpec((8, width), lambda i: (0, 0)), vec(units)],
        out_shape=[pltpu.HBM((rows, units), BF16)]
        + [pltpu.HBM((unit, width), F32)] * parts
        + [shape((8, width), F32), shape((1, units), F32)],
        scratch_shapes=[
            pltpu.VMEM((size, width), BF16),
            pltpu.VMEM((size, width), BF16),
            pltpu.VMEM((size, units), BF16),
            pltpu.VMEM((3, size, columns), BF16),
            pltpu.VMEM(w_in.shape, BF16),
            pltpu.VMEM(w_out.shape, BF16),
            pltpu.VMEM((size, width), F32),
            pltpu.VMEM((size, width), F32),
            pltpu.VMEM((size, width), F32),
            pltpu.VMEM((size, units), BF16),
            pltpu.VMEM((size, width), F32),
            pltpu.SemaphoreType.DMA((4 + steps + sends,)),
        ],
        input_output_aliases=aliases,
        compiler_params=params(38),
        cost_estimate=cost(2 * size * width * (2 * units + 3 * columns), 2 * width * (2 * units + 3 * columns) + 16 * size * width, start == 0),
        name="backward_rows",
    )(*operands)


def take_in(flag, unit, came, operand, out, out_at, out_rows, out_shape, after, last):
    rows, width = came.shape
    has_unit, has_total = unit is not None, operand is not None
    more = 0 if has_unit or not has_total else rows - out_rows

    def body(*refs):
        flag_ref, came_ref = refs[:2]
        results = list(refs[-has_unit - has_total - (more > 0) - 2 * has_total :])
        if has_unit:
            held_ref = results.pop(0)
        if has_total:
            out_ref = results.pop(0)
            rounded_ref, sem = results[-2:]
            part = slice(0, out_rows)
            mine_ref = refs[2 + has_unit]
            rounded_ref[...] = jnp.where(flag_ref[0] == 1, mine_ref[part], came_ref[part]).astype(BF16)
            copy = pltpu.make_async_copy(rounded_ref, out_ref.at[pl.ds(out_at * out_rows, out_rows)], sem)
            copy.start()
            if more:
                results[0][...] = jnp.where(flag_ref[0] == 1, mine_ref[out_rows:], came_ref[out_rows:])
        if has_unit:
            held_ref[...] = refs[2][...] + came_ref[...]
        if has_total:
            copy.wait()

    operands, specs = [flag, in_vmem(came)], [SMEM, VMEM]
    outs, out_specs, aliases, scratch = [], [], {}, []
    if has_unit:
        operands.append(unit)
        specs.append(VMEM)
        outs.append(pltpu.VMEM((rows, width), F32))
        out_specs.append(VMEM)
    if has_total:
        operands.append(in_vmem(operand))
        specs.append(VMEM)
        outs.append(pltpu.HBM(out_shape, BF16))
        out_specs.append(HBM)
        scratch = [pltpu.VMEM((out_rows, width), BF16), pltpu.SemaphoreType.DMA]
        if out is not None:
            aliases = {len(operands): len(outs) - 1}
            operands.append(in_hbm(out))
            specs.append(HBM)
        if more:
            outs.append(shape((more, width), F32))
            out_specs.append(VMEM)
    operands += after
    specs += [ANY] * len(after)
    result = list(
        pl.pallas_call(
            body,
            in_specs=specs,
            out_specs=out_specs,
            out_shape=outs,
            scratch_shapes=scratch,
            input_output_aliases=aliases,
            compiler_params=pltpu.CompilerParams(vmem_limit_bytes=SMALL_LIMIT),
            cost_estimate=(alone if last else light)(4 * rows * width, 16 * rows * width),
            name="take_in",
        )(*operands)
    )
    held = result.pop(0) if has_unit else None
    out = result.pop(0) if has_total else out
    return held, out, (result[0] if more else None)


def pass_on(flag, held, met, unit, after, carried, last):
    rows, width = (held if unit is None else unit).shape
    both = min(rows, held.shape[0])

    def body(flag_ref, held_ref, met_ref, *refs):
        out_ref = refs[-1 - len(carried)]
        total = held_ref[:both] + met_ref[:both]
        if unit is not None:
            total = jnp.where(flag_ref[0] == 1, total, refs[0][:both])
        out_ref[:both] = total
        if both < rows:
            out_ref[both:] = refs[0][both:]

    more = [] if unit is None else [unit]
    return pl.pallas_call(
        body,
        in_specs=[SMEM] + [VMEM] * (2 + len(more)) + [HBM] * len(carried) + [ANY] * len(after),
        out_specs=[VMEM] + [HBM] * len(carried),
        out_shape=[pltpu.VMEM((rows, width), F32)] + [pltpu.HBM(c.shape, c.dtype) for c in carried],
        input_output_aliases={3 + len(more) + i: 1 + i for i in range(len(carried))},
        compiler_params=pltpu.CompilerParams(vmem_limit_bytes=SMALL_LIMIT),
        cost_estimate=(alone if last else light)(2 * rows * width, 16 * rows * width),
        name="pass_on",
    )(flag, in_vmem(held), in_vmem(met), *more, *map(in_hbm, carried), *after)


def append_rows(top, bottom, after):
    rows, width = top.shape

    def body(top_ref, bottom_ref, *refs):
        refs[-1][:rows] = top_ref[...]
        refs[-1][rows:] = bottom_ref[...]

    return pl.pallas_call(
        body,
        in_specs=[VMEM] * 2 + [ANY] * len(after),
        out_specs=VMEM,
        out_shape=shape((rows + bottom.shape[0], width), F32),
        compiler_params=pltpu.CompilerParams(vmem_limit_bytes=SMALL_LIMIT),
        cost_estimate=light(0, 8 * rows * width),
        name="append_rows",
    )(top, bottom, *after)


def add_up(arrays, after, long=False):
    def body(*refs):
        total = refs[0][...]
        for ref in refs[1 : len(arrays)]:
            total = total + ref[...]
        refs[-1][...] = total

    return pl.pallas_call(
        body,
        in_specs=[VMEM] * len(arrays) + [ANY] * len(after),
        out_specs=VMEM,
        out_shape=shape(arrays[0].shape, F32),
        compiler_params=pltpu.CompilerParams(vmem_limit_bytes=SMALL_LIMIT),
        cost_estimate=light(1e11, 0) if long else light(0, 0),
        name="add_up",
    )(*arrays, *after)


def split_rows(array, at, after):
    rows, width = array.shape
    step = math.gcd(at, rows - at)
    first = at // step

    def body(in_ref, *refs):
        one_ref, two_ref = refs[-2:]
        i = pl.program_id(0)

        @pl.when(i < first)
        def _():
            one_ref[...] = in_ref[...]

        @pl.when(i >= first)
        def _():
            two_ref[...] = in_ref[...]

    block = (step, width)
    return pl.pallas_call(
        body,
        grid=(rows // step,),
        in_specs=[pl.BlockSpec(block, lambda i: (i, 0))] + [ANY] * len(after),
        out_specs=[
            pl.BlockSpec(block, lambda i: (jnp.minimum(i, first - 1), 0)),
            pl.BlockSpec(block, lambda i: (jnp.maximum(i - first, 0), 0)),
        ],
        out_shape=[pltpu.HBM((at, width), F32), pltpu.HBM((rows - at, width), F32)],
        compiler_params=pltpu.CompilerParams(vmem_limit_bytes=SMALL_LIMIT),
        cost_estimate=light(0, 8 * rows * width),
        name="split_rows",
    )(in_hbm(array), *after)


def rounded(array):
    def body(in_ref, out_ref):
        out_ref[...] = in_ref[...].astype(BF16)

    block = pl.BlockSpec((min(128, array.shape[0]), array.shape[1]), lambda i: (i, 0))
    return pl.pallas_call(
        body,
        grid=(array.shape[0] // block.block_shape[0],),
        in_specs=[block],
        out_specs=block,
        out_shape=shape(array.shape, BF16),
        name="rounded",
    )(array)


def whole_sum(unit, n):
    if n == 1:
        return unit
    if n % 2:
        return lax.psum(unit, "tensor")
    me, half = lax.axis_index("tensor"), n // 2
    held = unit
    for j in range(half - 1):
        held = unit + lax.ppermute(held, "tensor", [(j, j + 1), (n - 1 - j, n - 2 - j)])
    total = held + lax.ppermute(held, "tensor", [(half - 1, half), (half, half - 1)])
    for j in reversed(range(half - 1)):
        came = lax.ppermute(total, "tensor", [(j + 1, j), (n - 2 - j, n - 1 - j)])
        total = jnp.where((me == j) | (me == n - 1 - j), came, total)
    return total


class Line:
    LAG = 3

    def __init__(self, count, flag, finish):
        self.count, self.flag, self.finish = count, flag, finish
        self.units, self.operands, self.came, self.held, self.met = [], {}, {}, {}, {}
        self.step = 0

    def send(self, step, operand):
        pairs = [(0, 1), (3, 2)] * (step < self.count) + [(1, 0), (2, 3)] * (step >= self.LAG)
        self.operands[step] = operand
        self.came[step] = lax.ppermute(operand, "tensor", pairs)

    def pump(self, after, carried=()):
        step = self.step
        self.step += 1
        last = step >= self.count - 2
        unit = self.units[step] if step < self.count else None
        held = self.finish(self, step - self.LAG, unit, self.came[step], after, last)
        if unit is not None:
            self.held[step] = held
            self.met[step] = lax.ppermute(held, "tensor", [(1, 2), (2, 1)])
            after = [held]
        if step == 0:
            self.send(2, self.units[2])
        elif step <= self.count:
            ahead = step + 2
            unit = self.units[ahead] if ahead < self.count else None
            operand, *carried = pass_on(
                self.flag, self.held[step - 1], self.met[step - 1], unit, after, carried, last
            )
            self.send(ahead, operand)
            after = [operand]
        return after, *carried


class SmallSum:
    def __init__(self, values, axis, n):
        self.values, self.axis, self.n, self.apart, self.came = values, axis, n, 1, None

    def exchange(self):
        if self.n & (self.n - 1):
            self.values, self.apart = lax.psum(self.values, self.axis), self.n
        if self.apart >= self.n:
            return False
        self.came = lax.ppermute(self.values, self.axis, [(i, i ^ self.apart) for i in range(self.n)])
        self.apart *= 2
        return True

    def add(self, after, long=False):
        if self.came is not None:
            self.values, self.came = add_up([self.values, self.came], after, long), None
        return [self.values]


def rotary(span):
    half = ROT // 2
    inverse = 10000.0 ** (-(2.0 * np.arange(half)) / ROT)
    angle = np.arange(span)[:, None] * inverse[None, :]
    cosine, sine = np.cos(angle), np.sin(angle)
    ones, zeros = np.ones((span, 128 - ROT)), np.zeros((span, 128 - ROT))
    nil = np.zeros((span, half))
    tables = (
        np.concatenate([cosine, cosine, ones], 1),
        np.concatenate([-sine, nil, zeros], 1),
        np.concatenate([nil, sine, zeros], 1),
    )
    return [jnp.asarray(t, F32) for t in tables]


def make_local(dp, tp):
    def local(
        layer_input,
        lengths,
        ln1_gain,
        ln1_shift,
        w_qkv,
        b_qkv,
        w_dense,
        b_dense,
        ln2_gain,
        ln2_shift,
        w_in,
        b_in,
        w_out,
        b_out,
        grad_out,
    ):
        rows, width = layer_input.shape
        assert lengths.shape[0] == 1
        columns, units = w_dense.shape[0], w_in.shape[1]
        tables = rotary(rows)
        w_three = jnp.transpose(w_qkv, (1, 0, 2))
        vec = lambda v: v.reshape(1, -1)
        gains = (vec(ln1_gain), vec(ln1_shift), vec(ln2_gain), vec(ln2_shift))
        size, unit = 256, 128
        starts = list(range(0, rows, size))
        each = rows // unit
        me = lax.axis_index("tensor")
        flag = jnp.stack([(me == 1) | (me == 2), me == 0]).astype(jnp.int32)
        outs = [None, None]

        last = []

        def finish(line, done, unit, came, after, final):
            if done < 0:
                return take_in(flag, unit, came, None, None, 0, 0, None, after, final)[0]
            which, at = divmod(done, each)
            held, outs[which], more = take_in(
                flag, unit, came, line.operands[done + line.LAG], outs[which], at, rows // each, layer_input.shape, after,
                final,
            )
            last[:] = [more]
            return held

        straight = tp != 4
        line = None if straight else Line(2 * each, flag, finish)
        queue = [] if straight else line.units

        def pump(after, *carried):
            if straight or line.step == line.count + line.LAG:
                return (after, *carried)
            return line.pump(after, carried)

        def forward(start, size, held, after, carried=()):
            result = forward_rows(
                start, size, unit, layer_input, lengths, flag, gains, w_three, b_qkv, w_in, b_in, (b_dense, b_out),
                w_dense, w_out, tables, held, after, carried,
            )
            parts = size // unit
            queue.extend(result[6 : 6 + parts])
            return result[:6], [result[6 + parts]], result[7 + parts :]

        held, after, _ = forward(0, size, None, [])
        if not straight:
            line.send(0, queue[0])
        held, after, (queue[1],) = forward(size, size, held, [], [queue[1]])
        if not straight:
            line.send(1, queue[1])
        cotan, b_out_grad = mask_rows(lengths, grad_out, after)
        after = [b_out_grad]
        for start in starts[2:]:
            held, after, _ = forward(start, size, held, pump(after)[0])
        a_one, a_two, qkv, mixed, hidden, slope = held

        core = lax.rem(lax.axis_index("dp"), 2).astype(jnp.int32).reshape(1)
        blocks = dp // 2
        pairs = [(i, i ^ 1) for i in range(dp)]
        groups = [[2 * i + c for i in range(blocks)] for c in range(2)]

        def other_half(name, lefts, right, slide_left, after, long=False):
            half, token = pair_product(lefts, right, slide_left, 1 - core, None, blocks, after, name, long)
            return half, [token]

        def own_half(name, lefts, right, slide_left, came, after, long=False):
            half, token = pair_product(lefts, right, slide_left, core, came, blocks, after, name, long)
            return half, [token]

        def swap(half):
            return lax.ppermute(half, "dp", pairs)

        def over_chips(half):
            return lax.psum_scatter(half, "dp", scatter_dimension=0, axis_index_groups=groups, tiled=True)[0]

        out_parts = ([hidden, mixed], cotan[None], False)
        half, after = other_half("w_out_other", *out_parts, pump(after)[0])
        after, half = pump(after, half)
        came_out = swap(half)
        dqkv, b_qkv_grad = attend_back(lengths, qkv, cotan, w_dense, tables, after)
        out_half, after = own_half("w_out_own", *out_parts, came_out, pump([b_qkv_grad])[0])
        after, out_half = pump(after, out_half)
        out_grads = over_chips(out_half)

        dhpre, smalls, biases = None, [], []

        def backward(i, after):
            nonlocal dhpre
            dhpre, *dx, small, bias = backward_rows(
                starts[i], size, unit, layer_input, flag, cotan, slope, dqkv, w_three, w_in, w_out, gains, dhpre, after
            )
            queue.extend(dx)
            smalls.append(small)
            biases.append(bias)
            return [bias]

        after = backward(0, after)
        zero = jnp.zeros(1, jnp.int32)
        qkv_grads, token = pair_product([a_one], dqkv, True, zero, None, dp, pump(after)[0], "w_qkv_grad", apart=1)
        after, qkv_grads = pump([token], qkv_grads)
        qkv_grads = lax.psum_scatter(qkv_grads, "dp", scatter_dimension=0, tiled=True)[0]
        after = backward(1, after)
        after = backward(2, pump(after)[0])
        after = backward(3, pump(after)[0])

        flat = jnp.concatenate(
            [sum(smalls)[:4].reshape(-1), b_out_grad.reshape(-1), sum(biases).reshape(-1), b_qkv_grad.reshape(-1)]
        )
        small = SmallSum(flat.reshape(-1, 128), "dp", dp)
        small.exchange()
        in_parts = ([a_two], dhpre[None], True)
        half, after = other_half("w_in_other", *in_parts, pump(after)[0])
        after, half = pump(after, half)
        came_in = swap(half)
        after = small.add(after + [out_grads], True)
        while small.exchange():
            after = small.add(after)
        flat = small.values.reshape(-1)
        norms = jnp.concatenate([flat[: 4 * width].reshape(4, width), jnp.zeros((4, width), F32)])
        queue[-1] = append_rows(queue[-1], norms, after)
        in_half, after = own_half("w_in_own", *in_parts, came_in, pump([queue[-1]])[0])
        after, in_half = pump(after, in_half)
        in_grads = over_chips(in_half)
        w_out_grad, w_dense_grad = split_rows(out_grads[0], units, after + [qkv_grads])
        after = [w_dense_grad]
        while not straight and line.step < line.count + line.LAG:
            (after,) = pump(after)
        b_out_grad = flat[4 * width : 5 * width]
        b_in_grad = flat[5 * width : 5 * width + units]
        b_qkv_grad = flat[5 * width + units :].reshape(3, columns)
        w_qkv_grad = jnp.transpose(qkv_grads, (1, 0, 2))
        w_in_grad = in_grads[0]

        if straight:
            totals = [whole_sum(one, tp) for one in queue]
            last = [totals[-1][unit:]]
            totals[-1] = totals[-1][:unit]
            outs = [rounded(jnp.concatenate(totals[:each])), rounded(jnp.concatenate(totals[each:]))]
        gain_one, shift_one, gain_two, shift_two = (last[0][i] for i in range(4))
        layer_output, input_grad = outs
        return (
            layer_output,
            input_grad,
            gain_one,
            shift_one,
            w_qkv_grad,
            b_qkv_grad,
            w_dense_grad,
            b_out_grad,
            gain_two,
            shift_two,
            w_in_grad,
            b_in_grad,
            w_out_grad,
            b_out_grad,
        )

    return local


def solution(mesh):
    return jax.shard_map(
        make_local(mesh.shape["dp"], mesh.shape["tensor"]),
        mesh=mesh,
        in_specs=(
            P("dp", None),
            P("dp"),
            P(),
            P(),
            P(None, None, "tensor"),
            P(None, "tensor"),
            P("tensor", None),
            P(),
            P(),
            P(),
            P(None, "tensor"),
            P("tensor"),
            P("tensor", None),
            P(),
            P("dp", None),
        ),
        out_specs=(
            P("dp", None),
            P("dp", None),
            P(),
            P(),
            P("dp", None, "tensor"),
            P(None, "tensor"),
            P("tensor", "dp"),
            P(),
            P(),
            P(),
            P("dp", "tensor"),
            P("tensor"),
            P("tensor", "dp"),
            P(),
        ),
        check_vma=False,
    )
```

```python
import math

import jax
import jax.numpy as jnp
import numpy as np
from jax import lax
from jax.experimental import pallas as pl
from jax.experimental.pallas import tpu as pltpu
from jax.sharding import PartitionSpec as P

HD = 256
ROT = 64
EPS = 1e-05
F32 = jnp.float32
BF16 = jnp.bfloat16
SMALL_LIMIT = 8 * 1024 * 1024
NT = (((1,), (1,)), ((), ()))
TN = (((0,), (0,)), ((), ()))


def dot(a, b, dims=(((1,), (0,)), ((), ()))):
    return lax.dot_general(a, b, dims, preferred_element_type=F32)


def params(mebibytes):
    return pltpu.CompilerParams(vmem_limit_bytes=mebibytes * 1024 * 1024)


def cost(flops, nbytes, long=False):
    return pl.CostEstimate(flops=int(3e11 if long else 4e10), bytes_accessed=int(nbytes), transcendentals=0)


def alone(flops, nbytes):
    return pl.CostEstimate(flops=int(3e10), bytes_accessed=int(nbytes), transcendentals=0)


def light(flops, nbytes):
    return pl.CostEstimate(flops=int(flops), bytes_accessed=int(nbytes), transcendentals=0)


ANY = pl.BlockSpec(memory_space=pl.ANY)
HBM = pl.BlockSpec(memory_space=pltpu.HBM)
VMEM = pl.BlockSpec(memory_space=pltpu.VMEM)
SMEM = pl.BlockSpec(memory_space=pltpu.SMEM)


def shape(dims, dtype):
    return jax.ShapeDtypeStruct(dims, dtype)


TOKEN = shape((8, 128), F32)


def in_hbm(array):
    return pltpu.with_memory_space_constraint(array, pltpu.HBM)


def in_vmem(array):
    return pltpu.with_memory_space_constraint(array, pltpu.VMEM)


def turned(values, cosine, lower, upper):
    head = values[:, :128]
    head = (
        head * cosine
        + pltpu.roll(head, 128 - ROT // 2, 1) * lower
        + pltpu.roll(head, ROT // 2, 1) * upper
    )
    return jnp.concatenate([head, values[:, 128:]], 1)


class Stream:
    def __init__(self, pieces, sems, window=4):
        self.copies = [pltpu.make_async_copy(a, b, sems.at[i]) for i, (a, b) in enumerate(pieces)]
        self.window = window
        self.done = 0
        for copy in self.copies[:window]:
            copy.start()

    def next(self):
        self.copies[self.done].wait()
        ahead = self.done + self.window
        if ahead < len(self.copies):
            self.copies[ahead].start()
        self.done += 1


class Out:
    def __init__(self, sems):
        self.sems, self.copies = sems, []

    def send(self, source, target):
        copy = pltpu.make_async_copy(source, target, self.sems.at[len(self.copies)])
        copy.start()
        self.copies.append(copy)

    def finish(self):
        for copy in self.copies:
            copy.wait()


def forward_rows(start, size, unit, x, lengths, flag, gains, w_three, b_three, w_in, b_in, b_after, w_dense, w_out, tables, held, after, carried=()):
    rows, width = x.shape
    columns, units = w_dense.shape[0], w_in.shape[1]
    heads = columns // HD
    piece = min(512, units)
    wide = min(512, width)
    scale = 1.0 / math.sqrt(HD)
    past = start > 0
    band = min(256, size)
    bands = size // band
    parts = size // unit
    steps = 3 + units // piece + 1 + width // wide
    first = 4
    sends = 4 + 2 * (units // piece) + (band // unit) * (width // wide)
    vecs = 8 + len(b_after)

    def body(*refs):
        len_ref, flag_ref, g1, s1, g2, s2, b3_ref, bi_ref, *ba_refs = refs[:vecs]
        x_hbm, c_hbm, l_hbm, u_hbm, w3_hbm, wi_hbm, wd_hbm, wo_hbm = refs[vecs : vecs + 8]
        outs = refs[-24 - parts - len(carried) : -17]
        one_hbm, two_hbm, qkv_hbm, o_hbm, hidden_hbm, slope_hbm = outs[:6]
        part_hbms, token_ref = outs[6 : 6 + parts], outs[6 + parts]
        x_ref, c_ref, l_ref, u_ref, w3, wi, wd, wo, kv_ref = refs[-17:-8]
        one_ref, two_ref, qkv_ref, o_ref, hidden_ref, slope_ref, part_ref, sems = refs[-8:]
        token_ref[...] = jnp.zeros_like(token_ref)
        mine = pl.ds(start, size)
        heads_in = [
            pltpu.make_async_copy(a.at[mine], b, sems.at[i])
            for i, (a, b) in enumerate(((x_hbm, x_ref), (c_hbm, c_ref), (l_hbm, l_ref), (u_hbm, u_ref)))
        ]
        for copy in heads_in:
            copy.start()
        pieces = [(w3_hbm.at[c], w3.at[c]) for c in range(3)]
        for low in range(0, units, piece):
            here = pl.ds(low, piece)
            pieces.append((wi_hbm.at[:, here], wi.at[:, here]))
        pieces.append((wd_hbm, wd))
        for low in range(0, width, wide):
            here = pl.ds(low, wide)
            pieces.append((wo_hbm.at[:, here], wo.at[:, here]))
        stream = Stream(pieces, sems.at[pl.ds(first, steps)])
        if past:
            earlier = pltpu.make_async_copy(
                refs[vecs + 10].at[pl.ds(1, 2), pl.ds(0, start)],
                kv_ref.at[:, pl.ds(0, start)],
                sems.at[first + steps + bands * sends],
            )
            earlier.start()
        def block(index, row, local, mine, out):
            values = x_ref[local].astype(F32)
            center = values - jnp.mean(values, -1, keepdims=True)
            spread = jnp.mean(center * center, -1, keepdims=True)
            normed = center * lax.rsqrt(spread + EPS)
            one_ref[...] = (normed * g1[...] + s1[...]).astype(BF16)
            two_ref[...] = (normed * g2[...] + s2[...]).astype(BF16)
            out.send(one_ref, one_hbm.at[mine])
            out.send(two_ref, two_hbm.at[mine])
            if index == 0:
                for copy in heads_in[1:]:
                    copy.wait()

            def place(c, acc):
                for h in range(heads):
                    cols = slice(h * HD, (h + 1) * HD)
                    one_head = acc[:, cols] + b3_ref[c : c + 1, cols]
                    if c < 2:
                        one_head = turned(one_head, c_ref[local], l_ref[local], u_ref[local])
                    qkv_ref[c, :, cols] = one_head.astype(BF16)

            before = None
            for c in range(3):
                if index == 0:
                    stream.next()
                acc = dot(one_ref[...], w3[c])
                if before is not None:
                    place(c - 1, before)
                before = acc
            place(2, before)
            out.send(qkv_ref, qkv_hbm.at[:, mine])
            if index + 1 < bands:
                kv_ref[:, row : row + band] = qkv_ref[1:]

            here = lax.broadcasted_iota(jnp.int32, (band, band), 0)
            there = lax.broadcasted_iota(jnp.int32, (band, band), 1)
            seen = (there <= here) & (there + row < length)
            if row:
                inside = lax.broadcasted_iota(jnp.int32, (band, row), 1) < length
                if index == 0:
                    earlier.wait()
            for h in range(heads):
                cols = slice(h * HD, (h + 1) * HD)
                query = qkv_ref[0, :, cols]
                now = jnp.where(seen, dot(query, qkv_ref[1, :, cols], NT) * scale, -1e30)
                top = jnp.max(now, -1, keepdims=True)
                if row:
                    old = jnp.where(inside, dot(query, kv_ref[0, :row, cols], NT) * scale, -1e30)
                    top = jnp.maximum(top, jnp.max(old, -1, keepdims=True))
                    old = jnp.exp(old - top)
                now = jnp.exp(now - top)
                total = jnp.sum(now, -1, keepdims=True)
                if row:
                    total = total + jnp.sum(old, -1, keepdims=True)
                share = 1.0 / total
                mixed = dot((now * share).astype(BF16), qkv_ref[2, :, cols])
                if row:
                    mixed = mixed + dot((old * share).astype(BF16), kv_ref[1, :row, cols])
                o_ref[:, cols] = mixed.astype(BF16)
            out.send(o_ref, o_hbm.at[mine])

            def bend(low, acc):
                cols = slice(low, low + piece)
                pre = acc + bi_ref[:, cols]
                share = 0.5 + 0.5 * lax.erf(pre * (1.0 / math.sqrt(2.0)))
                hidden_ref[:, cols] = (pre * share).astype(BF16)
                bell = jnp.exp(-0.5 * pre * pre) * (1.0 / math.sqrt(2.0 * math.pi))
                slope_ref[:, cols] = (share + pre * bell).astype(BF16)
                there = pl.ds(low, piece)
                out.send(hidden_ref.at[:, there], hidden_hbm.at[mine, there])
                out.send(slope_ref.at[:, there], slope_hbm.at[mine, there])

            before = None
            for low in range(0, units, piece):
                if index == 0:
                    stream.next()
                acc = dot(two_ref[...], wi[:, low : low + piece])
                if before is not None:
                    bend(low - piece, before)
                before = acc
            bend(units - piece, before)

            if index == 0:
                stream.next()
            for low in range(0, width, wide):
                cols = slice(low, low + wide)
                if index == 0:
                    stream.next()
                acc = dot(o_ref[...], wd[:, cols]) + dot(hidden_ref[...], wo[:, cols])
                more = x_ref[local, cols].astype(F32)
                for ba_ref in ba_refs:
                    more = more + ba_ref[:, cols]
                part_ref[:, cols] = acc + own * more
                for i, part_hbm in enumerate(part_hbms[index * (band // unit) : (index + 1) * (band // unit)]):
                    there = pl.ds(low, wide)
                    out.send(part_ref.at[pl.ds(i * unit, unit), there], part_hbm.at[:, there])

        length = len_ref[0]
        own = flag_ref[1].astype(F32)
        heads_in[0].wait()
        for index in range(bands):
            row = start + index * band
            local = slice(index * band, (index + 1) * band)
            mine = pl.ds(row, band)
            out = Out(sems.at[pl.ds(first + steps + index * sends, sends)])
            block(index, row, local, mine, out)
            out.finish()

    flat = lambda v: v.reshape(1, -1)
    small = [*gains, b_three, flat(b_in), *map(flat, b_after)]
    operands = [lengths, flag, *map(in_hbm, small), *map(in_hbm, (x, *tables, w_three, w_in, w_dense, w_out))]
    specs = [SMEM, SMEM] + [pl.BlockSpec(v.shape, lambda i: (0, 0)) for v in small] + [HBM] * 8
    aliases = {}
    if past:
        aliases = {len(operands) + i: i for i in range(6)}
        operands += [in_hbm(array) for array in held]
        specs += [HBM] * 6
    for i, array in enumerate(carried):
        aliases[len(operands)] = 7 + parts + i
        operands.append(in_hbm(array))
        specs.append(HBM)
    operands += list(after)
    specs += [ANY] * len(after)
    flops = 2 * size * width * (4 * columns + 2 * units)
    whole = [(rows, width), (rows, width), (3, rows, columns), (rows, columns), (rows, units), (rows, units)]
    mine = [(band, width), (band, width), (3, band, columns), (band, columns), (band, units), (band, units)]
    return pl.pallas_call(
        body,
        grid=(1,),
        in_specs=specs,
        out_specs=[HBM] * (6 + parts) + [pl.BlockSpec(TOKEN.shape, lambda i: (0, 0))] + [HBM] * len(carried),
        out_shape=[pltpu.HBM(dims, BF16) for dims in whole] + [pltpu.HBM((unit, width), F32)] * parts + [TOKEN] + [pltpu.HBM(c.shape, c.dtype) for c in carried],
        scratch_shapes=[pltpu.VMEM((size, width), BF16)]
        + [pltpu.VMEM((size, 128), F32)] * 3
        + [pltpu.VMEM(w.shape, BF16) for w in (w_three, w_in, w_dense, w_out)]
        + [pltpu.VMEM((2, max(start + size - band, 16), columns), BF16)]
        + [pltpu.VMEM(dims, BF16) for dims in mine]
        + [pltpu.VMEM((band, width), F32), pltpu.SemaphoreType.DMA((first + steps + bands * sends + 1,))],
        input_output_aliases=aliases,
        compiler_params=params(46),
        cost_estimate=cost(flops, 2 * width * (4 * columns + 2 * units) + size * width * 20),
        name="forward_rows",
    )(*operands)


def mask_rows(lengths, grad_out, after):
    rows, width = grad_out.shape
    step = 256

    def body(*refs):
        len_ref, g_ref = refs[:2]
        out_ref, sum_ref = refs[-2:]
        i = pl.program_id(0)
        here = lax.broadcasted_iota(jnp.int32, (step, 1), 0) + i * step
        valid = (here < len_ref[0]).astype(F32)
        kept = g_ref[...].astype(F32) * valid
        out_ref[...] = kept.astype(BF16)

        @pl.when(i == 0)
        def _():
            sum_ref[...] = jnp.zeros_like(sum_ref)

        sum_ref[...] += jnp.sum(kept, 0, keepdims=True)

    row = pl.BlockSpec((step, width), lambda i: (i, 0))
    return pl.pallas_call(
        body,
        grid=(rows // step,),
        in_specs=[SMEM, row] + [ANY] * len(after),
        out_specs=[row, pl.BlockSpec((1, width), lambda i: (0, 0))],
        out_shape=[pltpu.HBM((rows, width), BF16), shape((1, width), F32)],
        compiler_params=params(24),
        cost_estimate=cost(2 * rows * width, 4 * rows * width),
        name="mask_rows",
    )(lengths, in_hbm(grad_out), *after)


def pair_product(lefts, right, slide_left, parity, added, blocks, after, name, long=False, apart=2):
    rows = right.shape[-2]
    many = right.shape[0]
    left_width = sum(left.shape[1] for left in lefts)
    block = (left_width if slide_left else right.shape[2]) // (apart * blocks)
    tall, wide = (block, right.shape[2]) if slide_left else (left_width, block)

    def body(_, *refs):
        right_ref = refs[len(lefts)]
        out_ref, token_ref = refs[-2:]
        token_ref[...] = jnp.zeros_like(token_ref)
        for c in range(many):
            low = 0
            for left_ref in refs[: len(lefts)]:
                here = slice(low, low + left_ref.shape[1])
                low += left_ref.shape[1]
                acc = dot(left_ref[...], right_ref[c], TN)
                if added is not None:
                    acc = acc + refs[len(lefts) + 1][0, c, here]
                out_ref[0, c, here] = acc

    out = pl.BlockSpec((1, many, tall, wide), lambda i, p: (i, 0, 0, 0))
    if slide_left:
        specs = [pl.BlockSpec((rows, block), lambda i, p: (0, apart * i + p[0]))]
        specs.append(pl.BlockSpec(right.shape, lambda i, p: (0, 0, 0)))
    else:
        specs = [pl.BlockSpec(left.shape, lambda i, p: (0, 0)) for left in lefts]
        specs.append(pl.BlockSpec((many, rows, block), lambda i, p: (0, 0, apart * i + p[0])))
    operands = [*lefts, right]
    if added is not None:
        operands.append(added)
        specs.append(out)
    return pl.pallas_call(
        body,
        grid_spec=pltpu.PrefetchScalarGridSpec(
            num_scalar_prefetch=1,
            grid=(blocks,),
            in_specs=specs + [ANY] * len(after),
            out_specs=[out, pl.BlockSpec(TOKEN.shape, lambda i, p: (0, 0))],
        ),
        out_shape=[pltpu.HBM((blocks, many, tall, wide), F32), TOKEN],
        compiler_params=params(30),
        cost_estimate=cost(2 * rows * blocks * many * tall * wide, 2 * rows * (left_width + many * right.shape[2]) + 4 * blocks * many * tall * wide, long),
        name=name,
    )(parity, *map(in_hbm, operands), *after)


def mixed_back(cotan, w_dense, after):
    rows, width = cotan.shape
    columns = w_dense.shape[0]
    step = min(256, rows)

    def body(g_ref, w_ref, *refs):
        refs[-1][...] = dot(g_ref[...], w_ref[...], NT).astype(BF16)

    return pl.pallas_call(
        body,
        grid=(rows // step,),
        in_specs=[pl.BlockSpec((step, width), lambda i: (i, 0)), pl.BlockSpec((columns, width), lambda i: (0, 0))]
        + [ANY] * len(after),
        out_specs=pl.BlockSpec((step, columns), lambda i: (i, 0)),
        out_shape=pltpu.HBM((rows, columns), BF16),
        compiler_params=params(16),
        cost_estimate=light(2 * rows * columns * width, 2 * rows * (width + columns)),
        name="mixed_back",
    )(in_hbm(cotan), in_hbm(w_dense), *after)


def attend_back(lengths, qkv, dmixed, tables, after):
    rows, columns = qkv.shape[1:]
    sub = min(256, rows)
    scale = 1.0 / math.sqrt(HD)

    def body(len_ref, q_ref, k_ref, v_ref, d_ref, c_ref, l_ref, u_ref, *refs):
        out_ref, bias_ref, dk_ref, dv_ref = refs[-4:]
        length = len_ref[0]
        for low in range(0, rows, sub):
            stop = low + sub
            here = slice(low, stop)
            query, keys, values = q_ref[0, here], k_ref[0, :stop], v_ref[0, :stop]
            scores = dot(query, keys, NT) * scale
            mine = lax.broadcasted_iota(jnp.int32, scores.shape, 0) + low
            there = lax.broadcasted_iota(jnp.int32, scores.shape, 1)
            scores = jnp.where((there <= mine) & (there < length), scores, -1e30)
            expo = jnp.exp(scores - jnp.max(scores, -1, keepdims=True))
            probs = expo * (1.0 / jnp.sum(expo, -1, keepdims=True))
            dprobs = dot(d_ref[here], values, NT)
            delta = jnp.sum(probs * dprobs, -1, keepdims=True)
            dscores = (probs * (dprobs - delta)).astype(BF16)
            out_ref[0, here] = turned(
                dot(dscores, keys) * scale, c_ref[here], -l_ref[here], -u_ref[here]
            ).astype(BF16)
            dkey = dot(dscores, query, TN) * scale
            dvalue = dot(probs.astype(BF16), d_ref[here], TN)
            if low:
                dk_ref[:low] += dkey[:low]
                dv_ref[:low] += dvalue[:low]
            dk_ref[here] = dkey[low:]
            dv_ref[here] = dvalue[low:]
        out_ref[1] = turned(dk_ref[...], c_ref[...], -l_ref[...], -u_ref[...]).astype(BF16)
        out_ref[2] = dv_ref[...].astype(BF16)
        for part in range(3):
            bias_ref[part] = jnp.sum(out_ref[part].astype(F32), 0, keepdims=True)

    part = lambda c: pl.BlockSpec((1, rows, HD), lambda h: (c, 0, h))
    table = pl.BlockSpec((rows, 128), lambda h: (0, 0))
    return pl.pallas_call(
        body,
        grid=(columns // HD,),
        in_specs=[
            SMEM,
            part(0),
            part(1),
            part(2),
            pl.BlockSpec((rows, HD), lambda h: (0, h)),
            table,
            table,
            table,
        ]
        + [ANY] * len(after),
        out_specs=[
            pl.BlockSpec((3, rows, HD), lambda h: (0, 0, h)),
            pl.BlockSpec((3, 1, HD), lambda h: (0, 0, h)),
        ],
        out_shape=[pltpu.HBM((3, rows, columns), BF16), shape((3, 1, columns), F32)],
        scratch_shapes=[pltpu.VMEM((rows, HD), F32)] * 2,
        compiler_params=params(36),
        cost_estimate=cost(
            10 * rows * rows * columns,
            14 * rows * columns,
            True,
        ),
        name="attend_back",
    )(lengths, *map(in_hbm, (qkv, qkv, qkv, dmixed, *tables)), *after)


def backward_rows(start, size, unit, x, flag, cotan, slope, dqkv, w_three, w_in, w_out, gains, held, after):
    rows, width = x.shape
    columns, units = dqkv.shape[2], slope.shape[1]
    piece = min(512, units)
    wide = min(512, width)
    parts = size // unit
    steps = units // piece + width // wide
    sends = units // piece + parts

    def body(*refs):
        flag_ref, g1, g2, x_hbm, g_hbm, slope_hbm, q_hbm, w3, wi_hbm, wo_hbm = refs[:10]
        dh_hbm, *dx_hbms, small_ref, bias_ref = refs[-15 - parts : -12]
        x_ref, g_ref, slope_ref, q_ref, wi, wo, one, two, normed_ref, dh_ref, dx_ref, sems = refs[-12:]
        mine = pl.ds(start, size)
        sources = (g_hbm.at[mine], slope_hbm.at[mine], x_hbm.at[mine], q_hbm.at[:, mine])
        inward = [
            pltpu.make_async_copy(a, b, sems.at[i])
            for i, (a, b) in enumerate(zip(sources, (g_ref, slope_ref, x_ref, q_ref)))
        ]
        for copy in inward[:2]:
            copy.start()
        pieces = []
        for low in range(0, units, piece):
            here = pl.ds(low, piece)
            pieces.append((wo_hbm.at[here], wo.at[here]))
        for low in range(0, width, wide):
            here = pl.ds(low, wide)
            pieces.append((wi_hbm.at[here], wi.at[here]))
        stream = Stream(pieces, sems.at[pl.ds(4, steps)])
        out = Out(sems.at[pl.ds(4 + steps, sends)])

        def slope_times(low, acc):
            here = slice(low, low + piece)
            grad = (acc * slope_ref[:, here].astype(F32)).astype(BF16)
            dh_ref[:, here] = grad
            bias_ref[:, here] = jnp.sum(grad.astype(F32), 0, keepdims=True)
            there = pl.ds(low, piece)
            out.send(dh_ref.at[:, there], dh_hbm.at[mine, there])

        inward[0].wait()
        before = None
        for low in range(0, units, piece):
            stream.next()
            if low == 0:
                for copy in inward[2:]:
                    copy.start()
                inward[1].wait()
            acc = dot(g_ref[...], wo[low : low + piece], NT)
            if before is not None:
                slope_times(low - piece, before)
            before = acc
        slope_times(units - piece, before)
        for copy in inward[2:]:
            copy.wait()
        band = 64
        rstds = []
        for low in range(0, size, band):
            here = slice(low, low + band)
            values = x_ref[here].astype(F32)
            center = values - jnp.mean(values, -1, keepdims=True)
            rstds.append(lax.rsqrt(jnp.mean(center * center, -1, keepdims=True) + EPS))
            normed_ref[here] = center * rstds[-1]
        for low in range(0, width, wide):
            here = slice(low, low + wide)
            acc = dot(q_ref[0], w3[0, here], NT)
            for c in (1, 2):
                acc = acc + dot(q_ref[c], w3[c, here], NT)
            one[:, here] = acc
        for low in range(0, width, wide):
            here = slice(low, low + wide)
            stream.next()
            two[:, here] = dot(dh_ref[...], wi[here], NT)
        gain_one, gain_two = g1[...], g2[...]
        own = flag_ref[1].astype(F32)
        sums = [jnp.zeros((1, width), F32)] * 4
        for at, low in enumerate(range(0, size, band)):
            here = slice(low, low + band)
            normed, d_one, d_two = normed_ref[here], one[here], two[here]
            grad = d_one * gain_one + d_two * gain_two
            dx_ref[here] = rstds[at] * (
                grad
                - jnp.mean(grad, -1, keepdims=True)
                - normed * jnp.mean(grad * normed, -1, keepdims=True)
            ) + own * g_ref[here].astype(F32)
            terms = (d_one * normed, d_one, d_two * normed, d_two)
            sums = [s + jnp.sum(t, 0, keepdims=True) for s, t in zip(sums, terms)]
            if (low + band) % unit == 0:
                i = low // unit
                out.send(dx_ref.at[pl.ds(i * unit, unit)], dx_hbms[i])
        small_ref[...] = jnp.concatenate(sums + [jnp.zeros((4, width), F32)], 0)
        out.finish()

    vec = lambda n: pl.BlockSpec((1, n), lambda i: (0, 0))
    operands = [flag, *map(in_hbm, (gains[0], gains[2], x, cotan, slope, dqkv)), in_vmem(w_three), in_hbm(w_in), in_hbm(w_out)]
    specs = [SMEM, vec(width), vec(width)] + [HBM] * 4 + [VMEM] + [HBM] * 2
    aliases = {}
    if held is not None:
        aliases = {len(operands): 0}
        operands.append(in_hbm(held))
        specs.append(HBM)
    operands += list(after)
    specs += [ANY] * len(after)
    return pl.pallas_call(
        body,
        grid=(1,),
        in_specs=specs,
        out_specs=[HBM] * (1 + parts) + [pl.BlockSpec((8, width), lambda i: (0, 0)), vec(units)],
        out_shape=[pltpu.HBM((rows, units), BF16)]
        + [pltpu.HBM((unit, width), F32)] * parts
        + [shape((8, width), F32), shape((1, units), F32)],
        scratch_shapes=[
            pltpu.VMEM((size, width), BF16),
            pltpu.VMEM((size, width), BF16),
            pltpu.VMEM((size, units), BF16),
            pltpu.VMEM((3, size, columns), BF16),
            pltpu.VMEM(w_in.shape, BF16),
            pltpu.VMEM(w_out.shape, BF16),
            pltpu.VMEM((size, width), F32),
            pltpu.VMEM((size, width), F32),
            pltpu.VMEM((size, width), F32),
            pltpu.VMEM((size, units), BF16),
            pltpu.VMEM((size, width), F32),
            pltpu.SemaphoreType.DMA((4 + steps + sends,)),
        ],
        input_output_aliases=aliases,
        compiler_params=params(38),
        cost_estimate=cost(2 * size * width * (2 * units + 3 * columns), 2 * width * (2 * units + 3 * columns) + 16 * size * width, start == 0),
        name="backward_rows",
    )(*operands)


def take_in(flag, unit, came, operand, out, out_at, out_rows, out_shape, after, last):
    rows, width = came.shape
    has_unit, has_total = unit is not None, operand is not None
    more = 0 if has_unit or not has_total else rows - out_rows

    def body(*refs):
        flag_ref, came_ref = refs[:2]
        results = list(refs[-has_unit - has_total - (more > 0) - 2 * has_total :])
        if has_unit:
            held_ref = results.pop(0)
        if has_total:
            out_ref = results.pop(0)
            rounded_ref, sem = results[-2:]
            part = slice(0, out_rows)
            mine_ref = refs[2 + has_unit]
            rounded_ref[...] = jnp.where(flag_ref[0] == 1, mine_ref[part], came_ref[part]).astype(BF16)
            copy = pltpu.make_async_copy(rounded_ref, out_ref.at[pl.ds(out_at * out_rows, out_rows)], sem)
            copy.start()
            if more:
                results[0][...] = jnp.where(flag_ref[0] == 1, mine_ref[out_rows:], came_ref[out_rows:])
        if has_unit:
            held_ref[...] = refs[2][...] + came_ref[...]
        if has_total:
            copy.wait()

    operands, specs = [flag, in_vmem(came)], [SMEM, VMEM]
    outs, out_specs, aliases, scratch = [], [], {}, []
    if has_unit:
        operands.append(unit)
        specs.append(VMEM)
        outs.append(pltpu.VMEM((rows, width), F32))
        out_specs.append(VMEM)
    if has_total:
        operands.append(in_vmem(operand))
        specs.append(VMEM)
        outs.append(pltpu.HBM(out_shape, BF16))
        out_specs.append(HBM)
        scratch = [pltpu.VMEM((out_rows, width), BF16), pltpu.SemaphoreType.DMA]
        if out is not None:
            aliases = {len(operands): len(outs) - 1}
            operands.append(in_hbm(out))
            specs.append(HBM)
        if more:
            outs.append(shape((more, width), F32))
            out_specs.append(VMEM)
    operands += after
    specs += [ANY] * len(after)
    result = list(
        pl.pallas_call(
            body,
            in_specs=specs,
            out_specs=out_specs,
            out_shape=outs,
            scratch_shapes=scratch,
            input_output_aliases=aliases,
            compiler_params=pltpu.CompilerParams(vmem_limit_bytes=SMALL_LIMIT),
            cost_estimate=(alone if last else light)(4 * rows * width, 16 * rows * width),
            name="take_in",
        )(*operands)
    )
    held = result.pop(0) if has_unit else None
    out = result.pop(0) if has_total else out
    return held, out, (result[0] if more else None)


def pass_on(flag, held, met, unit, after, carried, last, long):
    rows, width = (held if unit is None else unit).shape
    both = min(rows, held.shape[0])

    def body(flag_ref, held_ref, met_ref, *refs):
        out_ref = refs[-1 - len(carried)]
        total = held_ref[:both] + met_ref[:both]
        if unit is not None:
            total = jnp.where(flag_ref[0] == 1, total, refs[0][:both])
        out_ref[:both] = total
        if both < rows:
            out_ref[both:] = refs[0][both:]

    more = [] if unit is None else [unit]
    return pl.pallas_call(
        body,
        in_specs=[SMEM] + [VMEM] * (2 + len(more)) + [HBM] * len(carried) + [ANY] * len(after),
        out_specs=[VMEM] + [HBM] * len(carried),
        out_shape=[pltpu.VMEM((rows, width), F32)] + [pltpu.HBM(c.shape, c.dtype) for c in carried],
        input_output_aliases={3 + len(more) + i: 1 + i for i in range(len(carried))},
        compiler_params=pltpu.CompilerParams(vmem_limit_bytes=SMALL_LIMIT),
        cost_estimate=cost(0, 0, True) if long else (alone if last else light)(2 * rows * width, 16 * rows * width),
        name="pass_on",
    )(flag, in_vmem(held), in_vmem(met), *more, *map(in_hbm, carried), *after)


def append_rows(top, bottom, after):
    rows, width = top.shape

    def body(top_ref, bottom_ref, *refs):
        refs[-1][:rows] = top_ref[...]
        refs[-1][rows:] = bottom_ref[...]

    return pl.pallas_call(
        body,
        in_specs=[VMEM] * 2 + [ANY] * len(after),
        out_specs=VMEM,
        out_shape=shape((rows + bottom.shape[0], width), F32),
        compiler_params=pltpu.CompilerParams(vmem_limit_bytes=SMALL_LIMIT),
        cost_estimate=light(0, 8 * rows * width),
        name="append_rows",
    )(top, bottom, *after)


def add_up(arrays, after, long=False):
    def body(*refs):
        total = refs[0][...]
        for ref in refs[1 : len(arrays)]:
            total = total + ref[...]
        refs[-1][...] = total

    return pl.pallas_call(
        body,
        in_specs=[VMEM] * len(arrays) + [ANY] * len(after),
        out_specs=VMEM,
        out_shape=shape(arrays[0].shape, F32),
        compiler_params=pltpu.CompilerParams(vmem_limit_bytes=SMALL_LIMIT),
        cost_estimate=light(1e11, 0) if long else light(0, 0),
        name="add_up",
    )(*arrays, *after)


def split_rows(array, at, after):
    rows, width = array.shape
    step = math.gcd(at, rows - at)
    first = at // step

    def body(in_ref, *refs):
        one_ref, two_ref = refs[-2:]
        i = pl.program_id(0)

        @pl.when(i < first)
        def _():
            one_ref[...] = in_ref[...]

        @pl.when(i >= first)
        def _():
            two_ref[...] = in_ref[...]

    block = (step, width)
    return pl.pallas_call(
        body,
        grid=(rows // step,),
        in_specs=[pl.BlockSpec(block, lambda i: (i, 0))] + [ANY] * len(after),
        out_specs=[
            pl.BlockSpec(block, lambda i: (jnp.minimum(i, first - 1), 0)),
            pl.BlockSpec(block, lambda i: (jnp.maximum(i - first, 0), 0)),
        ],
        out_shape=[pltpu.HBM((at, width), F32), pltpu.HBM((rows - at, width), F32)],
        compiler_params=pltpu.CompilerParams(vmem_limit_bytes=SMALL_LIMIT),
        cost_estimate=light(0, 8 * rows * width),
        name="split_rows",
    )(in_hbm(array), *after)


def rounded(array):
    def body(in_ref, out_ref):
        out_ref[...] = in_ref[...].astype(BF16)

    block = pl.BlockSpec((min(128, array.shape[0]), array.shape[1]), lambda i: (i, 0))
    return pl.pallas_call(
        body,
        grid=(array.shape[0] // block.block_shape[0],),
        in_specs=[block],
        out_specs=block,
        out_shape=shape(array.shape, BF16),
        name="rounded",
    )(array)


def whole_sum(unit, n):
    if n == 1:
        return unit
    if n % 2:
        return lax.psum(unit, "tensor")
    me, half = lax.axis_index("tensor"), n // 2
    held = unit
    for j in range(half - 1):
        held = unit + lax.ppermute(held, "tensor", [(j, j + 1), (n - 1 - j, n - 2 - j)])
    total = held + lax.ppermute(held, "tensor", [(half - 1, half), (half, half - 1)])
    for j in reversed(range(half - 1)):
        came = lax.ppermute(total, "tensor", [(j + 1, j), (n - 2 - j, n - 1 - j)])
        total = jnp.where((me == j) | (me == n - 1 - j), came, total)
    return total


class Line:
    LAG = 3

    def __init__(self, count, flag, finish):
        self.count, self.flag, self.finish = count, flag, finish
        self.units, self.operands, self.came, self.held, self.met = [], {}, {}, {}, {}
        self.step = 0

    def send(self, step, operand):
        pairs = [(0, 1), (3, 2)] * (step < self.count) + [(1, 0), (2, 3)] * (step >= self.LAG)
        self.operands[step] = operand
        self.came[step] = lax.ppermute(operand, "tensor", pairs)

    def pump(self, after, carried=(), long=False):
        step = self.step
        self.step += 1
        last = step >= self.count - 2
        unit = self.units[step] if step < self.count else None
        held = self.finish(self, step - self.LAG, unit, self.came[step], after, last)
        if unit is not None:
            self.held[step] = held
            self.met[step] = lax.ppermute(held, "tensor", [(1, 2), (2, 1)])
            after = [held]
        if step == 0:
            self.send(2, self.units[2])
        elif step <= self.count:
            ahead = step + 2
            unit = self.units[ahead] if ahead < self.count else None
            operand, *carried = pass_on(
                self.flag, self.held[step - 1], self.met[step - 1], unit, after, carried, last, long
            )
            self.send(ahead, operand)
            after = [operand]
        return after, *carried


class SmallSum:
    def __init__(self, values, axis, n):
        self.values, self.axis, self.n, self.apart, self.came = values, axis, n, 1, None

    def exchange(self):
        if self.n & (self.n - 1):
            self.values, self.apart = lax.psum(self.values, self.axis), self.n
        if self.apart >= self.n:
            return False
        self.came = lax.ppermute(self.values, self.axis, [(i, i ^ self.apart) for i in range(self.n)])
        self.apart *= 2
        return True

    def add(self, after, long=False):
        if self.came is not None:
            self.values, self.came = add_up([self.values, self.came], after, long), None
        return [self.values]


def rotary(span):
    half = ROT // 2
    inverse = 10000.0 ** (-(2.0 * np.arange(half)) / ROT)
    angle = np.arange(span)[:, None] * inverse[None, :]
    cosine, sine = np.cos(angle), np.sin(angle)
    ones, zeros = np.ones((span, 128 - ROT)), np.zeros((span, 128 - ROT))
    nil = np.zeros((span, half))
    tables = (
        np.concatenate([cosine, cosine, ones], 1),
        np.concatenate([-sine, nil, zeros], 1),
        np.concatenate([nil, sine, zeros], 1),
    )
    return [jnp.asarray(t, F32) for t in tables]


def make_local(dp, tp):
    def local(
        layer_input,
        lengths,
        ln1_gain,
        ln1_shift,
        w_qkv,
        b_qkv,
        w_dense,
        b_dense,
        ln2_gain,
        ln2_shift,
        w_in,
        b_in,
        w_out,
        b_out,
        grad_out,
    ):
        rows, width = layer_input.shape
        assert lengths.shape[0] == 1
        columns, units = w_dense.shape[0], w_in.shape[1]
        tables = rotary(rows)
        w_three = jnp.transpose(w_qkv, (1, 0, 2))
        vec = lambda v: v.reshape(1, -1)
        gains = (vec(ln1_gain), vec(ln1_shift), vec(ln2_gain), vec(ln2_shift))
        size, unit = 256, 128
        starts = list(range(0, rows, size))
        each = rows // unit
        me = lax.axis_index("tensor")
        flag = jnp.stack([(me == 1) | (me == 2), me == 0]).astype(jnp.int32)
        outs = [None, None]

        last = []

        def finish(line, done, unit, came, after, final):
            if done < 0:
                return take_in(flag, unit, came, None, None, 0, 0, None, after, final)[0]
            which, at = divmod(done, each)
            held, outs[which], more = take_in(
                flag, unit, came, line.operands[done + line.LAG], outs[which], at, rows // each, layer_input.shape, after,
                final,
            )
            last[:] = [more]
            return held

        straight = tp != 4
        line = None if straight else Line(2 * each, flag, finish)
        queue = [] if straight else line.units

        def pump(after, *carried, long=False):
            if straight or line.step == line.count + line.LAG:
                return (after, *carried)
            return line.pump(after, carried, long)

        def forward(start, size, held, after, carried=()):
            result = forward_rows(
                start, size, unit, layer_input, lengths, flag, gains, w_three, b_qkv, w_in, b_in, (b_dense, b_out),
                w_dense, w_out, tables, held, after, carried,
            )
            parts = size // unit
            queue.extend(result[6 : 6 + parts])
            return result[:6], [result[6 + parts]], result[7 + parts :]

        held, after, _ = forward(0, size, None, [])
        if not straight:
            line.send(0, queue[0])
        held, after, (queue[1],) = forward(size, size, held, [], [queue[1]])
        if not straight:
            line.send(1, queue[1])
        cotan, b_out_grad = mask_rows(lengths, grad_out, after)
        after = [b_out_grad]
        for start in starts[2:]:
            held, after, _ = forward(start, size, held, pump(after)[0])
        a_one, a_two, qkv, mixed, hidden, slope = held

        core = lax.rem(lax.axis_index("dp"), 2).astype(jnp.int32).reshape(1)
        blocks = dp // 2
        pairs = [(i, i ^ 1) for i in range(dp)]
        groups = [[2 * i + c for i in range(blocks)] for c in range(2)]

        def other_half(name, lefts, right, slide_left, after, long=False):
            half, token = pair_product(lefts, right, slide_left, 1 - core, None, blocks, after, name, long)
            return half, [token]

        def own_half(name, lefts, right, slide_left, came, after, long=False):
            half, token = pair_product(lefts, right, slide_left, core, came, blocks, after, name, long)
            return half, [token]

        def swap(half):
            return lax.ppermute(half, "dp", pairs)

        def over_chips(half):
            return lax.psum_scatter(half, "dp", scatter_dimension=0, axis_index_groups=groups, tiled=True)[0]

        out_parts = ([hidden, mixed], cotan[None], False)
        half, after = other_half("w_out_other", *out_parts, pump(after)[0])
        dmixed = mixed_back(cotan, w_dense, after)
        after, half = pump([dmixed], half)
        came_out = swap(half)
        dqkv, b_qkv_grad = attend_back(lengths, qkv, dmixed, tables, after)
        out_half, after = own_half("w_out_own", *out_parts, came_out, pump([b_qkv_grad])[0])
        out_grads = over_chips(out_half)
        (after,) = pump(after, long=True)

        dhpre, smalls, biases = None, [], []

        def backward(i, after):
            nonlocal dhpre
            dhpre, *dx, small, bias = backward_rows(
                starts[i], size, unit, layer_input, flag, cotan, slope, dqkv, w_three, w_in, w_out, gains, dhpre, after
            )
            queue.extend(dx)
            smalls.append(small)
            biases.append(bias)
            return [bias]

        after = backward(0, after)
        zero = jnp.zeros(1, jnp.int32)
        qkv_grads, token = pair_product([a_one], dqkv, True, zero, None, dp, pump(after)[0], "w_qkv_grad", apart=1)
        after, qkv_grads = pump([token], qkv_grads)
        qkv_grads = lax.psum_scatter(qkv_grads, "dp", scatter_dimension=0, tiled=True)[0]
        after = backward(1, after)
        after = backward(2, pump(after)[0])
        after = backward(3, pump(after)[0])

        flat = jnp.concatenate(
            [sum(smalls)[:4].reshape(-1), b_out_grad.reshape(-1), sum(biases).reshape(-1), b_qkv_grad.reshape(-1)]
        )
        small = SmallSum(flat.reshape(-1, 128), "dp", dp)
        small.exchange()
        in_parts = ([a_two], dhpre[None], True)
        half, after = other_half("w_in_other", *in_parts, pump(after)[0])
        after, half = pump(after, half)
        came_in = swap(half)
        after = small.add(after + [out_grads], True)
        while small.exchange():
            after = small.add(after)
        flat = small.values.reshape(-1)
        norms = jnp.concatenate([flat[: 4 * width].reshape(4, width), jnp.zeros((4, width), F32)])
        queue[-1] = append_rows(queue[-1], norms, after)
        in_half, after = own_half("w_in_own", *in_parts, came_in, pump([queue[-1]])[0])
        after, in_half = pump(after, in_half)
        in_grads = over_chips(in_half)
        w_out_grad, w_dense_grad = split_rows(out_grads[0], units, after + [qkv_grads])
        after = [w_dense_grad]
        while not straight and line.step < line.count + line.LAG:
            (after,) = pump(after)
        b_out_grad = flat[4 * width : 5 * width]
        b_in_grad = flat[5 * width : 5 * width + units]
        b_qkv_grad = flat[5 * width + units :].reshape(3, columns)
        w_qkv_grad = jnp.transpose(qkv_grads, (1, 0, 2))
        w_in_grad = in_grads[0]

        if straight:
            totals = [whole_sum(one, tp) for one in queue]
            last = [totals[-1][unit:]]
            totals[-1] = totals[-1][:unit]
            outs = [rounded(jnp.concatenate(totals[:each])), rounded(jnp.concatenate(totals[each:]))]
        gain_one, shift_one, gain_two, shift_two = (last[0][i] for i in range(4))
        layer_output, input_grad = outs
        return (
            layer_output,
            input_grad,
            gain_one,
            shift_one,
            w_qkv_grad,
            b_qkv_grad,
            w_dense_grad,
            b_out_grad,
            gain_two,
            shift_two,
            w_in_grad,
            b_in_grad,
            w_out_grad,
            b_out_grad,
        )

    return local


def solution(mesh):
    return jax.shard_map(
        make_local(mesh.shape["dp"], mesh.shape["tensor"]),
        mesh=mesh,
        in_specs=(
            P("dp", None),
            P("dp"),
            P(),
            P(),
            P(None, None, "tensor"),
            P(None, "tensor"),
            P("tensor", None),
            P(),
            P(),
            P(),
            P(None, "tensor"),
            P("tensor"),
            P("tensor", None),
            P(),
            P("dp", None),
        ),
        out_specs=(
            P("dp", None),
            P("dp", None),
            P(),
            P(),
            P("dp", None, "tensor"),
            P(None, "tensor"),
            P("tensor", "dp"),
            P(),
            P(),
            P(),
            P("dp", "tensor"),
            P("tensor"),
            P("tensor", "dp"),
            P(),
        ),
        check_vma=False,
    )
```

```python
import math

import jax
import jax.numpy as jnp
import numpy as np
from jax import lax
from jax.experimental import pallas as pl
from jax.experimental.pallas import tpu as pltpu
from jax.sharding import PartitionSpec as P

HD = 256
ROT = 64
EPS = 1e-05
F32 = jnp.float32
BF16 = jnp.bfloat16
SMALL_LIMIT = 8 * 1024 * 1024
NT = (((1,), (1,)), ((), ()))
TN = (((0,), (0,)), ((), ()))


def dot(a, b, dims=(((1,), (0,)), ((), ()))):
    return lax.dot_general(a, b, dims, preferred_element_type=F32)


def params(mebibytes):
    return pltpu.CompilerParams(vmem_limit_bytes=mebibytes * 1024 * 1024)


def cost(flops, nbytes, long=False):
    return pl.CostEstimate(flops=int(3e11 if long else 4e10), bytes_accessed=int(nbytes), transcendentals=0)


def alone(flops, nbytes):
    return pl.CostEstimate(flops=int(3e10), bytes_accessed=int(nbytes), transcendentals=0)


def light(flops, nbytes):
    return pl.CostEstimate(flops=int(flops), bytes_accessed=int(nbytes), transcendentals=0)


ANY = pl.BlockSpec(memory_space=pl.ANY)
HBM = pl.BlockSpec(memory_space=pltpu.HBM)
VMEM = pl.BlockSpec(memory_space=pltpu.VMEM)
SMEM = pl.BlockSpec(memory_space=pltpu.SMEM)


def shape(dims, dtype):
    return jax.ShapeDtypeStruct(dims, dtype)


TOKEN = shape((8, 128), F32)


def in_hbm(array):
    return pltpu.with_memory_space_constraint(array, pltpu.HBM)


def in_vmem(array):
    return pltpu.with_memory_space_constraint(array, pltpu.VMEM)


def turned(values, cosine, lower, upper):
    head = values[:, :128]
    head = (
        head * cosine
        + pltpu.roll(head, 128 - ROT // 2, 1) * lower
        + pltpu.roll(head, ROT // 2, 1) * upper
    )
    return jnp.concatenate([head, values[:, 128:]], 1)


class Stream:
    def __init__(self, pieces, sems, window=4):
        self.copies = [pltpu.make_async_copy(a, b, sems.at[i]) for i, (a, b) in enumerate(pieces)]
        self.window = window
        self.done = 0
        for copy in self.copies[:window]:
            copy.start()

    def next(self):
        self.copies[self.done].wait()
        ahead = self.done + self.window
        if ahead < len(self.copies):
            self.copies[ahead].start()
        self.done += 1


class Out:
    def __init__(self, sems):
        self.sems, self.copies = sems, []

    def send(self, source, target):
        copy = pltpu.make_async_copy(source, target, self.sems.at[len(self.copies)])
        copy.start()
        self.copies.append(copy)

    def finish(self):
        for copy in self.copies:
            copy.wait()


def forward_rows(start, size, unit, x, lengths, flag, gains, w_three, b_three, w_in, b_in, b_after, w_dense, w_out, tables, held, after, carried=()):
    rows, width = x.shape
    columns, units = w_dense.shape[0], w_in.shape[1]
    heads = columns // HD
    piece = min(512, units)
    wide = min(512, width)
    scale = 1.0 / math.sqrt(HD)
    past = start > 0
    band = min(256, size)
    bands = size // band
    parts = size // unit
    steps = 3 + units // piece + 1 + width // wide
    first = 4
    sends = 4 + 2 * (units // piece) + (band // unit) * (width // wide)
    vecs = 8 + len(b_after)

    def body(*refs):
        len_ref, flag_ref, g1, s1, g2, s2, b3_ref, bi_ref, *ba_refs = refs[:vecs]
        x_hbm, c_hbm, l_hbm, u_hbm, w3_hbm, wi_hbm, wd_hbm, wo_hbm = refs[vecs : vecs + 8]
        outs = refs[-24 - parts - len(carried) : -17]
        one_hbm, two_hbm, qkv_hbm, o_hbm, hidden_hbm, slope_hbm = outs[:6]
        part_hbms, token_ref = outs[6 : 6 + parts], outs[6 + parts]
        x_ref, c_ref, l_ref, u_ref, w3, wi, wd, wo, kv_ref = refs[-17:-8]
        one_ref, two_ref, qkv_ref, o_ref, hidden_ref, slope_ref, part_ref, sems = refs[-8:]
        token_ref[...] = jnp.zeros_like(token_ref)
        mine = pl.ds(start, size)
        heads_in = [
            pltpu.make_async_copy(a.at[mine], b, sems.at[i])
            for i, (a, b) in enumerate(((x_hbm, x_ref), (c_hbm, c_ref), (l_hbm, l_ref), (u_hbm, u_ref)))
        ]
        for copy in heads_in:
            copy.start()
        pieces = [(w3_hbm.at[c], w3.at[c]) for c in range(3)]
        for low in range(0, units, piece):
            here = pl.ds(low, piece)
            pieces.append((wi_hbm.at[:, here], wi.at[:, here]))
        pieces.append((wd_hbm, wd))
        for low in range(0, width, wide):
            here = pl.ds(low, wide)
            pieces.append((wo_hbm.at[:, here], wo.at[:, here]))
        stream = Stream(pieces, sems.at[pl.ds(first, steps)])
        if past:
            earlier = pltpu.make_async_copy(
                refs[vecs + 10].at[pl.ds(1, 2), pl.ds(0, start)],
                kv_ref.at[:, pl.ds(0, start)],
                sems.at[first + steps + bands * sends],
            )
            earlier.start()
        def block(index, row, local, mine, out):
            values = x_ref[local].astype(F32)
            center = values - jnp.mean(values, -1, keepdims=True)
            spread = jnp.mean(center * center, -1, keepdims=True)
            normed = center * lax.rsqrt(spread + EPS)
            one_ref[...] = (normed * g1[...] + s1[...]).astype(BF16)
            two_ref[...] = (normed * g2[...] + s2[...]).astype(BF16)
            out.send(one_ref, one_hbm.at[mine])
            out.send(two_ref, two_hbm.at[mine])
            if index == 0:
                for copy in heads_in[1:]:
                    copy.wait()

            def place(c, acc):
                for h in range(heads):
                    cols = slice(h * HD, (h + 1) * HD)
                    one_head = acc[:, cols] + b3_ref[c : c + 1, cols]
                    if c < 2:
                        one_head = turned(one_head, c_ref[local], l_ref[local], u_ref[local])
                    qkv_ref[c, :, cols] = one_head.astype(BF16)

            before = None
            for c in range(3):
                if index == 0:
                    stream.next()
                acc = dot(one_ref[...], w3[c])
                if before is not None:
                    place(c - 1, before)
                before = acc
            place(2, before)
            out.send(qkv_ref, qkv_hbm.at[:, mine])
            if index + 1 < bands:
                kv_ref[:, row : row + band] = qkv_ref[1:]

            here = lax.broadcasted_iota(jnp.int32, (band, band), 0)
            there = lax.broadcasted_iota(jnp.int32, (band, band), 1)
            seen = (there <= here) & (there + row < length)
            if row:
                inside = lax.broadcasted_iota(jnp.int32, (band, row), 1) < length
                if index == 0:
                    earlier.wait()
            for h in range(heads):
                cols = slice(h * HD, (h + 1) * HD)
                query = qkv_ref[0, :, cols]
                now = jnp.where(seen, dot(query, qkv_ref[1, :, cols], NT) * scale, -1e30)
                top = jnp.max(now, -1, keepdims=True)
                if row:
                    old = jnp.where(inside, dot(query, kv_ref[0, :row, cols], NT) * scale, -1e30)
                    top = jnp.maximum(top, jnp.max(old, -1, keepdims=True))
                    old = jnp.exp(old - top)
                now = jnp.exp(now - top)
                total = jnp.sum(now, -1, keepdims=True)
                if row:
                    total = total + jnp.sum(old, -1, keepdims=True)
                share = 1.0 / total
                mixed = dot((now * share).astype(BF16), qkv_ref[2, :, cols])
                if row:
                    mixed = mixed + dot((old * share).astype(BF16), kv_ref[1, :row, cols])
                o_ref[:, cols] = mixed.astype(BF16)
            out.send(o_ref, o_hbm.at[mine])

            def bend(low, acc):
                cols = slice(low, low + piece)
                pre = acc + bi_ref[:, cols]
                share = 0.5 + 0.5 * lax.erf(pre * (1.0 / math.sqrt(2.0)))
                hidden_ref[:, cols] = (pre * share).astype(BF16)
                bell = jnp.exp(-0.5 * pre * pre) * (1.0 / math.sqrt(2.0 * math.pi))
                slope_ref[:, cols] = (share + pre * bell).astype(BF16)
                there = pl.ds(low, piece)
                out.send(hidden_ref.at[:, there], hidden_hbm.at[mine, there])
                out.send(slope_ref.at[:, there], slope_hbm.at[mine, there])

            before = None
            for low in range(0, units, piece):
                if index == 0:
                    stream.next()
                acc = dot(two_ref[...], wi[:, low : low + piece])
                if before is not None:
                    bend(low - piece, before)
                before = acc
            bend(units - piece, before)

            if index == 0:
                stream.next()
            for low in range(0, width, wide):
                cols = slice(low, low + wide)
                if index == 0:
                    stream.next()
                acc = dot(o_ref[...], wd[:, cols]) + dot(hidden_ref[...], wo[:, cols])
                more = x_ref[local, cols].astype(F32)
                for ba_ref in ba_refs:
                    more = more + ba_ref[:, cols]
                part_ref[:, cols] = acc + own * more
                for i, part_hbm in enumerate(part_hbms[index * (band // unit) : (index + 1) * (band // unit)]):
                    there = pl.ds(low, wide)
                    out.send(part_ref.at[pl.ds(i * unit, unit), there], part_hbm.at[:, there])

        length = len_ref[0]
        own = flag_ref[1].astype(F32)
        heads_in[0].wait()
        for index in range(bands):
            row = start + index * band
            local = slice(index * band, (index + 1) * band)
            mine = pl.ds(row, band)
            out = Out(sems.at[pl.ds(first + steps + index * sends, sends)])
            block(index, row, local, mine, out)
            out.finish()

    flat = lambda v: v.reshape(1, -1)
    small = [*gains, b_three, flat(b_in), *map(flat, b_after)]
    operands = [lengths, flag, *map(in_hbm, small), *map(in_hbm, (x, *tables, w_three, w_in, w_dense, w_out))]
    specs = [SMEM, SMEM] + [pl.BlockSpec(v.shape, lambda i: (0, 0)) for v in small] + [HBM] * 8
    aliases = {}
    if past:
        aliases = {len(operands) + i: i for i in range(6)}
        operands += [in_hbm(array) for array in held]
        specs += [HBM] * 6
    for i, array in enumerate(carried):
        aliases[len(operands)] = 7 + parts + i
        operands.append(in_hbm(array))
        specs.append(HBM)
    operands += list(after)
    specs += [ANY] * len(after)
    flops = 2 * size * width * (4 * columns + 2 * units)
    whole = [(rows, width), (rows, width), (3, rows, columns), (rows, columns), (rows, units), (rows, units)]
    mine = [(band, width), (band, width), (3, band, columns), (band, columns), (band, units), (band, units)]
    return pl.pallas_call(
        body,
        grid=(1,),
        in_specs=specs,
        out_specs=[HBM] * (6 + parts) + [pl.BlockSpec(TOKEN.shape, lambda i: (0, 0))] + [HBM] * len(carried),
        out_shape=[pltpu.HBM(dims, BF16) for dims in whole] + [pltpu.HBM((unit, width), F32)] * parts + [TOKEN] + [pltpu.HBM(c.shape, c.dtype) for c in carried],
        scratch_shapes=[pltpu.VMEM((size, width), BF16)]
        + [pltpu.VMEM((size, 128), F32)] * 3
        + [pltpu.VMEM(w.shape, BF16) for w in (w_three, w_in, w_dense, w_out)]
        + [pltpu.VMEM((2, max(start + size - band, 16), columns), BF16)]
        + [pltpu.VMEM(dims, BF16) for dims in mine]
        + [pltpu.VMEM((band, width), F32), pltpu.SemaphoreType.DMA((first + steps + bands * sends + 1,))],
        input_output_aliases=aliases,
        compiler_params=params(46),
        cost_estimate=cost(flops, 2 * width * (4 * columns + 2 * units) + size * width * 20),
        name="forward_rows",
    )(*operands)


def mask_rows(lengths, grad_out, after):
    rows, width = grad_out.shape
    step = 256

    def body(*refs):
        len_ref, g_ref = refs[:2]
        out_ref, sum_ref = refs[-2:]
        i = pl.program_id(0)
        here = lax.broadcasted_iota(jnp.int32, (step, 1), 0) + i * step
        valid = (here < len_ref[0]).astype(F32)
        kept = g_ref[...].astype(F32) * valid
        out_ref[...] = kept.astype(BF16)

        @pl.when(i == 0)
        def _():
            sum_ref[...] = jnp.zeros_like(sum_ref)

        sum_ref[...] += jnp.sum(kept, 0, keepdims=True)

    row = pl.BlockSpec((step, width), lambda i: (i, 0))
    return pl.pallas_call(
        body,
        grid=(rows // step,),
        in_specs=[SMEM, row] + [ANY] * len(after),
        out_specs=[row, pl.BlockSpec((1, width), lambda i: (0, 0))],
        out_shape=[pltpu.HBM((rows, width), BF16), shape((1, width), F32)],
        compiler_params=params(24),
        cost_estimate=cost(2 * rows * width, 4 * rows * width),
        name="mask_rows",
    )(lengths, in_hbm(grad_out), *after)


def pair_product(lefts, right, slide_left, parity, added, blocks, after, name, long=False, apart=2):
    rows = right.shape[-2]
    many = right.shape[0]
    left_width = sum(left.shape[1] for left in lefts)
    block = (left_width if slide_left else right.shape[2]) // (apart * blocks)
    tall, wide = (block, right.shape[2]) if slide_left else (left_width, block)

    def body(_, *refs):
        right_ref = refs[len(lefts)]
        out_ref, token_ref = refs[-2:]
        token_ref[...] = jnp.zeros_like(token_ref)
        for c in range(many):
            low = 0
            for left_ref in refs[: len(lefts)]:
                here = slice(low, low + left_ref.shape[1])
                low += left_ref.shape[1]
                acc = dot(left_ref[...], right_ref[c], TN)
                if added is not None:
                    acc = acc + refs[len(lefts) + 1][0, c, here]
                out_ref[0, c, here] = acc

    out = pl.BlockSpec((1, many, tall, wide), lambda i, p: (i, 0, 0, 0))
    if slide_left:
        specs = [pl.BlockSpec((rows, block), lambda i, p: (0, apart * i + p[0]))]
        specs.append(pl.BlockSpec(right.shape, lambda i, p: (0, 0, 0)))
    else:
        specs = [pl.BlockSpec(left.shape, lambda i, p: (0, 0)) for left in lefts]
        specs.append(pl.BlockSpec((many, rows, block), lambda i, p: (0, 0, apart * i + p[0])))
    operands = [*lefts, right]
    if added is not None:
        operands.append(added)
        specs.append(out)
    return pl.pallas_call(
        body,
        grid_spec=pltpu.PrefetchScalarGridSpec(
            num_scalar_prefetch=1,
            grid=(blocks,),
            in_specs=specs + [ANY] * len(after),
            out_specs=[out, pl.BlockSpec(TOKEN.shape, lambda i, p: (0, 0))],
        ),
        out_shape=[pltpu.HBM((blocks, many, tall, wide), F32), TOKEN],
        compiler_params=params(30),
        cost_estimate=cost(2 * rows * blocks * many * tall * wide, 2 * rows * (left_width + many * right.shape[2]) + 4 * blocks * many * tall * wide, long),
        name=name,
    )(parity, *map(in_hbm, operands), *after)


def mixed_back(cotan, w_dense, after):
    rows, width = cotan.shape
    columns = w_dense.shape[0]
    step = min(256, rows)

    def body(g_ref, w_ref, *refs):
        refs[-1][...] = dot(g_ref[...], w_ref[...], NT).astype(BF16)

    return pl.pallas_call(
        body,
        grid=(rows // step,),
        in_specs=[pl.BlockSpec((step, width), lambda i: (i, 0)), pl.BlockSpec((columns, width), lambda i: (0, 0))]
        + [ANY] * len(after),
        out_specs=pl.BlockSpec((step, columns), lambda i: (i, 0)),
        out_shape=pltpu.HBM((rows, columns), BF16),
        compiler_params=params(16),
        cost_estimate=light(2 * rows * columns * width, 2 * rows * (width + columns)),
        name="mixed_back",
    )(in_hbm(cotan), in_hbm(w_dense), *after)


def attend_back(lengths, qkv, dmixed, tables, after):
    rows, columns = qkv.shape[1:]
    sub = min(256, rows)
    scale = 1.0 / math.sqrt(HD)

    def body(len_ref, q_ref, k_ref, v_ref, d_ref, c_ref, l_ref, u_ref, *refs):
        out_ref, bias_ref, dk_ref, dv_ref = refs[-4:]
        length = len_ref[0]
        for low in range(0, rows, sub):
            stop = low + sub
            here = slice(low, stop)
            query, keys, values = q_ref[0, here], k_ref[0, :stop], v_ref[0, :stop]
            scores = dot(query, keys, NT) * scale
            mine = lax.broadcasted_iota(jnp.int32, scores.shape, 0) + low
            there = lax.broadcasted_iota(jnp.int32, scores.shape, 1)
            scores = jnp.where((there <= mine) & (there < length), scores, -1e30)
            expo = jnp.exp(scores - jnp.max(scores, -1, keepdims=True))
            probs = expo * (1.0 / jnp.sum(expo, -1, keepdims=True))
            dprobs = dot(d_ref[here], values, NT)
            delta = jnp.sum(probs * dprobs, -1, keepdims=True)
            dscores = (probs * (dprobs - delta)).astype(BF16)
            out_ref[0, here] = turned(
                dot(dscores, keys) * scale, c_ref[here], -l_ref[here], -u_ref[here]
            ).astype(BF16)
            dkey = dot(dscores, query, TN) * scale
            dvalue = dot(probs.astype(BF16), d_ref[here], TN)
            if low:
                dk_ref[:low] += dkey[:low]
                dv_ref[:low] += dvalue[:low]
            dk_ref[here] = dkey[low:]
            dv_ref[here] = dvalue[low:]
        out_ref[1] = turned(dk_ref[...], c_ref[...], -l_ref[...], -u_ref[...]).astype(BF16)
        out_ref[2] = dv_ref[...].astype(BF16)
        for part in range(3):
            bias_ref[part] = jnp.sum(out_ref[part].astype(F32), 0, keepdims=True)

    part = lambda c: pl.BlockSpec((1, rows, HD), lambda h: (c, 0, h))
    table = pl.BlockSpec((rows, 128), lambda h: (0, 0))
    return pl.pallas_call(
        body,
        grid=(columns // HD,),
        in_specs=[
            SMEM,
            part(0),
            part(1),
            part(2),
            pl.BlockSpec((rows, HD), lambda h: (0, h)),
            table,
            table,
            table,
        ]
        + [ANY] * len(after),
        out_specs=[
            pl.BlockSpec((3, rows, HD), lambda h: (0, 0, h)),
            pl.BlockSpec((3, 1, HD), lambda h: (0, 0, h)),
        ],
        out_shape=[pltpu.HBM((3, rows, columns), BF16), shape((3, 1, columns), F32)],
        scratch_shapes=[pltpu.VMEM((rows, HD), F32)] * 2,
        compiler_params=params(36),
        cost_estimate=cost(
            10 * rows * rows * columns,
            14 * rows * columns,
            True,
        ),
        name="attend_back",
    )(lengths, *map(in_hbm, (qkv, qkv, qkv, dmixed, *tables)), *after)


def backward_rows(start, size, unit, x, flag, cotan, slope, dqkv, w_three, w_in, w_out, gains, held, after):
    rows, width = x.shape
    columns, units = dqkv.shape[2], slope.shape[1]
    piece = min(512, units)
    wide = min(512, width)
    parts = size // unit
    steps = units // piece + width // wide
    sends = units // piece + parts

    def body(*refs):
        flag_ref, g1, g2, x_hbm, g_hbm, slope_hbm, q_hbm, w3, wi_hbm, wo_hbm = refs[:10]
        dh_hbm, *dx_hbms, small_ref, bias_ref = refs[-15 - parts : -12]
        x_ref, g_ref, slope_ref, q_ref, wi, wo, one, two, normed_ref, dh_ref, dx_ref, sems = refs[-12:]
        mine = pl.ds(start, size)
        sources = (g_hbm.at[mine], slope_hbm.at[mine], x_hbm.at[mine], q_hbm.at[:, mine])
        inward = [
            pltpu.make_async_copy(a, b, sems.at[i])
            for i, (a, b) in enumerate(zip(sources, (g_ref, slope_ref, x_ref, q_ref)))
        ]
        for copy in inward[:2]:
            copy.start()
        pieces = []
        for low in range(0, units, piece):
            here = pl.ds(low, piece)
            pieces.append((wo_hbm.at[here], wo.at[here]))
        for low in range(0, width, wide):
            here = pl.ds(low, wide)
            pieces.append((wi_hbm.at[here], wi.at[here]))
        stream = Stream(pieces, sems.at[pl.ds(4, steps)])
        out = Out(sems.at[pl.ds(4 + steps, sends)])

        def slope_times(low, acc):
            here = slice(low, low + piece)
            grad = (acc * slope_ref[:, here].astype(F32)).astype(BF16)
            dh_ref[:, here] = grad
            bias_ref[:, here] = jnp.sum(grad.astype(F32), 0, keepdims=True)
            there = pl.ds(low, piece)
            out.send(dh_ref.at[:, there], dh_hbm.at[mine, there])

        inward[0].wait()
        before = None
        for low in range(0, units, piece):
            stream.next()
            if low == 0:
                for copy in inward[2:]:
                    copy.start()
                inward[1].wait()
            acc = dot(g_ref[...], wo[low : low + piece], NT)
            if before is not None:
                slope_times(low - piece, before)
            before = acc
        slope_times(units - piece, before)
        for copy in inward[2:]:
            copy.wait()
        band = 64
        rstds = []
        for low in range(0, size, band):
            here = slice(low, low + band)
            values = x_ref[here].astype(F32)
            center = values - jnp.mean(values, -1, keepdims=True)
            rstds.append(lax.rsqrt(jnp.mean(center * center, -1, keepdims=True) + EPS))
            normed_ref[here] = center * rstds[-1]
        for low in range(0, width, wide):
            here = slice(low, low + wide)
            acc = dot(q_ref[0], w3[0, here], NT)
            for c in (1, 2):
                acc = acc + dot(q_ref[c], w3[c, here], NT)
            one[:, here] = acc
        for low in range(0, width, wide):
            here = slice(low, low + wide)
            stream.next()
            two[:, here] = dot(dh_ref[...], wi[here], NT)
        gain_one, gain_two = g1[...], g2[...]
        own = flag_ref[1].astype(F32)
        sums = [jnp.zeros((1, width), F32)] * 4
        for at, low in enumerate(range(0, size, band)):
            here = slice(low, low + band)
            normed, d_one, d_two = normed_ref[here], one[here], two[here]
            grad = d_one * gain_one + d_two * gain_two
            dx_ref[here] = rstds[at] * (
                grad
                - jnp.mean(grad, -1, keepdims=True)
                - normed * jnp.mean(grad * normed, -1, keepdims=True)
            ) + own * g_ref[here].astype(F32)
            terms = (d_one * normed, d_one, d_two * normed, d_two)
            sums = [s + jnp.sum(t, 0, keepdims=True) for s, t in zip(sums, terms)]
            if (low + band) % unit == 0:
                i = low // unit
                out.send(dx_ref.at[pl.ds(i * unit, unit)], dx_hbms[i])
        small_ref[...] = jnp.concatenate(sums + [jnp.zeros((4, width), F32)], 0)
        out.finish()

    vec = lambda n: pl.BlockSpec((1, n), lambda i: (0, 0))
    operands = [flag, *map(in_hbm, (gains[0], gains[2], x, cotan, slope, dqkv)), in_vmem(w_three), in_hbm(w_in), in_hbm(w_out)]
    specs = [SMEM, vec(width), vec(width)] + [HBM] * 4 + [VMEM] + [HBM] * 2
    aliases = {}
    if held is not None:
        aliases = {len(operands): 0}
        operands.append(in_hbm(held))
        specs.append(HBM)
    operands += list(after)
    specs += [ANY] * len(after)
    return pl.pallas_call(
        body,
        grid=(1,),
        in_specs=specs,
        out_specs=[HBM] * (1 + parts) + [pl.BlockSpec((8, width), lambda i: (0, 0)), vec(units)],
        out_shape=[pltpu.HBM((rows, units), BF16)]
        + [pltpu.HBM((unit, width), F32)] * parts
        + [shape((8, width), F32), shape((1, units), F32)],
        scratch_shapes=[
            pltpu.VMEM((size, width), BF16),
            pltpu.VMEM((size, width), BF16),
            pltpu.VMEM((size, units), BF16),
            pltpu.VMEM((3, size, columns), BF16),
            pltpu.VMEM(w_in.shape, BF16),
            pltpu.VMEM(w_out.shape, BF16),
            pltpu.VMEM((size, width), F32),
            pltpu.VMEM((size, width), F32),
            pltpu.VMEM((size, width), F32),
            pltpu.VMEM((size, units), BF16),
            pltpu.VMEM((size, width), F32),
            pltpu.SemaphoreType.DMA((4 + steps + sends,)),
        ],
        input_output_aliases=aliases,
        compiler_params=params(38),
        cost_estimate=cost(2 * size * width * (2 * units + 3 * columns), 2 * width * (2 * units + 3 * columns) + 16 * size * width, start == 0),
        name="backward_rows",
    )(*operands)


def take_in(flag, unit, came, operand, out, out_at, out_rows, out_shape, after, last):
    rows, width = came.shape
    has_unit, has_total = unit is not None, operand is not None
    more = 0 if has_unit or not has_total else rows - out_rows

    def body(*refs):
        flag_ref, came_ref = refs[:2]
        results = list(refs[-has_unit - has_total - (more > 0) - 2 * has_total :])
        if has_unit:
            held_ref = results.pop(0)
        if has_total:
            out_ref = results.pop(0)
            rounded_ref, sem = results[-2:]
            part = slice(0, out_rows)
            mine_ref = refs[2 + has_unit]
            rounded_ref[...] = jnp.where(flag_ref[0] == 1, mine_ref[part], came_ref[part]).astype(BF16)
            copy = pltpu.make_async_copy(rounded_ref, out_ref.at[pl.ds(out_at * out_rows, out_rows)], sem)
            copy.start()
            if more:
                results[0][...] = jnp.where(flag_ref[0] == 1, mine_ref[out_rows:], came_ref[out_rows:])
        if has_unit:
            held_ref[...] = refs[2][...] + came_ref[...]
        if has_total:
            copy.wait()

    operands, specs = [flag, in_vmem(came)], [SMEM, VMEM]
    outs, out_specs, aliases, scratch = [], [], {}, []
    if has_unit:
        operands.append(unit)
        specs.append(VMEM)
        outs.append(pltpu.VMEM((rows, width), F32))
        out_specs.append(VMEM)
    if has_total:
        operands.append(in_vmem(operand))
        specs.append(VMEM)
        outs.append(pltpu.HBM(out_shape, BF16))
        out_specs.append(HBM)
        scratch = [pltpu.VMEM((out_rows, width), BF16), pltpu.SemaphoreType.DMA]
        if out is not None:
            aliases = {len(operands): len(outs) - 1}
            operands.append(in_hbm(out))
            specs.append(HBM)
        if more:
            outs.append(shape((more, width), F32))
            out_specs.append(VMEM)
    operands += after
    specs += [ANY] * len(after)
    result = list(
        pl.pallas_call(
            body,
            in_specs=specs,
            out_specs=out_specs,
            out_shape=outs,
            scratch_shapes=scratch,
            input_output_aliases=aliases,
            compiler_params=pltpu.CompilerParams(vmem_limit_bytes=SMALL_LIMIT),
            cost_estimate=(alone if last else light)(4 * rows * width, 16 * rows * width),
            name="take_in",
        )(*operands)
    )
    held = result.pop(0) if has_unit else None
    out = result.pop(0) if has_total else out
    return held, out, (result[0] if more else None)


def pass_on(flag, held, met, unit, after, carried, last, long):
    rows, width = (held if unit is None else unit).shape
    both = min(rows, held.shape[0])

    def body(flag_ref, held_ref, met_ref, *refs):
        out_ref = refs[-1 - len(carried)]
        total = held_ref[:both] + met_ref[:both]
        if unit is not None:
            total = jnp.where(flag_ref[0] == 1, total, refs[0][:both])
        out_ref[:both] = total
        if both < rows:
            out_ref[both:] = refs[0][both:]

    more = [] if unit is None else [unit]
    return pl.pallas_call(
        body,
        in_specs=[SMEM] + [VMEM] * (2 + len(more)) + [HBM] * len(carried) + [ANY] * len(after),
        out_specs=[VMEM] + [HBM] * len(carried),
        out_shape=[pltpu.VMEM((rows, width), F32)] + [pltpu.HBM(c.shape, c.dtype) for c in carried],
        input_output_aliases={3 + len(more) + i: 1 + i for i in range(len(carried))},
        compiler_params=pltpu.CompilerParams(vmem_limit_bytes=SMALL_LIMIT),
        cost_estimate=cost(0, 0, True) if long else (alone if last else light)(2 * rows * width, 16 * rows * width),
        name="pass_on",
    )(flag, in_vmem(held), in_vmem(met), *more, *map(in_hbm, carried), *after)


def append_rows(top, bottom, after):
    rows, width = top.shape

    def body(top_ref, bottom_ref, *refs):
        refs[-1][:rows] = top_ref[...]
        refs[-1][rows:] = bottom_ref[...]

    return pl.pallas_call(
        body,
        in_specs=[VMEM] * 2 + [ANY] * len(after),
        out_specs=VMEM,
        out_shape=shape((rows + bottom.shape[0], width), F32),
        compiler_params=pltpu.CompilerParams(vmem_limit_bytes=SMALL_LIMIT),
        cost_estimate=light(0, 8 * rows * width),
        name="append_rows",
    )(top, bottom, *after)


def add_up(arrays, after, long=False):
    def body(*refs):
        total = refs[0][...]
        for ref in refs[1 : len(arrays)]:
            total = total + ref[...]
        refs[-1][...] = total

    return pl.pallas_call(
        body,
        in_specs=[VMEM] * len(arrays) + [ANY] * len(after),
        out_specs=VMEM,
        out_shape=shape(arrays[0].shape, F32),
        compiler_params=pltpu.CompilerParams(vmem_limit_bytes=SMALL_LIMIT),
        cost_estimate=light(1e11, 0) if long else light(0, 0),
        name="add_up",
    )(*arrays, *after)


def split_rows(array, at, after):
    rows, width = array.shape
    step = math.gcd(at, rows - at)
    first = at // step

    def body(in_ref, *refs):
        one_ref, two_ref = refs[-2:]
        i = pl.program_id(0)

        @pl.when(i < first)
        def _():
            one_ref[...] = in_ref[...]

        @pl.when(i >= first)
        def _():
            two_ref[...] = in_ref[...]

    block = (step, width)
    return pl.pallas_call(
        body,
        grid=(rows // step,),
        in_specs=[pl.BlockSpec(block, lambda i: (i, 0))] + [ANY] * len(after),
        out_specs=[
            pl.BlockSpec(block, lambda i: (jnp.minimum(i, first - 1), 0)),
            pl.BlockSpec(block, lambda i: (jnp.maximum(i - first, 0), 0)),
        ],
        out_shape=[pltpu.HBM((at, width), F32), pltpu.HBM((rows - at, width), F32)],
        compiler_params=pltpu.CompilerParams(vmem_limit_bytes=SMALL_LIMIT),
        cost_estimate=light(0, 8 * rows * width),
        name="split_rows",
    )(in_hbm(array), *after)


def rounded(array):
    def body(in_ref, out_ref):
        out_ref[...] = in_ref[...].astype(BF16)

    block = pl.BlockSpec((min(128, array.shape[0]), array.shape[1]), lambda i: (i, 0))
    return pl.pallas_call(
        body,
        grid=(array.shape[0] // block.block_shape[0],),
        in_specs=[block],
        out_specs=block,
        out_shape=shape(array.shape, BF16),
        name="rounded",
    )(array)


def whole_sum(unit, n):
    if n == 1:
        return unit
    if n % 2:
        return lax.psum(unit, "tensor")
    me, half = lax.axis_index("tensor"), n // 2
    held = unit
    for j in range(half - 1):
        held = unit + lax.ppermute(held, "tensor", [(j, j + 1), (n - 1 - j, n - 2 - j)])
    total = held + lax.ppermute(held, "tensor", [(half - 1, half), (half, half - 1)])
    for j in reversed(range(half - 1)):
        came = lax.ppermute(total, "tensor", [(j + 1, j), (n - 2 - j, n - 1 - j)])
        total = jnp.where((me == j) | (me == n - 1 - j), came, total)
    return total


class Line:
    LAG = 3

    def __init__(self, count, flag, finish):
        self.count, self.flag, self.finish = count, flag, finish
        self.units, self.operands, self.came, self.held, self.met = [], {}, {}, {}, {}
        self.step = 0

    def send(self, step, operand):
        pairs = [(0, 1), (3, 2)] * (step < self.count) + [(1, 0), (2, 3)] * (step >= self.LAG)
        self.operands[step] = operand
        self.came[step] = lax.ppermute(operand, "tensor", pairs)

    def pump(self, after, carried=(), long=False):
        step = self.step
        self.step += 1
        last = step >= self.count - 2
        unit = self.units[step] if step < self.count else None
        held = self.finish(self, step - self.LAG, unit, self.came[step], after, last)
        if unit is not None:
            self.held[step] = held
            self.met[step] = lax.ppermute(held, "tensor", [(1, 2), (2, 1)])
            after = [held]
        if step == 0:
            self.send(2, self.units[2])
        elif step <= self.count:
            ahead = step + 2
            unit = self.units[ahead] if ahead < self.count else None
            operand, *carried = pass_on(
                self.flag, self.held[step - 1], self.met[step - 1], unit, after, carried, last, long
            )
            self.send(ahead, operand)
            after = [operand]
        return after, *carried


class SmallSum:
    def __init__(self, values, axis, n):
        self.values, self.axis, self.n, self.apart, self.came = values, axis, n, 1, None

    def exchange(self):
        if self.n & (self.n - 1):
            self.values, self.apart = lax.psum(self.values, self.axis), self.n
        if self.apart >= self.n:
            return False
        self.came = lax.ppermute(self.values, self.axis, [(i, i ^ self.apart) for i in range(self.n)])
        self.apart *= 2
        return True

    def add(self, after, long=False):
        if self.came is not None:
            self.values, self.came = add_up([self.values, self.came], after, long), None
        return [self.values]


def rotary(span):
    half = ROT // 2
    inverse = 10000.0 ** (-(2.0 * np.arange(half)) / ROT)
    angle = np.arange(span)[:, None] * inverse[None, :]
    cosine, sine = np.cos(angle), np.sin(angle)
    ones, zeros = np.ones((span, 128 - ROT)), np.zeros((span, 128 - ROT))
    nil = np.zeros((span, half))
    tables = (
        np.concatenate([cosine, cosine, ones], 1),
        np.concatenate([-sine, nil, zeros], 1),
        np.concatenate([nil, sine, zeros], 1),
    )
    return [jnp.asarray(t, F32) for t in tables]


def make_local(dp, tp):
    def local(
        layer_input,
        lengths,
        ln1_gain,
        ln1_shift,
        w_qkv,
        b_qkv,
        w_dense,
        b_dense,
        ln2_gain,
        ln2_shift,
        w_in,
        b_in,
        w_out,
        b_out,
        grad_out,
    ):
        rows, width = layer_input.shape
        assert lengths.shape[0] == 1
        columns, units = w_dense.shape[0], w_in.shape[1]
        tables = rotary(rows)
        w_three = jnp.transpose(w_qkv, (1, 0, 2))
        vec = lambda v: v.reshape(1, -1)
        gains = (vec(ln1_gain), vec(ln1_shift), vec(ln2_gain), vec(ln2_shift))
        size, unit = 256, 128
        starts = list(range(0, rows, size))
        each = rows // unit
        me = lax.axis_index("tensor")
        flag = jnp.stack([(me == 1) | (me == 2), me == 0]).astype(jnp.int32)
        outs = [None, None]

        last = []

        def finish(line, done, unit, came, after, final):
            if done < 0:
                return take_in(flag, unit, came, None, None, 0, 0, None, after, final)[0]
            which, at = divmod(done, each)
            held, outs[which], more = take_in(
                flag, unit, came, line.operands[done + line.LAG], outs[which], at, rows // each, layer_input.shape, after,
                final,
            )
            last[:] = [more]
            return held

        straight = tp != 4
        line = None if straight else Line(2 * each, flag, finish)
        queue = [] if straight else line.units

        def pump(after, *carried, long=False):
            if straight or line.step == line.count + line.LAG:
                return (after, *carried)
            return line.pump(after, carried, long)

        def forward(start, size, held, after, carried=()):
            result = forward_rows(
                start, size, unit, layer_input, lengths, flag, gains, w_three, b_qkv, w_in, b_in, (b_dense, b_out),
                w_dense, w_out, tables, held, after, carried,
            )
            parts = size // unit
            queue.extend(result[6 : 6 + parts])
            return result[:6], [result[6 + parts]], result[7 + parts :]

        held, after, _ = forward(0, size, None, [])
        if not straight:
            line.send(0, queue[0])
        held, after, (queue[1],) = forward(size, size, held, [], [queue[1]])
        if not straight:
            line.send(1, queue[1])
        cotan, b_out_grad = mask_rows(lengths, grad_out, after)
        after = [b_out_grad]
        for start in starts[2:]:
            held, after, _ = forward(start, size, held, pump(after)[0])
        a_one, a_two, qkv, mixed, hidden, slope = held

        core = lax.rem(lax.axis_index("dp"), 2).astype(jnp.int32).reshape(1)
        blocks = dp // 2
        pairs = [(i, i ^ 1) for i in range(dp)]
        groups = [[2 * i + c for i in range(blocks)] for c in range(2)]

        def other_half(name, lefts, right, slide_left, after, long=False):
            half, token = pair_product(lefts, right, slide_left, 1 - core, None, blocks, after, name, long)
            return half, [token]

        def own_half(name, lefts, right, slide_left, came, after, long=False):
            half, token = pair_product(lefts, right, slide_left, core, came, blocks, after, name, long)
            return half, [token]

        def swap(half):
            return lax.ppermute(half, "dp", pairs)

        def over_chips(half):
            return lax.psum_scatter(half, "dp", scatter_dimension=0, axis_index_groups=groups, tiled=True)[0]

        out_parts = ([hidden, mixed], cotan[None], False)
        half, after = other_half("w_out_other", *out_parts, pump(after)[0])
        dmixed = mixed_back(cotan, w_dense, after)
        after, half = pump([dmixed], half)
        came_out = swap(half)
        dqkv, b_qkv_grad = attend_back(lengths, qkv, dmixed, tables, after)
        out_half, after = own_half("w_out_own", *out_parts, came_out, pump([b_qkv_grad])[0])
        out_grads = over_chips(out_half)
        (after,) = pump(after, long=True)

        dhpre, smalls, biases = None, [], []

        def backward(i, after):
            nonlocal dhpre
            dhpre, *dx, small, bias = backward_rows(
                starts[i], size, unit, layer_input, flag, cotan, slope, dqkv, w_three, w_in, w_out, gains, dhpre, after
            )
            queue.extend(dx)
            smalls.append(small)
            biases.append(bias)
            return [bias]

        after = backward(0, after)
        zero = jnp.zeros(1, jnp.int32)
        qkv_grads, token = pair_product([a_one], dqkv, True, zero, None, dp, pump(after)[0], "w_qkv_grad", apart=1)
        after, qkv_grads = pump([token], qkv_grads)
        qkv_grads = lax.psum_scatter(qkv_grads, "dp", scatter_dimension=0, tiled=True)[0]
        after = backward(1, after)
        after = backward(2, pump(after)[0])
        after = backward(3, pump(after)[0])

        flat = jnp.concatenate(
            [sum(smalls)[:4].reshape(-1), b_out_grad.reshape(-1), sum(biases).reshape(-1), b_qkv_grad.reshape(-1)]
        )
        small = SmallSum(flat.reshape(-1, 128), "dp", dp)
        small.exchange()
        in_parts = ([a_two], dhpre[None], True)
        half, after = other_half("w_in_other", *in_parts, pump(after)[0])
        after, half = pump(after, half)
        came_in = swap(half)
        after = small.add(after + [out_grads], True)
        small.exchange()
        (after,) = pump(after)
        after = small.add(after)
        small.exchange()
        in_half, after = own_half("w_in_own", *in_parts, came_in, after)
        after = small.add(after)
        while small.exchange():
            after = small.add(after)
        flat = small.values.reshape(-1)
        norms = jnp.concatenate([flat[: 4 * width].reshape(4, width), jnp.zeros((4, width), F32)])
        queue[-1] = append_rows(queue[-1], norms, after)
        after, in_half = pump([queue[-1]], in_half)
        in_grads = over_chips(in_half)
        w_out_grad, w_dense_grad = split_rows(out_grads[0], units, after + [qkv_grads])
        after = [w_dense_grad]
        while not straight and line.step < line.count + line.LAG:
            (after,) = pump(after)
        b_out_grad = flat[4 * width : 5 * width]
        b_in_grad = flat[5 * width : 5 * width + units]
        b_qkv_grad = flat[5 * width + units :].reshape(3, columns)
        w_qkv_grad = jnp.transpose(qkv_grads, (1, 0, 2))
        w_in_grad = in_grads[0]

        if straight:
            totals = [whole_sum(one, tp) for one in queue]
            last = [totals[-1][unit:]]
            totals[-1] = totals[-1][:unit]
            outs = [rounded(jnp.concatenate(totals[:each])), rounded(jnp.concatenate(totals[each:]))]
        gain_one, shift_one, gain_two, shift_two = (last[0][i] for i in range(4))
        layer_output, input_grad = outs
        return (
            layer_output,
            input_grad,
            gain_one,
            shift_one,
            w_qkv_grad,
            b_qkv_grad,
            w_dense_grad,
            b_out_grad,
            gain_two,
            shift_two,
            w_in_grad,
            b_in_grad,
            w_out_grad,
            b_out_grad,
        )

    return local


def solution(mesh):
    return jax.shard_map(
        make_local(mesh.shape["dp"], mesh.shape["tensor"]),
        mesh=mesh,
        in_specs=(
            P("dp", None),
            P("dp"),
            P(),
            P(),
            P(None, None, "tensor"),
            P(None, "tensor"),
            P("tensor", None),
            P(),
            P(),
            P(),
            P(None, "tensor"),
            P("tensor"),
            P("tensor", None),
            P(),
            P("dp", None),
        ),
        out_specs=(
            P("dp", None),
            P("dp", None),
            P(),
            P(),
            P("dp", None, "tensor"),
            P(None, "tensor"),
            P("tensor", "dp"),
            P(),
            P(),
            P(),
            P("dp", "tensor"),
            P("tensor"),
            P("tensor", "dp"),
            P(),
        ),
        check_vma=False,
    )
```
